256 devices in a mesh: dp: 4 (over x), gx: 2 (over core), yz: 32 (over z, y).
Axes of the slice: x: 4, y: 4, z: 8, core: 2. Of those that a mesh axis runs over, the one named last changes fastest.
Arguments:
- volumes: bfloat16 [4, 4, 2, 32, 16384], P('dp', None, 'gx', 'yz'), may hold values from -6 to 6
- first_kernel: bfloat16 [32, 4, 3, 3, 3], replicated, may hold values from -0.625 to 0.625
- second_kernel: bfloat16 [64, 32, 3, 3, 3], replicated, may hold values from -0.21875 to 0.21875
- cotangent: bfloat16 [4, 64, 2, 32, 256], P('dp', None, 'gx', 'yz'), may hold values from -6 to 6
Outputs:
- features: bfloat16 [4, 64, 2, 32, 256], P('dp', None, 'gx', 'yz')
- act_grad: float32 [4, 32, 2, 32, 2048], P('dp', None, 'gx', 'yz')
- first_grad: float32 [32, 4, 3, 3, 3], replicated
- second_grad: float32 [64, 32, 3, 3, 3], replicated
The draws below stay inside these ranges and needn't reach their ends.
All inputs are finite; a program needn't handle non-finite values.
Results may differ from the reference program's by a relative error of at most 0.019.
The reference program's roundings to bfloat16 on the way count: a program that leaves them out, or rounds other values in their place, can miss the bound.
Values may be sent and summed in bfloat16 or wider, within the bound.
A program may use at most 128 MiB of HBM per device.

```python
import jax
import jax.numpy as jnp
from jax import lax

IN_CH = 4
C1 = 32
C2 = 64
CX = 32
CY = 32
CZ = 16
PX = 2
PY = 4
PZ = 8
BLOCKS = 32
VOLS = 4
N_GX = 2


def block_scale(rng, shape, shards, smallest, largest):
    def one(axis_at, parts):
        steps = jax.random.uniform(jax.random.fold_in(jax.random.fold_in(rng, 6), axis_at), (parts,), jnp.float32, smallest / len(shards), largest / len(shards))
        return jnp.repeat(jnp.exp(steps), shape[axis_at] // parts).reshape((-1,) + (1,) * (len(shape) - axis_at - 1))

    loudness = one(*shards[0])
    for cut in shards[1:]:
        loudness = loudness * one(*cut)
    return loudness


def normal_values(rng, extent, scale, reach, cuts=(), held_as=jnp.bfloat16):
    drawn = scale * jax.random.normal(rng, extent, jnp.float32)
    if cuts:
        drawn = drawn * block_scale(rng, extent, cuts, -0.22, 0.18)
    return jnp.clip(drawn, -reach, reach).astype(held_as)


def setup_inputs(seed: int = 0) -> dict:
    key_of = jax.random.split(jax.random.key(seed), 5)
    return {
        "volumes": normal_values(key_of[0], (VOLS, IN_CH, PX, BLOCKS, CX * CY * CZ), 1.0, 6.0, ((0, 4), (2, 2), (3, 32))),
        "first_kernel": normal_values(key_of[1], (C1, IN_CH, 3, 3, 3), (27 * IN_CH) ** -0.5, 0.625),
        "second_kernel": normal_values(key_of[2], (C2, C1, 3, 3, 3), (27 * C1) ** -0.5, 0.21875),
        "cotangent": normal_values(key_of[3], (VOLS, C2, PX, BLOCKS, CX * CY * CZ // 64), 1.0, 6.0, ((0, 4), (2, 2), (3, 32))),
    }


SLOPE = 0.3

def convolve_same(values, kernel):
    return lax.conv_general_dilated(values, kernel, (1, 1, 1), 'SAME', dimension_numbers=('NCDHW', 'OIDHW', 'NCDHW'), preferred_element_type=jnp.float32)

def kernel_grad(padded, grad):
    result = lax.conv_general_dilated(padded, grad, (1, 1, 1), 'VALID', dimension_numbers=('CNDHW', 'IODHW', 'NCDHW'), preferred_element_type=jnp.float32)
    return result.transpose(1, 0, 2, 3, 4)

def leaky(values):
    return jnp.where(values > 0, values, SLOPE * values)

def leaky_slope(values):
    return jnp.where(values > 0, jnp.float32(1.0), jnp.float32(SLOPE))

def average_pool(values):
    bat, chan, xs, ys, zs = values.shape
    return values.reshape(bat, chan, xs // 2, 2, ys // 2, 2, zs // 2, 2).mean(axis=(3, 5, 7))

def spread_back(values):
    bat, chan, xs, ys, zs = values.shape
    grown = jnp.broadcast_to(values[:, :, :, None, :, None, :, None], (bat, chan, xs, 2, ys, 2, zs, 2))
    return grown.reshape(bat, chan, 2 * xs, 2 * ys, 2 * zs) * 0.125

def pad_all(values):
    return jnp.pad(values, ((0, 0), (0, 0), (1, 1), (1, 1), (1, 1)))

def to_space(values, factor):
    bat, chan = (values.shape[0], values.shape[1])
    xs, ys, zs = (CX // factor, CY // factor, CZ // factor)
    grid = values.reshape(bat, chan, N_GX, PY, PZ, xs, ys, zs).transpose(0, 1, 2, 5, 3, 6, 4, 7)
    return grid.reshape(bat, chan, N_GX * xs, PY * ys, PZ * zs)

def to_blocks(values):
    bat, chan, xs, ys, zs = values.shape
    lx, ly, lz = (xs // N_GX, ys // PY, zs // PZ)
    grid = values.reshape(bat, chan, N_GX, lx, PY, ly, PZ, lz).transpose(0, 1, 2, 4, 6, 3, 5, 7)
    return grid.reshape(bat, chan, N_GX, PY * PZ, lx * ly * lz)

def reference(volumes, first_kernel, second_kernel, cotangent):
    flipped = jnp.flip(second_kernel, (2, 3, 4)).transpose(1, 0, 2, 3, 4)
    spatial_in = to_space(volumes, 1)
    spatial_up = to_space(cotangent, 4)

    def one_volume(pair):
        single = pair[0][None]
        upstream = pair[1][None]
        pre_first = convolve_same(single, first_kernel)
        act_first = average_pool(leaky(pre_first)).astype(jnp.bfloat16)
        pre_second = convolve_same(act_first, second_kernel)
        feature_out = average_pool(leaky(pre_second)).astype(jnp.bfloat16)
        grad_second = (spread_back(upstream.astype(jnp.float32)) * leaky_slope(pre_second)).astype(jnp.bfloat16)
        act_grad = convolve_same(grad_second, flipped)
        grad_first = (spread_back(act_grad) * leaky_slope(pre_first)).astype(jnp.bfloat16)
        second_part = kernel_grad(pad_all(act_first), grad_second)
        first_part = kernel_grad(pad_all(single), grad_first)
        return (feature_out[0], act_grad[0], first_part, second_part)
    feature_all, grad_all, first_parts, second_parts = lax.map(one_volume, (spatial_in, spatial_up))
    return (to_blocks(feature_all), to_blocks(grad_all), lax.optimization_barrier(jnp.sum(first_parts, axis=0)), lax.optimization_barrier(jnp.sum(second_parts, axis=0)))
```

```python
import functools

import jax
import jax.numpy as jnp
import numpy as np
from jax import lax
from jax.experimental import pallas as pl
from jax.experimental.pallas import tpu as pltpu
from jax.sharding import PartitionSpec as P

F32 = jnp.float32
BF16 = jnp.bfloat16
PY, PZ = 4, 8
NY = 4
KRAW = 1408
MESH = pl.DeviceIdType.MESH


def plane_order(rim):
    lanes = {(y, z): y * 8 + z for y in range(16) for z in range(8)}
    for y in range(-rim, 16 + rim):
        for z in range(-rim, 8 + rim):
            if (y, z) not in lanes:
                lanes[(y, z)] = len(lanes)
    return lanes


def raw_lane(y, z):
    row = y + 5 if y < 0 else y - 32
    col = z + 5 if z < 0 else z - 16
    if 0 <= y < 32 and 0 <= z < 16:
        return y * 16 + z
    if 0 <= z < 16:
        return (512 if y < 0 else 640) + row * 16 + z
    if 0 <= y < 32:
        return (768 if z < 0 else 1024) + col * 32 + y
    return 1280 + ((y >= 32) * 2 + (z >= 16)) * 32 + row * 5 + col


@functools.cache
def matrices():
    wide, ring = plane_order(2), plane_order(1)
    gather = np.zeros((16, KRAW, 256), np.float32)
    for dy in range(4):
        for dz in range(4):
            for (y, z), lane in wide.items():
                gather[dy * 4 + dz, raw_lane(2 * y - 1 + dy, 2 * z - 1 + dz), lane] = 1
    outgoing = np.zeros((512, 896), np.float32)
    for r in range(5):
        for z in range(16):
            outgoing[(27 + r) * 16 + z, r * 16 + z] = 1
            outgoing[r * 16 + z, 128 + r * 16 + z] = 1
    for c in range(5):
        for y in range(32):
            outgoing[y * 16 + 11 + c, 256 + c * 32 + y] = 1
            outgoing[y * 16 + c, 512 + c * 32 + y] = 1
    for k in range(4):
        for r in range(5):
            for c in range(5):
                y = r if k // 2 else 27 + r
                z = c if k % 2 else 11 + c
                outgoing[y * 16 + z, 768 + k * 32 + r * 5 + c] = 1
    second = np.zeros((9, 256, 256), np.float32)
    back = np.zeros((5, 256, 256), np.float32)
    for dy in range(3):
        for dz in range(3):
            tap = dy * 3 + dz
            for (y, z), lane in ring.items():
                second[tap, wide[(y + dy - 1, z + dz - 1)], lane] = 1
            for y in range(16):
                for z in range(8):
                    source = ring[(y - dy + 1, z - dz + 1)]
                    back[tap // 2, source, (tap % 2) * 128 + y * 8 + z] = 1
    fold = np.zeros((128, 2048), np.float32)
    for phase in range(8):
        px, py, pz = phase // 4, phase // 2 % 2, phase % 2
        for tx in range(3):
            for ty in range(3):
                for tz in range(3):
                    for channel in range(4):
                        x, y, z = tx + px, ty + py, tz + pz
                        row = (y * 4 + z) * 16 + ((x - 1) % 4) * 4 + channel
                        fold[((tx * 3 + ty) * 3 + tz) * 4 + channel, phase * 256 + row] = 1
    pool = np.zeros((512, 128), np.float32)
    for x in range(4):
        for y in range(16):
            for z in range(8):
                pool[x * 128 + y * 8 + z, x * 32 + (y // 2) * 4 + z // 2] = 1
    cot_out = np.zeros((256, 256), np.float32)
    cot_in = np.zeros((384, 1024), np.float32)
    for x in range(8):
        for y in range(8):
            cot_out[x * 32 + y * 4, x * 8 + y] = 1
            cot_out[x * 32 + y * 4 + 3, 64 + x * 8 + y] = 1
        for z in range(4):
            cot_out[x * 32 + z, 128 + x * 4 + z] = 1
            cot_out[x * 32 + 28 + z, 160 + x * 4 + z] = 1
        for (y, z), lane in ring.items():
            if lane < 128:
                continue
            if 0 <= y < 16:
                source = x * 8 + y // 2 + (64 if z < 0 else 0)
            elif 0 <= z < 8:
                source = 128 + x * 4 + z // 2 + (32 if y < 0 else 0)
            else:
                source = 256 + x * 4 + (3 if z < 0 else 0) + (32 if y < 0 else 0)
            cot_in[source, x * 128 + lane - 128] = 1
    sides = np.zeros((8, 256), np.float32)
    for (y, z), lane in wide.items():
        sides[:4, lane] = (y < 0, y >= 16, z < 0, z >= 8)
    sixteen = (gather, outgoing, second, back, fold, pool, cot_out, cot_in)
    return tuple(m.astype(jnp.bfloat16) for m in sixteen) + (sides,)


def mm(a, b):
    return jnp.dot(a, b, preferred_element_type=F32)


def mm_nt(a, b):
    return lax.dot_general(a, b, (((1,), (1,)), ((), ())), preferred_element_type=F32)


def identity(n):
    rows = lax.broadcasted_iota(jnp.int32, (n, n), 0)
    return jnp.where(rows == lax.broadcasted_iota(jnp.int32, (n, n), 1), 1.0, 0.0).astype(BF16)


def leaky(t):
    return jnp.where(t > 0, t, 0.3 * t)


def slope(t):
    return jnp.where(t > 0, jnp.float32(1.0), jnp.float32(0.3))


def split(t):
    high = t.astype(BF16)
    return high, (t - high.astype(F32)).astype(BF16)


FACES = ((1, 0), (-1, 0), (0, 1), (0, -1))
CORNERS = ((1, 1), (1, -1), (-1, 1), (-1, -1))
DIRS = FACES + CORNERS
XY = tuple((a, b) for a in range(4) for b in range(4) if (a, b) != (0, 0))
S_RAW, S_COT, S_CORE, S_XY, S_Z, S_AG = 0, 8, 16, 24, 40, 48


def body(
    vol, k1, w2, cot, gather_h, outgoing_h, second_h, back_h, fold_h, pool_h, cot_out_h, cot_in_h, sides,
    feat_out, grad_out, first_out, second_out,
    gather, outgoing, second, back, fold, pool, cot_out, cot_in,
    rows32, lraw, sy_buf, sz_buf, sc_buf, ry_buf, rz_buf, rc_buf, edge_in,
    cot_send, cot_recv, x4, x4i, pre1, weights1, forward2, backward2, k1s,
    p2, b2i, b2r, t2i, t2r, spread_i, spread_r, pooled, pg, gshift, bg, t3, g1,
    total, core_in, xy_in, z_in, final,
    local_sem, send_sem, recv_sem,
):
    dp, g, s = lax.axis_index("dp"), lax.axis_index("gx"), lax.axis_index("yz")
    by, bz = s // PZ, s % PZ
    yi, zi = s % NY, s // NY
    other = (dp, 1 - g, s)
    near = [(dp, g, ((by + a) % PY) * PZ + (bz + b) % PZ) for a, b in DIRS]
    flat = [((dp + a) % 4, g, zi * NY + (yi + b) % NY) for a, b in XY]
    tall = [(dp, g, ((zi + k) % 8) * NY + yi) for k in range(1, 8)]

    loads = [
        pltpu.make_async_copy(a, b, local_sem.at[i])
        for i, (a, b) in enumerate(
            (
                (outgoing_h, outgoing), (cot_out_h, cot_out), (fold_h, fold), (pool_h, pool), (cot_in_h, cot_in),
                (gather_h, gather), (second_h, second), (back_h, back),
            )
        )
    ]
    for load in loads:
        load.start()

    barrier = pltpu.get_barrier_semaphore()
    everyone = [other] + near + flat + tall
    for device in everyone:
        pl.semaphore_signal(barrier, inc=1, device_id=device, device_id_type=MESH)

    def remote(source, target, slot, device):
        return pltpu.make_async_remote_copy(
            src_ref=source, dst_ref=target, send_sem=send_sem.at[slot], recv_sem=recv_sem.at[slot],
            device_id=device, device_id_type=MESH,
        )

    def valid(a, b):
        ok = jnp.logical_and(
            jnp.logical_and(by + a >= 0, by + a < PY), jnp.logical_and(bz + b >= 0, bz + b < PZ)
        )
        return jnp.where(ok, jnp.float32(1.0), jnp.float32(0.0))

    lane = lax.broadcasted_iota(jnp.int32, (1, 128), 1)

    for x in range(32):
        rows32[4 * x : 4 * x + 4, :] = vol[:, x * 512 : (x + 1) * 512].astype(F32)
    lraw[0:128, 0:512] = rows32[...].astype(BF16)
    loads[0].wait()
    out = mm(lraw[0:128, 0:512], outgoing[...])
    sy_buf[0] = (out[:, 0:128] * valid(1, 0)).astype(BF16)
    sy_buf[1] = (out[:, 128:256] * valid(-1, 0)).astype(BF16)
    sz_buf[0] = (out[:, 256:512] * valid(0, 1)).astype(BF16)
    sz_buf[1] = (out[:, 512:768] * valid(0, -1)).astype(BF16)
    for k, (a, b) in enumerate(CORNERS):
        packed = jnp.zeros((32, 128), F32)
        for j in range(4):
            piece = out[32 * j : 32 * j + 32, 768:896]
            moved = pltpu.roll(piece, (32 * (j - k)) % 128, 1) if j != k else piece
            packed = jnp.where(lane // 32 == j, moved, packed)
        sc_buf[k] = (packed * valid(a, b)).astype(BF16)
    loads[1].wait()
    strips = mm(cot[...], cot_out[...])
    for i, (a, b) in enumerate(DIRS):
        part = strips[:, 0:128] if a == 0 else strips[:, 128:256]
        cot_send[i] = (part * valid(a, b)).astype(BF16)

    pl.semaphore_wait(barrier, len(everyone))
    raw_copies = []
    for i in (4, 5, 6, 7, 0, 1, 2, 3):
        if i >= 4:
            pair = (sc_buf.at[i - 4], rc_buf.at[i - 4])
        elif i >= 2:
            pair = (sz_buf.at[i - 2], rz_buf.at[i - 2])
        else:
            pair = (sy_buf.at[i], ry_buf.at[i])
        copy = remote(pair[0], pair[1], S_RAW + i, near[i])
        copy.start()
        raw_copies.append(copy)
    cot_copies = []
    for i in range(8):
        copy = remote(cot_send.at[i], cot_recv.at[i], S_COT + i, near[i])
        copy.start()
        cot_copies.append(copy)

    k1s[...] = jnp.zeros_like(k1s)
    for tap in range(27):
        k1s[4 * tap : 4 * tap + 4, :] = k1[tap].astype(F32)
    loads[2].wait()
    k1t = mm_nt(identity(32), k1s[...].astype(BF16)).astype(BF16)
    for phase in range(8):
        weights1[32 * phase : 32 * phase + 32, :] = mm(k1t, fold[:, 256 * phase : 256 * phase + 256]).astype(BF16)
    eye = identity(64)
    for x in range(3):
        block = w2[9 * x : 9 * x + 9].reshape(288, 64)
        forward2[64 * x : 64 * x + 64, :] = mm_nt(eye, block).astype(BF16)
        for a in (0, 2, 4, 6):
            both = jnp.concatenate([w2[9 * x + a].astype(F32), w2[9 * x + a + 1].astype(F32)], axis=1)
            backward2[32 * x : 32 * x + 32, 64 * a : 64 * a + 128] = both.astype(BF16)
        backward2[32 * x : 32 * x + 32, 512:576] = w2[9 * x + 8]
    loads[3].wait()
    for half in range(2):
        spread_i[:, 512 * half : 512 * half + 512] = mm_nt(cot[:, 128 * half : 128 * half + 128], pool[...])
    far = pl.multiple_of(g * (17 * 32), 32)
    p2[pl.ds(far, 32), :] = jnp.zeros((32, 256), BF16)
    far = pl.multiple_of(g * (17 * 64), 64)
    pg[pl.ds(far, 64), :] = jnp.zeros((64, 256), BF16)
    gshift[...] = jnp.zeros_like(gshift)
    lraw[128:144, :] = jnp.zeros((16, KRAW), BF16)
    for load in loads[4:]:
        load.wait()

    for copy in raw_copies:
        copy.wait_recv()
    lraw[0:128, 512:640] = ry_buf[0]
    lraw[0:128, 640:768] = ry_buf[1]
    lraw[0:128, 768:1024] = rz_buf[0]
    lraw[0:128, 1024:1280] = rz_buf[1]
    for j in range(4):
        corner = jnp.zeros((32, 128), F32)
        for k in range(4):
            piece = rc_buf[k].astype(F32)
            moved = pltpu.roll(piece, (32 * (k - j)) % 128, 1) if j != k else piece
            corner = jnp.where(lane // 32 == k, moved, corner)
        lraw[32 * j : 32 * j + 32, 1280:1408] = corner.astype(BF16)
    mine = pl.multiple_of(jnp.where(g == 0, 112, 0), 16)
    copy = remote(lraw.at[pl.ds(mine, 16), :], edge_in, S_CORE, other)
    copy.start()
    core_copies = [copy]
    copy.wait_recv()
    first_core = jnp.where(g == 0, jnp.float32(1.0), jnp.float32(0.0))
    edge = edge_in[...].astype(F32)
    half_row = lax.broadcasted_iota(jnp.int32, (8, 1), 0)
    edge = jnp.where(half_row < 4, edge[0:8] * first_core, edge[8:16] * (1.0 - first_core))
    lraw[128:144, :] = jnp.concatenate([edge, jnp.zeros_like(edge)], axis=0).astype(BF16)

    def gather_step(tap, carry):
        got = mm(lraw[...], gather[tap])
        low = half_row < 4
        at = pl.multiple_of(tap * 16, 16)
        for x in range(16):
            after = got[8 * x + 8 : 8 * x + 16]
            before = got[8 * x - 8 : 8 * x] if x else got[128:136]
            block = jnp.concatenate([got[8 * x : 8 * x + 8], jnp.where(low, after, before)], axis=0).astype(BF16)
            x4[x, pl.ds(at, 16), :] = block
            x4i[pl.ds(at, 16), 128 * x : 128 * x + 128] = block[:, 0:128]
        return carry

    lax.fori_loop(0, 16, gather_step, 0)

    def flag(test):
        return jnp.where(test, jnp.float32(1.0), jnp.float32(0.0))

    outside = jnp.maximum(
        jnp.maximum(sides[0:1, :] * flag(by == 0), sides[1:2, :] * flag(by == PY - 1)),
        jnp.maximum(sides[2:3, :] * flag(bz == 0), sides[3:4, :] * flag(bz == PZ - 1)),
    )
    scale = (1.0 - outside) * 0.125

    def first_layer(x, carry):
        pre = mm(weights1[...], x4[x])
        pre1[x] = pre[:, 0:128]
        act = leaky(pre[0:32])
        for phase in range(1, 8):
            act = act + leaky(pre[32 * phase : 32 * phase + 32])
        p2[pl.ds(pl.multiple_of(32 * x + 32, 32), 32), :] = (act * scale).astype(BF16)
        return carry

    lax.fori_loop(0, 16, first_layer, 0)
    near_src = pl.multiple_of(jnp.where(g == 0, 16 * 32, 32), 32)
    near_dst = pl.multiple_of(jnp.where(g == 0, 0, 17 * 32), 32)
    copy = remote(p2.at[pl.ds(near_src, 32), :], p2.at[pl.ds(near_dst, 32), :], S_CORE + 1, other)
    copy.start()
    core_copies.append(copy)

    for cot_copy in cot_copies:
        cot_copy.wait_recv()
    down, up, left, right = (cot_recv[i] for i in range(4))
    zs = jnp.where(lane >= 64, left.astype(F32), right.astype(F32))
    ys = jnp.where(lane >= 32, down.astype(F32), up.astype(F32))
    late = lane % 4 == 3
    cs = jnp.where(
        lane >= 32,
        jnp.where(late, cot_recv[4].astype(F32), cot_recv[5].astype(F32)),
        jnp.where(late, cot_recv[6].astype(F32), cot_recv[7].astype(F32)),
    )
    rim = jnp.concatenate([zs, ys, cs], axis=1).astype(BF16)
    spread_r[...] = mm(rim, cot_in[...])

    copy.wait_recv()

    def shift_step(tap, carry):
        got = mm(p2[...], second[tap])
        at = pl.multiple_of(tap * 32, 32)
        for x in range(18):
            block = got[32 * x : 32 * x + 32].astype(BF16)
            b2i[pl.ds(at, 32), 128 * x : 128 * x + 128] = block[:, 0:128]
            b2r[pl.ds(at, 32), 128 * x : 128 * x + 128] = block[:, 128:256]
        return carry

    lax.fori_loop(0, 9, shift_step, 0)

    def second_layer(chunk, carry):
        at = pl.ds(pl.multiple_of(chunk * 256, 256), 256)
        t2i[:, at] = mm(forward2[...], b2i[:, at])
        t2r[:, at] = mm(forward2[...], b2r[:, at])
        return carry

    lax.fori_loop(0, 9, second_layer, 0)

    for half in range(8):
        lifted = spread_i[:, 128 * half : 128 * half + 128] * 0.125
        lifted_rim = spread_r[:, 128 * half : 128 * half + 128] * 0.125
        pair = jnp.zeros((64, 128), F32)
        for x in (2 * half, 2 * half + 1):
            at = [slice(128 * (x + d), 128 * (x + d) + 128) for d in range(3)]
            pre = t2i[0:64, at[0]] + t2i[64:128, at[1]] + t2i[128:192, at[2]]
            pair = pair + leaky(pre)
            grad = (lifted * slope(pre)).astype(BF16)
            pg[64 * x + 64 : 64 * x + 128, 0:128] = grad
            for d in range(3):
                gshift[64 * d : 64 * d + 64, at[d]] = grad
            pre = t2r[0:64, at[0]] + t2r[64:128, at[1]] + t2r[128:192, at[2]]
            pg[64 * x + 64 : 64 * x + 128, 128:256] = (lifted_rim * slope(pre)).astype(BF16)
        high, low = split(pair)
        at = slice(128 * (half % 4), 128 * (half % 4) + 128)
        pooled[half // 4, 0:64, at] = high
        pooled[half // 4, 64:128, at] = low
    near_src = pl.multiple_of(jnp.where(g == 0, 16 * 64, 64), 64)
    near_dst = pl.multiple_of(jnp.where(g == 0, 0, 17 * 64), 64)
    copy = remote(pg.at[pl.ds(near_src, 64), :], pg.at[pl.ds(near_dst, 64), :], S_CORE + 2, other)
    copy.start()
    core_copies.append(copy)
    for half in range(2):
        sums = mm(pooled[half], pool[...])
        feat_out[:, 128 * half : 128 * half + 128] = ((sums[0:64] + sums[64:128]) * 0.125).astype(BF16)

    grad2 = mm_nt(b2i[...], gshift[...])
    total[0:288, :] = grad2[:, 0:128]
    total[288:432, 0:64] = grad2[0:144, 128:192]
    total[288:432, 64:128] = grad2[144:288, 128:192]
    total[464:512, :] = jnp.zeros((48, 128), F32)
    copy.wait_recv()

    def back_step(step, carry):
        got = mm(pg[...], back[step])
        at = pl.multiple_of(step * 128, 128)
        for x in range(18):
            block = got[64 * x : 64 * x + 64].astype(BF16)
            bg[pl.ds(at, 64), 128 * x : 128 * x + 128] = block[:, 0:128]
            bg[pl.ds(at + 64, 64), 128 * x : 128 * x + 128] = block[:, 128:256]
        return carry

    lax.fori_loop(0, 5, back_step, 0)

    def back_layer(chunk, carry):
        at = pl.ds(pl.multiple_of(chunk * 256, 256), 256)
        t3[:, at] = mm(backward2[...], bg[0:576, at])
        return carry

    lax.fori_loop(0, 9, back_layer, 0)

    for x in range(16):
        grad = (
            t3[0:32, 128 * (x + 2) : 128 * (x + 3)]
            + t3[32:64, 128 * (x + 1) : 128 * (x + 2)]
            + t3[64:96, 128 * x : 128 * (x + 1)]
        )
        grad_out[pl.ds(x, 32, stride=16), :] = grad
        eighth = grad * 0.125
        for phase in range(8):
            at = slice(32 * phase, 32 * phase + 32)
            g1[at, 128 * x : 128 * x + 128] = (eighth * slope(pre1[x, at, :])).astype(BF16)
    wide = mm_nt(g1[...], x4i[...])
    partial = jnp.zeros((64, 128), F32)
    for phase in range(8):
        high, low = split(wide[32 * phase : 32 * phase + 32])
        partial = partial + mm_nt(jnp.concatenate([high, low], axis=0), fold[:, 256 * phase : 256 * phase + 256])
    total[432:464, :] = partial[0:32] + partial[32:64]

    mine = pl.multiple_of(g * 256, 256)
    theirs = pl.multiple_of((1 - g) * 256, 256)
    copy = remote(total.at[pl.ds(theirs, 256), :], core_in, S_CORE + 3, other)
    copy.start()
    copy.wait()
    core_in[...] = core_in[...] + total[pl.ds(mine, 256), :]
    xy_copies = []
    for i, (a, b) in enumerate(XY):
        piece = ((dp + a) % 4) * 4 + (yi + b) % 4
        source = core_in.at[pl.ds(pl.multiple_of(piece * 16, 16), 16), :]
        copy = remote(source, xy_in.at[i], S_XY + i, flat[i])
        copy.start()
        xy_copies.append(copy)
    place = pl.multiple_of((dp * 4 + yi) * 16, 16)
    part = core_in[pl.ds(place, 16), :]
    for i, copy in enumerate(xy_copies):
        copy.wait_recv()
        part = part + xy_in[i]
    z_in[zi] = part
    z_copies = []
    for k in range(7):
        copy = remote(z_in.at[zi], z_in.at[zi], S_Z + k, tall[k])
        copy.start()
        z_copies.append(copy)
    for copy in z_copies:
        copy.wait_recv()
    part = z_in[0]
    for k in range(1, 8):
        part = part + z_in[k]
    rows = pl.ds(pl.multiple_of(mine + place, 16), 16)
    final[rows, :] = part
    ag_copies = []
    for i in range(15):
        copy = remote(final.at[rows, :], final.at[rows, :], S_AG + i, flat[i])
        copy.start()
        ag_copies.append(copy)
    for copy in ag_copies:
        copy.wait_recv()
    half = pl.ds(mine, 256)
    copy = remote(final.at[half, :], final.at[half, :], S_CORE + 4, other)
    copy.start()
    core_copies.append(copy)
    copy.wait_recv()

    for a in range(9):
        at = slice(32 * a, 32 * a + 32)
        second_out[a] = final[at, 0:64]
        second_out[9 + a] = final[at, 64:128]
    for a in range(36):
        row = 288 + (8 * a) % 144
        lanes = slice(0, 64) if a < 18 else slice(64, 128)
        second_out[18 + a // 4, 8 * (a % 4) : 8 * (a % 4) + 8, :] = final[row : row + 8, lanes]
    flipped = final[432:464, :].T
    for tap in range(27):
        first_out[tap] = flipped[4 * tap : 4 * tap + 4, :]

    for copy in raw_copies + cot_copies + core_copies + xy_copies + z_copies + ag_copies:
        copy.wait_send()


def on_device(volumes, first_kernel, second_kernel, cotangent):
    consts = matrices()
    here = pl.BlockSpec(memory_space=pltpu.VMEM)
    there = pl.BlockSpec(memory_space=pl.ANY)
    vmem = pltpu.VMEM
    scratch = [vmem(m.shape, BF16) for m in consts[:8]] + [
        vmem((128, 512), F32), vmem((144, KRAW), BF16),
        vmem((2, 128, 128), BF16), vmem((2, 128, 256), BF16), vmem((4, 32, 128), BF16),
        vmem((2, 128, 128), BF16), vmem((2, 128, 256), BF16), vmem((4, 32, 128), BF16), vmem((16, KRAW), BF16),
        vmem((8, 64, 128), BF16), vmem((8, 64, 128), BF16),
        vmem((16, 256, 256), BF16), vmem((256, 2048), BF16), vmem((16, 256, 128), F32),
        vmem((256, 256), BF16), vmem((192, 288), BF16), vmem((96, 576), BF16), vmem((128, 32), F32),
        vmem((576, 256), BF16), vmem((288, 2304), BF16), vmem((288, 2304), BF16),
        vmem((192, 2304), F32), vmem((192, 2304), F32), vmem((64, 1024), F32), vmem((64, 1024), F32),
        vmem((2, 128, 512), BF16), vmem((1152, 256), BF16), vmem((192, 2304), BF16),
        vmem((640, 2304), BF16), vmem((96, 2304), F32), vmem((256, 2048), BF16),
        vmem((512, 128), F32), vmem((256, 128), F32), vmem((15, 16, 128), F32), vmem((8, 16, 128), F32), vmem((512, 128), F32),
        pltpu.SemaphoreType.DMA((8,)), pltpu.SemaphoreType.DMA((63,)), pltpu.SemaphoreType.DMA((63,)),
    ]
    features, act_grad, first_grad, second_grad = pl.pallas_call(
        body,
        out_shape=(
            jax.ShapeDtypeStruct((64, 256), BF16),
            jax.ShapeDtypeStruct((512, 128), F32),
            jax.ShapeDtypeStruct((27, 4, 32), F32),
            jax.ShapeDtypeStruct((27, 32, 64), F32),
        ),
        in_specs=[here] * 4 + [there] * 8 + [here],
        out_specs=(here,) * 4,
        scratch_shapes=scratch,
        compiler_params=pltpu.CompilerParams(
            collective_id=0, has_side_effects=True, vmem_limit_bytes=56 * 1024 * 1024
        ),
    )(
        volumes.reshape(4, 16384),
        first_kernel.transpose(2, 3, 4, 1, 0).reshape(27, 4, 32),
        second_kernel.transpose(2, 3, 4, 1, 0).reshape(27, 32, 64),
        cotangent.reshape(64, 256),
        *(jnp.asarray(m) for m in consts),
    )
    return (
        features.reshape(1, 64, 1, 1, 256),
        act_grad.reshape(1, 32, 1, 1, 2048),
        first_grad.reshape(3, 3, 3, 4, 32).transpose(4, 3, 0, 1, 2),
        second_grad.reshape(3, 3, 3, 32, 64).transpose(4, 3, 0, 1, 2),
    )


def solution(mesh):
    placed = (P("dp", None, "gx", "yz", None), P(), P(), P("dp", None, "gx", "yz", None))
    return jax.shard_map(
        on_device,
        mesh=mesh,
        in_specs=placed,
        out_specs=(P("dp", None, "gx", "yz", None), P("dp", None, "gx", "yz", None), P(), P()),
        check_vma=False,
    )
```

```python
import functools

import jax
import jax.numpy as jnp
import numpy as np
from jax import lax
from jax.experimental import pallas as pl
from jax.experimental.pallas import tpu as pltpu
from jax.sharding import PartitionSpec as P

F32 = jnp.float32
BF16 = jnp.bfloat16
PY, PZ = 4, 8
NY = 4
KRAW = 1280
MESH = pl.DeviceIdType.MESH


def plane_order(rim):
    lanes = {(y, z): y * 8 + z for y in range(16) for z in range(8)}
    for y in range(-rim, 16 + rim):
        for z in range(-rim, 8 + rim):
            if (y, z) not in lanes:
                lanes[(y, z)] = len(lanes)
    return lanes


def on_edge(y, z):
    return y in (0, 31) or z in (0, 15)


EDGE = {place: i for i, place in enumerate((y, z) for y in range(32) for z in range(16) if on_edge(y, z))}


def rim_lane(y, z):
    if 0 <= y < 32 and 0 <= z < 16:
        return 640 + EDGE[(y, z)]
    if 0 <= z < 16:
        if y in (-1, 32):
            return (0 if y < 0 else 16) + z
        return 256 + ((y + 5) * 16 if y < 0 else 64 + (y - 33) * 16) + z
    if 0 <= y < 32:
        if z in (-1, 16):
            return (32 if z < 0 else 64) + y
        return 384 + ((z + 5) * 32 if z < 0 else 128 + (z - 17) * 32) + y
    row = y + 5 if y < 0 else y - 32
    col = z + 5 if z < 0 else z - 16
    return 128 + ((y >= 32) * 2 + (z >= 16)) * 32 + row * 5 + col


@functools.cache
def matrices():
    wide, ring = plane_order(2), plane_order(1)
    inside = np.zeros((8, 512, 256), np.float32)
    nearby = np.zeros((8, 256, 256), np.float32)
    around = np.zeros((8, 768, 256), np.float32)
    for dy in range(4):
        for dz in range(4):
            step, shift = divmod(dy * 4 + dz, 2)
            for (qy, qz), lane in wide.items():
                y, z = 2 * qy - 1 + dy, 2 * qz - 1 + dz
                if lane >= 128:
                    around[step, rim_lane(y, z), shift * 128 + lane - 128] = 1
                elif 0 <= y < 32 and 0 <= z < 16:
                    inside[step, y * 16 + z, shift * 128 + lane] = 1
                else:
                    nearby[step, rim_lane(y, z), shift * 128 + lane] = 1
    outgoing = np.zeros((512, 768), np.float32)
    for r in range(4):
        for z in range(16):
            outgoing[(27 + r) * 16 + z, r * 16 + z] = 1
            outgoing[(1 + r) * 16 + z, 64 + r * 16 + z] = 1
    for z in range(16):
        outgoing[31 * 16 + z, 128 + z] = 1
        outgoing[z, 144 + z] = 1
    for y in range(32):
        outgoing[y * 16 + 15, 160 + y] = 1
        outgoing[y * 16, 192 + y] = 1
        for c in range(4):
            outgoing[y * 16 + 11 + c, 256 + c * 32 + y] = 1
            outgoing[y * 16 + 1 + c, 384 + c * 32 + y] = 1
    for k in range(4):
        for r in range(5):
            for c in range(5):
                y = r if k // 2 else 27 + r
                z = c if k % 2 else 11 + c
                outgoing[y * 16 + z, 512 + k * 32 + r * 5 + c] = 1
    for (y, z), i in EDGE.items():
        outgoing[y * 16 + z, 640 + i] = 1
    second = np.zeros((9, 256, 256), np.float32)
    back = np.zeros((5, 256, 256), np.float32)
    for dy in range(3):
        for dz in range(3):
            tap = dy * 3 + dz
            for (y, z), lane in ring.items():
                second[tap, wide[(y + dy - 1, z + dz - 1)], lane] = 1
            for y in range(16):
                for z in range(8):
                    source = ring[(y - dy + 1, z - dz + 1)]
                    back[tap // 2, source, (tap % 2) * 128 + y * 8 + z] = 1
    fold = np.zeros((128, 2048), np.float32)
    for phase in range(8):
        px, py, pz = phase // 4, phase // 2 % 2, phase % 2
        for tx in range(3):
            for ty in range(3):
                for tz in range(3):
                    for channel in range(4):
                        x, y, z = tx + px, ty + py, tz + pz
                        row = (y * 4 + z) * 16 + ((x - 1) % 4) * 4 + channel
                        fold[((tx * 3 + ty) * 3 + tz) * 4 + channel, phase * 256 + row] = 1
    pool = np.zeros((512, 128), np.float32)
    for x in range(4):
        for y in range(16):
            for z in range(8):
                pool[x * 128 + y * 8 + z, x * 32 + (y // 2) * 4 + z // 2] = 1
    cot_out = np.zeros((256, 256), np.float32)
    cot_in = np.zeros((384, 1024), np.float32)
    for x in range(8):
        for y in range(8):
            cot_out[x * 32 + y * 4, x * 8 + y] = 1
            cot_out[x * 32 + y * 4 + 3, 64 + x * 8 + y] = 1
        for z in range(4):
            cot_out[x * 32 + z, 128 + x * 4 + z] = 1
            cot_out[x * 32 + 28 + z, 160 + x * 4 + z] = 1
        for (y, z), lane in ring.items():
            if lane < 128:
                continue
            if 0 <= y < 16:
                source = x * 8 + y // 2 + (64 if z < 0 else 0)
            elif 0 <= z < 8:
                source = 128 + x * 4 + z // 2 + (32 if y < 0 else 0)
            else:
                source = 256 + x * 4 + (3 if z < 0 else 0) + (32 if y < 0 else 0)
            cot_in[source, x * 128 + lane - 128] = 1
    sides = np.zeros((8, 256), np.float32)
    for (y, z), lane in wide.items():
        sides[:4, lane] = (y < 0, y >= 16, z < 0, z >= 8)
    sixteen = (inside, nearby, around, outgoing, second, back, fold, pool, cot_out, cot_in)
    return tuple(m.astype(jnp.bfloat16) for m in sixteen) + (sides,)


def mm(a, b):
    return jnp.dot(a, b, preferred_element_type=F32)


def mm_nt(a, b):
    return lax.dot_general(a, b, (((1,), (1,)), ((), ())), preferred_element_type=F32)


def identity(n):
    rows = lax.broadcasted_iota(jnp.int32, (n, n), 0)
    return jnp.where(rows == lax.broadcasted_iota(jnp.int32, (n, n), 1), 1.0, 0.0).astype(BF16)


def leaky(t):
    return jnp.where(t > 0, t, 0.3 * t)


def slope(t):
    return jnp.where(t > 0, jnp.float32(1.0), jnp.float32(0.3))


def strip(block, start, width):
    parts = 128 // width
    rows = block.shape[0] // parts
    lane = lax.broadcasted_iota(jnp.int32, (1, 128), 1)
    packed = jnp.zeros((rows, 128), F32)
    for j in range(parts):
        piece = block[rows * j : rows * j + rows]
        shift = (width * j - start) % 128
        packed = jnp.where(lane // width == j, pltpu.roll(piece, shift, 1) if shift else piece, packed)
    return packed


def unstrip(packed, start, width, j):
    shift = (start - width * j) % 128
    return pltpu.roll(packed, shift, 1) if shift else packed


def split(t):
    high = t.astype(BF16)
    return high, (t - high.astype(F32)).astype(BF16)


FACES = ((1, 0), (-1, 0), (0, 1), (0, -1))
CORNERS = ((1, 1), (1, -1), (-1, 1), (-1, -1))
DIRS = FACES + CORNERS
XY = tuple((a, b) for a in range(4) for b in range(4) if (a, b) != (0, 0))
S_RIM, S_CORE, S_XY, S_Z, S_AG, S_FXY, S_FZ = 0, 8, 16, 31, 38, 53, 68


def body(
    vol, k1, w2, cot, inside_h, nearby_h, around_h, outgoing_h, second_h, back_h, fold_h, pool_h, cot_out_h, cot_in_h,
    sides, feat_out, grad_out, second_out, first_out,
    inside, nearby, around, outgoing, second, back, fold, pool, cot_out, cot_in,
    rows32, lraw, y_send, z_send, c_send, y_recv, z_recv, c_recv, edge_a, edge_b, early,
    x4, x4i, pre1, weights1, forward2, backward2, k1s,
    p2, b2i, b2r, t2i, t2r, spread_i, spread_r, pooled, pg, gshift, bg, t3, g1,
    total, core_in, xy_in, z_in, final, first_part, first_in, first_xy, first_z, first_final,
    local_sem, send_sem, recv_sem,
):
    dp, g, s = lax.axis_index("dp"), lax.axis_index("gx"), lax.axis_index("yz")
    by, bz = s // PZ, s % PZ
    yi, zi = s % NY, s // NY
    other = (dp, 1 - g, s)
    near = [(dp, g, ((by + a) % PY) * PZ + (bz + b) % PZ) for a, b in DIRS]
    flat = [((dp + a) % 4, g, zi * NY + (yi + b) % NY) for a, b in XY]
    tall = [(dp, g, ((zi + k) % 8) * NY + yi) for k in range(1, 8)]

    loads = [
        pltpu.make_async_copy(a, b, local_sem.at[i])
        for i, (a, b) in enumerate(
            (
                (outgoing_h, outgoing), (cot_out_h, cot_out), (fold_h, fold), (pool_h, pool), (inside_h, inside),
                (cot_in_h, cot_in), (nearby_h, nearby), (around_h, around), (second_h, second), (back_h, back),
            )
        )
    ]
    for load in loads:
        load.start()

    barrier = pltpu.get_barrier_semaphore()
    everyone = [other] + near + flat + tall
    for device in everyone:
        pl.semaphore_signal(barrier, inc=1, device_id=device, device_id_type=MESH)

    def remote(source, target, slot, device):
        return pltpu.make_async_remote_copy(
            src_ref=source, dst_ref=target, send_sem=send_sem.at[slot], recv_sem=recv_sem.at[slot],
            device_id=device, device_id_type=MESH,
        )

    def valid(a, b):
        ok = jnp.logical_and(
            jnp.logical_and(by + a >= 0, by + a < PY), jnp.logical_and(bz + b >= 0, bz + b < PZ)
        )
        return jnp.where(ok, jnp.float32(1.0), jnp.float32(0.0))

    lane = lax.broadcasted_iota(jnp.int32, (1, 128), 1)

    for x in range(32):
        rows32[4 * x : 4 * x + 4, :] = vol[:, x * 512 : (x + 1) * 512].astype(F32)
    lraw[0:128, 0:512] = rows32[...].astype(BF16)
    loads[0].wait()
    out = mm(lraw[0:128, 0:512], outgoing[...])
    loads[1].wait()
    strips = mm(cot[...], cot_out[...])
    for i, (a, b) in enumerate(DIRS):
        ok = valid(a, b)
        if i < 2:
            y_send[i, 0:64] = (strip(out[:, 0:128], 64 * i, 64) * ok).astype(BF16)
            y_send[i, 64:80] = (strip(out[:, 128:256], 16 * i, 16) * ok).astype(BF16)
            y_send[i, 80:96] = (strip(strips[:, 128:256], 32 - 32 * i, 32) * ok).astype(BF16)
        elif i < 4:
            j = i - 2
            z_send[j, 0:128] = (out[:, 256 + 128 * j : 384 + 128 * j] * ok).astype(BF16)
            z_send[j, 128:160] = (strip(out[:, 128:256], 32 + 32 * j, 32) * ok).astype(BF16)
            z_send[j, 160:192] = (strip(strips[:, 0:128], 64 - 64 * j, 64) * ok).astype(BF16)
        else:
            j = i - 4
            c_send[j, 0:32] = (strip(out[:, 512:640], 32 * j, 32) * ok).astype(BF16)
            c_send[j, 32:48] = (strip(strips[:, 128:256], 32 if a > 0 else 0, 32) * ok).astype(BF16)

    pl.semaphore_wait(barrier, len(everyone))
    rim_copies = []
    for i in (4, 5, 6, 7, 2, 3, 0, 1):
        pair = ((y_send, y_recv), (z_send, z_recv), (c_send, c_recv), (c_send, c_recv))[i // 2]
        slot = i - 4 if i >= 4 else i % 2
        copy = remote(pair[0].at[slot], pair[1].at[slot], S_RIM + i, near[i])
        copy.start()
        rim_copies.append(copy)
    mine = pl.multiple_of(jnp.where(g == 0, 112, 0), 16)
    early_edge = remote(lraw.at[pl.ds(mine, 16), 0:512], edge_a, S_CORE, other)
    early_edge.start()
    core_copies = [early_edge]
    lraw[0:128, 1152:1280] = out[:, 640:768].astype(BF16)

    k1s[...] = jnp.zeros_like(k1s)
    for tap in range(27):
        k1s[4 * tap : 4 * tap + 4, :] = k1[tap].astype(F32)
    loads[2].wait()
    k1t = mm_nt(identity(32), k1s[...].astype(BF16)).astype(BF16)
    for phase in range(8):
        weights1[32 * phase : 32 * phase + 32, :] = mm(k1t, fold[:, 256 * phase : 256 * phase + 256]).astype(BF16)
    eye = identity(64)
    for x in range(3):
        block = w2[9 * x : 9 * x + 9].reshape(288, 64)
        forward2[64 * x : 64 * x + 64, :] = mm_nt(eye, block).astype(BF16)
        for a in (0, 2, 4, 6):
            both = jnp.concatenate([w2[9 * x + a].astype(F32), w2[9 * x + a + 1].astype(F32)], axis=1)
            backward2[32 * x : 32 * x + 32, 64 * a : 64 * a + 128] = both.astype(BF16)
        backward2[32 * x : 32 * x + 32, 512:576] = w2[9 * x + 8]
    loads[3].wait()
    for half in range(2):
        spread_i[:, 512 * half : 512 * half + 512] = mm_nt(cot[:, 128 * half : 128 * half + 128], pool[...])
    far = pl.multiple_of(g * (17 * 32), 32)
    p2[pl.ds(far, 32), :] = jnp.zeros((32, 256), BF16)
    far = pl.multiple_of(g * (17 * 64), 64)
    pg[pl.ds(far, 64), :] = jnp.zeros((64, 256), BF16)
    gshift[...] = jnp.zeros_like(gshift)
    early_edge.wait_recv()
    first_core = jnp.where(g == 0, jnp.float32(1.0), jnp.float32(0.0))
    half_row = lax.broadcasted_iota(jnp.int32, (8, 1), 0)

    def beyond(edge):
        edge = edge.astype(F32)
        edge = jnp.where(half_row < 4, edge[0:8] * first_core, edge[8:16] * (1.0 - first_core))
        return jnp.concatenate([edge, jnp.zeros_like(edge)], axis=0).astype(BF16)

    lraw[128:144, 0:512] = beyond(edge_a[...])
    for load in loads[4:]:
        load.wait()

    def early_step(step, carry):
        early[step] = mm(lraw[:, 0:512], inside[step])
        return carry

    lax.fori_loop(0, 8, early_step, 0)

    for copy in rim_copies:
        copy.wait_recv()
    for j in range(2):
        low = unstrip(y_recv[0, 0:64].astype(F32), 0, 64, j)
        high = unstrip(y_recv[1, 0:64].astype(F32), 64, 64, j)
        lraw[64 * j : 64 * j + 64, 768:896] = jnp.where(lane < 64, low, high).astype(BF16)
    lraw[0:128, 896:1024] = z_recv[0, 0:128]
    lraw[0:128, 1024:1152] = z_recv[1, 0:128]
    y_low, y_high = y_recv[0, 64:80].astype(F32), y_recv[1, 64:80].astype(F32)
    for j in range(8):
        at = slice(128 + 16 * (j % 2), 144 + 16 * (j % 2))
        z_low, z_high = z_recv[0, at].astype(F32), z_recv[1, at].astype(F32)
        block = jnp.where(lane < 16, unstrip(y_low, 0, 16, j), unstrip(y_high, 16, 16, j))
        block = jnp.where(lane < 32, block, unstrip(z_low, 32, 32, j // 2))
        block = jnp.where(lane < 64, block, unstrip(z_high, 64, 32, j // 2))
        lraw[16 * j : 16 * j + 16, 512:640] = block.astype(BF16)
    for j in range(4):
        block = jnp.zeros((32, 128), F32)
        for k in range(4):
            block = jnp.where(lane // 32 == k, unstrip(c_recv[k, 0:32].astype(F32), 32 * k, 32, j), block)
        lraw[32 * j : 32 * j + 32, 640:768] = block.astype(BF16)
    copy = remote(lraw.at[pl.ds(mine, 16), 512:1280], edge_b, S_CORE + 1, other)
    copy.start()
    core_copies.append(copy)
    copy.wait_recv()
    lraw[128:144, 512:1280] = beyond(edge_b[...])

    def gather_step(step, carry):
        mid = mm(lraw[:, 512:768], nearby[step]) + early[step]
        rim = mm(lraw[:, 512:1280], around[step])
        low = half_row < 4
        for shift in range(2):
            at = pl.multiple_of(step * 32 + shift * 16, 16)
            lanes = slice(128 * shift, 128 * shift + 128)
            for x in range(16):
                for got, side in ((mid[:, lanes], 0), (rim[:, lanes], 1)):
                    after = got[8 * x + 8 : 8 * x + 16]
                    before = got[8 * x - 8 : 8 * x] if x else got[128:136]
                    block = jnp.concatenate([got[8 * x : 8 * x + 8], jnp.where(low, after, before)], axis=0)
                    block = block.astype(BF16)
                    x4[x, pl.ds(at, 16), 128 * side : 128 * side + 128] = block
                    if side == 0:
                        x4i[pl.ds(at, 16), 128 * x : 128 * x + 128] = block
        return carry

    lax.fori_loop(0, 8, gather_step, 0)

    def flag(test):
        return jnp.where(test, jnp.float32(1.0), jnp.float32(0.0))

    outside = jnp.maximum(
        jnp.maximum(sides[0:1, :] * flag(by == 0), sides[1:2, :] * flag(by == PY - 1)),
        jnp.maximum(sides[2:3, :] * flag(bz == 0), sides[3:4, :] * flag(bz == PZ - 1)),
    )
    scale = (1.0 - outside) * 0.125

    def first_layer(x, carry):
        pre = mm(weights1[...], x4[x])
        pre1[x] = pre[:, 0:128]
        act = leaky(pre[0:32])
        for phase in range(1, 8):
            act = act + leaky(pre[32 * phase : 32 * phase + 32])
        p2[pl.ds(pl.multiple_of(32 * x + 32, 32), 32), :] = (act * scale).astype(BF16)
        return carry

    lax.fori_loop(0, 16, first_layer, 0)
    near_src = pl.multiple_of(jnp.where(g == 0, 16 * 32, 32), 32)
    near_dst = pl.multiple_of(jnp.where(g == 0, 0, 17 * 32), 32)
    copy = remote(p2.at[pl.ds(near_src, 32), :], p2.at[pl.ds(near_dst, 32), :], S_CORE + 2, other)
    copy.start()
    core_copies.append(copy)

    zs, ys, cs = [], [], []
    for j in range(2):
        low, high = z_recv[0, 160:192].astype(F32), z_recv[1, 160:192].astype(F32)
        zs.append(jnp.where(lane >= 64, unstrip(low, 64, 64, j), unstrip(high, 0, 64, j)))
    late = lane % 4 == 3
    for j in range(4):
        low, high = y_recv[0, 80:96].astype(F32), y_recv[1, 80:96].astype(F32)
        ys.append(jnp.where(lane >= 32, unstrip(low, 32, 32, j), unstrip(high, 0, 32, j)))
        ends = [unstrip(c_recv[k, 32:48].astype(F32), 32 if k < 2 else 0, 32, j) for k in range(4)]
        cs.append(
            jnp.where(lane >= 32, jnp.where(late, ends[0], ends[1]), jnp.where(late, ends[2], ends[3]))
        )
    zs, ys, cs = (jnp.concatenate(parts, axis=0) for parts in (zs, ys, cs))
    rim = jnp.concatenate([zs, ys, cs], axis=1).astype(BF16)
    spread_r[...] = mm(rim, cot_in[...])

    copy.wait_recv()

    def shift_step(tap, carry):
        got = mm(p2[...], second[tap])
        at = pl.multiple_of(tap * 32, 32)
        for x in range(18):
            block = got[32 * x : 32 * x + 32].astype(BF16)
            b2i[pl.ds(at, 32), 128 * x : 128 * x + 128] = block[:, 0:128]
            b2r[pl.ds(at, 32), 128 * x : 128 * x + 128] = block[:, 128:256]
        return carry

    lax.fori_loop(0, 9, shift_step, 0)

    def second_layer(chunk, carry):
        at = pl.ds(pl.multiple_of(chunk * 256, 256), 256)
        t2i[:, at] = mm(forward2[...], b2i[:, at])
        t2r[:, at] = mm(forward2[...], b2r[:, at])
        return carry

    lax.fori_loop(0, 9, second_layer, 0)

    for half in range(8):
        lifted = spread_i[:, 128 * half : 128 * half + 128] * 0.125
        lifted_rim = spread_r[:, 128 * half : 128 * half + 128] * 0.125
        pair = jnp.zeros((64, 128), F32)
        for x in (2 * half, 2 * half + 1):
            at = [slice(128 * (x + d), 128 * (x + d) + 128) for d in range(3)]
            pre = t2i[0:64, at[0]] + t2i[64:128, at[1]] + t2i[128:192, at[2]]
            pair = pair + leaky(pre)
            grad = (lifted * slope(pre)).astype(BF16)
            pg[64 * x + 64 : 64 * x + 128, 0:128] = grad
            for d in range(3):
                gshift[64 * d : 64 * d + 64, at[d]] = grad
            pre = t2r[0:64, at[0]] + t2r[64:128, at[1]] + t2r[128:192, at[2]]
            pg[64 * x + 64 : 64 * x + 128, 128:256] = (lifted_rim * slope(pre)).astype(BF16)
        high, low = split(pair)
        at = slice(128 * (half % 4), 128 * (half % 4) + 128)
        pooled[half // 4, 0:64, at] = high
        pooled[half // 4, 64:128, at] = low
    near_src = pl.multiple_of(jnp.where(g == 0, 16 * 64, 64), 64)
    near_dst = pl.multiple_of(jnp.where(g == 0, 0, 17 * 64), 64)
    copy = remote(pg.at[pl.ds(near_src, 64), :], pg.at[pl.ds(near_dst, 64), :], S_CORE + 3, other)
    copy.start()
    core_copies.append(copy)
    for half in range(2):
        sums = mm(pooled[half], pool[...])
        feat_out[:, 128 * half : 128 * half + 128] = ((sums[0:64] + sums[64:128]) * 0.125).astype(BF16)

    grad2 = mm_nt(b2i[...], gshift[...])
    total[0:288, :] = grad2[:, 0:128]
    total[288:432, 0:64] = grad2[0:144, 128:192]
    total[288:432, 64:128] = grad2[144:288, 128:192]
    total[432:512, :] = jnp.zeros((80, 128), F32)
    mine = pl.multiple_of(g * 256, 256)
    theirs = pl.multiple_of((1 - g) * 256, 256)
    halves = remote(total.at[pl.ds(theirs, 256), :], core_in, S_CORE + 4, other)
    halves.start()
    core_copies.append(halves)
    copy.wait_recv()

    def back_step(step, carry):
        got = mm(pg[...], back[step])
        at = pl.multiple_of(step * 128, 128)
        for x in range(18):
            block = got[64 * x : 64 * x + 64].astype(BF16)
            bg[pl.ds(at, 64), 128 * x : 128 * x + 128] = block[:, 0:128]
            bg[pl.ds(at + 64, 64), 128 * x : 128 * x + 128] = block[:, 128:256]
        return carry

    lax.fori_loop(0, 5, back_step, 0)

    halves.wait_recv()
    core_in[...] = core_in[...] + total[pl.ds(mine, 256), :]
    xy_copies = []
    for i, (a, b) in enumerate(XY):
        piece = ((dp + a) % 4) * 4 + (yi + b) % 4
        source = core_in.at[pl.ds(pl.multiple_of(piece * 16, 16), 16), :]
        copy = remote(source, xy_in.at[i], S_XY + i, flat[i])
        copy.start()
        xy_copies.append(copy)

    def back_layer(chunk, carry):
        at = pl.ds(pl.multiple_of(chunk * 256, 256), 256)
        t3[:, at] = mm(backward2[...], bg[0:576, at])
        return carry

    lax.fori_loop(0, 9, back_layer, 0)

    for x in range(16):
        grad = (
            t3[0:32, 128 * (x + 2) : 128 * (x + 3)]
            + t3[32:64, 128 * (x + 1) : 128 * (x + 2)]
            + t3[64:96, 128 * x : 128 * (x + 1)]
        )
        grad_out[pl.ds(x, 32, stride=16), :] = grad
        eighth = grad * 0.125
        for phase in range(8):
            at = slice(32 * phase, 32 * phase + 32)
            g1[at, 128 * x : 128 * x + 128] = (eighth * slope(pre1[x, at, :])).astype(BF16)
    wide = mm_nt(g1[...], x4i[...])
    partial = jnp.zeros((64, 128), F32)
    for phase in range(8):
        high, low = split(wide[32 * phase : 32 * phase + 32])
        partial = partial + mm_nt(jnp.concatenate([high, low], axis=0), fold[:, 256 * phase : 256 * phase + 256])
    first_part[...] = partial[0:32] + partial[32:64]

    my_half = pl.multiple_of(g * 16, 16)
    their_half = pl.multiple_of((1 - g) * 16, 16)
    swap = remote(first_part.at[pl.ds(their_half, 16), :], first_in, S_CORE + 5, other)
    swap.start()
    core_copies.append(swap)
    spot = dp * 4 + yi
    place = pl.multiple_of(spot * 16, 16)
    part = core_in[pl.ds(place, 16), :]
    for i, copy in enumerate(xy_copies):
        copy.wait_recv()
        part = part + xy_in[i]
    z_in[zi] = part
    z_copies = []
    for k in range(7):
        copy = remote(z_in.at[zi], z_in.at[zi], S_Z + k, tall[k])
        copy.start()
        z_copies.append(copy)
    swap.wait_recv()
    first_xy[spot] = first_in[...] + first_part[pl.ds(my_half, 16), :]
    fxy_copies = []
    for i in range(15):
        copy = remote(first_xy.at[spot], first_xy.at[spot], S_FXY + i, flat[i])
        copy.start()
        fxy_copies.append(copy)
    for copy in z_copies:
        copy.wait_recv()
    part = z_in[0]
    for k in range(1, 8):
        part = part + z_in[k]
    rows = pl.ds(pl.multiple_of(mine + place, 16), 16)
    final[rows, :] = part
    ag_copies = []
    for i in range(15):
        copy = remote(final.at[rows, :], final.at[rows, :], S_AG + i, flat[i])
        copy.start()
        ag_copies.append(copy)
    for copy in fxy_copies:
        copy.wait_recv()
    part = first_xy[0]
    for k in range(1, 16):
        part = part + first_xy[k]
    first_z[zi] = part
    fz_copies = []
    for k in range(7):
        copy = remote(first_z.at[zi], first_z.at[zi], S_FZ + k, tall[k])
        copy.start()
        fz_copies.append(copy)
    for copy in ag_copies:
        copy.wait_recv()
    half = pl.ds(mine, 256)
    joined = remote(final.at[half, :], final.at[half, :], S_CORE + 6, other)
    joined.start()
    core_copies.append(joined)
    for copy in fz_copies:
        copy.wait_recv()
    part = first_z[0]
    for k in range(1, 8):
        part = part + first_z[k]
    half = pl.ds(my_half, 16)
    first_final[half, :] = part
    copy = remote(first_final.at[half, :], first_final.at[half, :], S_CORE + 7, other)
    copy.start()
    core_copies.append(copy)
    joined.wait_recv()
    second_out[...] = final[0:432, :]
    copy.wait_recv()
    first_out[...] = first_final[...]

    for copy in rim_copies + core_copies + xy_copies + z_copies + ag_copies + fxy_copies + fz_copies:
        copy.wait_send()


def arrange(feat, grad, second, first, feat_out, grad_out, first_out, second_out):
    feat_out[...] = feat[...]
    grad_out[...] = grad[...]
    for a in range(9):
        at = slice(32 * a, 32 * a + 32)
        second_out[a] = second[at, 0:64]
        second_out[9 + a] = second[at, 64:128]
    for a in range(36):
        row = 288 + (8 * a) % 144
        lanes = slice(0, 64) if a < 18 else slice(64, 128)
        second_out[18 + a // 4, 8 * (a % 4) : 8 * (a % 4) + 8, :] = second[row : row + 8, lanes]
    flipped = first[...].T
    for tap in range(27):
        first_out[tap] = flipped[4 * tap : 4 * tap + 4, :]


def on_device(volumes, first_kernel, second_kernel, cotangent):
    consts = matrices()
    here = pl.BlockSpec(memory_space=pltpu.VMEM)
    there = pl.BlockSpec(memory_space=pltpu.HBM)
    vmem = pltpu.VMEM
    scratch = [vmem(m.shape, BF16) for m in consts[:-1]] + [
        vmem((128, 512), F32), vmem((144, KRAW), BF16),
        vmem((2, 96, 128), BF16), vmem((2, 192, 128), BF16), vmem((4, 48, 128), BF16),
        vmem((2, 96, 128), BF16), vmem((2, 192, 128), BF16), vmem((4, 48, 128), BF16),
        vmem((16, 512), BF16), vmem((16, 768), BF16), vmem((8, 144, 256), F32),
        vmem((16, 256, 256), BF16), vmem((256, 2048), BF16), vmem((16, 256, 128), F32),
        vmem((256, 256), BF16), vmem((192, 288), BF16), vmem((96, 576), BF16), vmem((128, 32), F32),
        vmem((576, 256), BF16), vmem((288, 2304), BF16), vmem((288, 2304), BF16),
        vmem((192, 2304), F32), vmem((192, 2304), F32), vmem((64, 1024), F32), vmem((64, 1024), F32),
        vmem((2, 128, 512), BF16), vmem((1152, 256), BF16), vmem((192, 2304), BF16),
        vmem((640, 2304), BF16), vmem((96, 2304), F32), vmem((256, 2048), BF16),
        vmem((512, 128), F32), vmem((256, 128), F32), vmem((15, 16, 128), F32), vmem((8, 16, 128), F32), vmem((512, 128), F32),
        vmem((32, 128), F32), vmem((16, 128), F32), vmem((16, 16, 128), F32), vmem((8, 16, 128), F32), vmem((32, 128), F32),
        pltpu.SemaphoreType.DMA((10,)), pltpu.SemaphoreType.DMA((75,)), pltpu.SemaphoreType.DMA((75,)),
    ]
    parts = pl.pallas_call(
        body,
        out_shape=(
            jax.ShapeDtypeStruct((64, 256), BF16),
            jax.ShapeDtypeStruct((512, 128), F32),
            jax.ShapeDtypeStruct((432, 128), F32),
            jax.ShapeDtypeStruct((32, 128), F32),
        ),
        in_specs=[here] * 4 + [there] * 10 + [here],
        out_specs=(here,) * 4,
        scratch_shapes=scratch,
        compiler_params=pltpu.CompilerParams(
            collective_id=0, has_side_effects=True, vmem_limit_bytes=60 * 1024 * 1024
        ),
    )(
        volumes.reshape(4, 16384),
        first_kernel.transpose(2, 3, 4, 1, 0).reshape(27, 4, 32),
        second_kernel.transpose(2, 3, 4, 1, 0).reshape(27, 32, 64),
        cotangent.reshape(64, 256),
        *(jnp.asarray(m) for m in consts),
    )
    features, act_grad, first_grad, second_grad = pl.pallas_call(
        arrange,
        out_shape=(
            jax.ShapeDtypeStruct((64, 256), BF16),
            jax.ShapeDtypeStruct((512, 128), F32),
            jax.ShapeDtypeStruct((27, 4, 32), F32),
            jax.ShapeDtypeStruct((27, 32, 64), F32),
        ),
        in_specs=[here] * 4,
        out_specs=(here,) * 4,
    )(*parts)
    return (
        features.reshape(1, 64, 1, 1, 256),
        act_grad.reshape(1, 32, 1, 1, 2048),
        first_grad.reshape(3, 3, 3, 4, 32).transpose(4, 3, 0, 1, 2),
        second_grad.reshape(3, 3, 3, 32, 64).transpose(4, 3, 0, 1, 2),
    )


def solution(mesh):
    placed = (P("dp", None, "gx", "yz", None), P(), P(), P("dp", None, "gx", "yz", None))
    return jax.shard_map(
        on_device,
        mesh=mesh,
        in_specs=placed,
        out_specs=(P("dp", None, "gx", "yz", None), P("dp", None, "gx", "yz", None), P(), P()),
        check_vma=False,
    )
```

```python
import functools

import jax
import jax.numpy as jnp
import numpy as np
from jax import lax
from jax.experimental import pallas as pl
from jax.experimental.pallas import tpu as pltpu
from jax.sharding import PartitionSpec as P

F32 = jnp.float32
BF16 = jnp.bfloat16
PY, PZ = 4, 8
NY = 4
KRAW = 1280
MESH = pl.DeviceIdType.MESH


def plane_order(rim):
    lanes = {(y, z): y * 8 + z for y in range(16) for z in range(8)}
    for y in range(-rim, 16 + rim):
        for z in range(-rim, 8 + rim):
            if (y, z) not in lanes:
                lanes[(y, z)] = len(lanes)
    return lanes


def on_edge(y, z):
    return y in (0, 31) or z in (0, 15)


EDGE = {place: i for i, place in enumerate((y, z) for y in range(32) for z in range(16) if on_edge(y, z))}


def rim_lane(y, z):
    if 0 <= y < 32 and 0 <= z < 16:
        return 640 + EDGE[(y, z)]
    if 0 <= z < 16:
        if y in (-1, 32):
            return (0 if y < 0 else 16) + z
        return 256 + ((y + 5) * 16 if y < 0 else 64 + (y - 33) * 16) + z
    if 0 <= y < 32:
        if z in (-1, 16):
            return (32 if z < 0 else 64) + y
        return 384 + ((z + 5) * 32 if z < 0 else 128 + (z - 17) * 32) + y
    row = y + 5 if y < 0 else y - 32
    col = z + 5 if z < 0 else z - 16
    return 128 + ((y >= 32) * 2 + (z >= 16)) * 32 + row * 5 + col


@functools.cache
def matrices():
    wide, ring = plane_order(2), plane_order(1)
    inside = np.zeros((8, 512, 256), np.float32)
    nearby = np.zeros((8, 256, 256), np.float32)
    around = np.zeros((8, 768, 256), np.float32)
    for dy in range(4):
        for dz in range(4):
            step, shift = divmod(dy * 4 + dz, 2)
            for (qy, qz), lane in wide.items():
                y, z = 2 * qy - 1 + dy, 2 * qz - 1 + dz
                if lane >= 128:
                    around[step, rim_lane(y, z), shift * 128 + lane - 128] = 1
                elif 0 <= y < 32 and 0 <= z < 16:
                    inside[step, y * 16 + z, shift * 128 + lane] = 1
                else:
                    nearby[step, rim_lane(y, z), shift * 128 + lane] = 1
    outgoing = np.zeros((512, 768), np.float32)
    for r in range(4):
        for z in range(16):
            outgoing[(27 + r) * 16 + z, r * 16 + z] = 1
            outgoing[(1 + r) * 16 + z, 64 + r * 16 + z] = 1
    for z in range(16):
        outgoing[31 * 16 + z, 128 + z] = 1
        outgoing[z, 144 + z] = 1
    for y in range(32):
        outgoing[y * 16 + 15, 160 + y] = 1
        outgoing[y * 16, 192 + y] = 1
        for c in range(4):
            outgoing[y * 16 + 11 + c, 256 + c * 32 + y] = 1
            outgoing[y * 16 + 1 + c, 384 + c * 32 + y] = 1
    for k in range(4):
        for r in range(5):
            for c in range(5):
                y = r if k // 2 else 27 + r
                z = c if k % 2 else 11 + c
                outgoing[y * 16 + z, 512 + k * 32 + r * 5 + c] = 1
    for (y, z), i in EDGE.items():
        outgoing[y * 16 + z, 640 + i] = 1
    second = np.zeros((9, 256, 256), np.float32)
    back = np.zeros((5, 256, 256), np.float32)
    for dy in range(3):
        for dz in range(3):
            tap = dy * 3 + dz
            for (y, z), lane in ring.items():
                second[tap, wide[(y + dy - 1, z + dz - 1)], lane] = 1
            for y in range(16):
                for z in range(8):
                    source = ring[(y - dy + 1, z - dz + 1)]
                    back[tap // 2, source, (tap % 2) * 128 + y * 8 + z] = 1
    fold = np.zeros((128, 2048), np.float32)
    for phase in range(8):
        px, py, pz = phase // 4, phase // 2 % 2, phase % 2
        for tx in range(3):
            for ty in range(3):
                for tz in range(3):
                    for channel in range(4):
                        x, y, z = tx + px, ty + py, tz + pz
                        row = (y * 4 + z) * 16 + ((x - 1) % 4) * 4 + channel
                        fold[((tx * 3 + ty) * 3 + tz) * 4 + channel, phase * 256 + row] = 1
    pool = np.zeros((512, 128), np.float32)
    for x in range(4):
        for y in range(16):
            for z in range(8):
                pool[x * 128 + y * 8 + z, x * 32 + (y // 2) * 4 + z // 2] = 1
    cot_out = np.zeros((256, 256), np.float32)
    cot_in = np.zeros((384, 1024), np.float32)
    for x in range(8):
        for y in range(8):
            cot_out[x * 32 + y * 4, x * 8 + y] = 1
            cot_out[x * 32 + y * 4 + 3, 64 + x * 8 + y] = 1
        for z in range(4):
            cot_out[x * 32 + z, 128 + x * 4 + z] = 1
            cot_out[x * 32 + 28 + z, 160 + x * 4 + z] = 1
        for (y, z), lane in ring.items():
            if lane < 128:
                continue
            if 0 <= y < 16:
                source = x * 8 + y // 2 + (64 if z < 0 else 0)
            elif 0 <= z < 8:
                source = 128 + x * 4 + z // 2 + (32 if y < 0 else 0)
            else:
                source = 256 + x * 4 + (3 if z < 0 else 0) + (32 if y < 0 else 0)
            cot_in[source, x * 128 + lane - 128] = 1
    sides = np.zeros((8, 256), np.float32)
    for (y, z), lane in wide.items():
        sides[:4, lane] = (y < 0, y >= 16, z < 0, z >= 8)
    sixteen = (inside, nearby, around, outgoing, second, back, fold, pool, cot_out, cot_in)
    return tuple(m.astype(jnp.bfloat16) for m in sixteen) + (sides,)


def mm(a, b):
    return jnp.dot(a, b, preferred_element_type=F32)


def mm_nt(a, b):
    return lax.dot_general(a, b, (((1,), (1,)), ((), ())), preferred_element_type=F32)


def identity(n):
    rows = lax.broadcasted_iota(jnp.int32, (n, n), 0)
    return jnp.where(rows == lax.broadcasted_iota(jnp.int32, (n, n), 1), 1.0, 0.0).astype(BF16)


def leaky(t):
    return jnp.where(t > 0, t, 0.3 * t)


def slope(t):
    return jnp.where(t > 0, jnp.float32(1.0), jnp.float32(0.3))


def strip(block, start, width):
    parts = 128 // width
    rows = block.shape[0] // parts
    lane = lax.broadcasted_iota(jnp.int32, (1, 128), 1)
    packed = jnp.zeros((rows, 128), F32)
    for j in range(parts):
        piece = block[rows * j : rows * j + rows]
        shift = (width * j - start) % 128
        packed = jnp.where(lane // width == j, pltpu.roll(piece, shift, 1) if shift else piece, packed)
    return packed


def unstrip(packed, start, width, j):
    shift = (start - width * j) % 128
    return pltpu.roll(packed, shift, 1) if shift else packed


def split(t):
    high = t.astype(BF16)
    return high, (t - high.astype(F32)).astype(BF16)


FACES = ((1, 0), (-1, 0), (0, 1), (0, -1))
CORNERS = ((1, 1), (1, -1), (-1, 1), (-1, -1))
DIRS = FACES + CORNERS
XY = tuple((a, b) for a in range(4) for b in range(4) if (a, b) != (0, 0))
S_RIM, S_CORE, S_XY, S_Z, S_AG, S_FXY, S_FZ = 0, 8, 16, 31, 38, 53, 68


def body(
    vol_h, k1_h, w2_h, cot_h, inside_h, nearby_h, around_h, outgoing_h, second_h, back_h, fold_h, pool_h, cot_out_h, cot_in_h,
    sides_h, feat_out, grad_out, second_out, first_out,
    vol, k1, w2, cot, sides, feat, grads,
    inside, nearby, around, outgoing, second, back, fold, pool, cot_out, cot_in,
    rows32, lraw, y_send, z_send, c_send, y_recv, z_recv, c_recv, edge_a, edge_b, early,
    x4, x4i, pre1, weights1, forward2, backward2, k1s,
    p2, b2i, b2r, t2i, t2r, spread_i, spread_r, pooled, pg, gshift, bg, t3, g1,
    total, core_in, xy_in, z_in, final, first_part, first_in, first_xy, first_z, first_final,
    local_sem, send_sem, recv_sem,
):
    dp, g, s = lax.axis_index("dp"), lax.axis_index("gx"), lax.axis_index("yz")
    by, bz = s // PZ, s % PZ
    yi, zi = s % NY, s // NY
    other = (dp, 1 - g, s)
    near = [(dp, g, ((by + a) % PY) * PZ + (bz + b) % PZ) for a, b in DIRS]
    flat = [((dp + a) % 4, g, zi * NY + (yi + b) % NY) for a, b in XY]
    tall = [(dp, g, ((zi + k) % 8) * NY + yi) for k in range(1, 8)]

    loads = [
        pltpu.make_async_copy(a, b, local_sem.at[i])
        for i, (a, b) in enumerate(
            (
                (vol_h, vol), (outgoing_h, outgoing), (cot_h, cot), (cot_out_h, cot_out), (k1_h, k1), (w2_h, w2),
                (fold_h, fold), (pool_h, pool), (inside_h, inside), (cot_in_h, cot_in), (nearby_h, nearby),
                (around_h, around), (second_h, second), (back_h, back), (sides_h, sides),
            )
        )
    ]
    for load in loads:
        load.start()

    barrier = pltpu.get_barrier_semaphore()
    everyone = [other] + near + flat + tall
    for device in everyone:
        pl.semaphore_signal(barrier, inc=1, device_id=device, device_id_type=MESH)

    def remote(source, target, slot, device):
        return pltpu.make_async_remote_copy(
            src_ref=source, dst_ref=target, send_sem=send_sem.at[slot], recv_sem=recv_sem.at[slot],
            device_id=device, device_id_type=MESH,
        )

    def valid(a, b):
        ok = jnp.logical_and(
            jnp.logical_and(by + a >= 0, by + a < PY), jnp.logical_and(bz + b >= 0, bz + b < PZ)
        )
        return jnp.where(ok, jnp.float32(1.0), jnp.float32(0.0))

    lane = lax.broadcasted_iota(jnp.int32, (1, 128), 1)

    loads[0].wait()
    for x in range(32):
        rows32[4 * x : 4 * x + 4, :] = vol[:, x * 512 : (x + 1) * 512].astype(F32)
    lraw[0:128, 0:512] = rows32[...].astype(BF16)
    loads[1].wait()
    out = mm(lraw[0:128, 0:512], outgoing[...])
    loads[2].wait()
    loads[3].wait()
    strips = mm(cot[...], cot_out[...])
    for i, (a, b) in enumerate(DIRS):
        ok = valid(a, b)
        if i < 2:
            y_send[i, 0:64] = (strip(out[:, 0:128], 64 * i, 64) * ok).astype(BF16)
            y_send[i, 64:80] = (strip(out[:, 128:256], 16 * i, 16) * ok).astype(BF16)
            y_send[i, 80:96] = (strip(strips[:, 128:256], 32 - 32 * i, 32) * ok).astype(BF16)
        elif i < 4:
            j = i - 2
            z_send[j, 0:128] = (out[:, 256 + 128 * j : 384 + 128 * j] * ok).astype(BF16)
            z_send[j, 128:160] = (strip(out[:, 128:256], 32 + 32 * j, 32) * ok).astype(BF16)
            z_send[j, 160:192] = (strip(strips[:, 0:128], 64 - 64 * j, 64) * ok).astype(BF16)
        else:
            j = i - 4
            c_send[j, 0:32] = (strip(out[:, 512:640], 32 * j, 32) * ok).astype(BF16)
            c_send[j, 32:48] = (strip(strips[:, 128:256], 32 if a > 0 else 0, 32) * ok).astype(BF16)

    pl.semaphore_wait(barrier, len(everyone))
    rim_copies = []
    for i in (4, 5, 6, 7, 2, 3, 0, 1):
        pair = ((y_send, y_recv), (z_send, z_recv), (c_send, c_recv), (c_send, c_recv))[i // 2]
        slot = i - 4 if i >= 4 else i % 2
        copy = remote(pair[0].at[slot], pair[1].at[slot], S_RIM + i, near[i])
        copy.start()
        rim_copies.append(copy)
    mine = pl.multiple_of(jnp.where(g == 0, 112, 0), 16)
    early_edge = remote(lraw.at[pl.ds(mine, 16), 0:512], edge_a, S_CORE, other)
    early_edge.start()
    core_copies = [early_edge]
    lraw[0:128, 1152:1280] = out[:, 640:768].astype(BF16)

    loads[4].wait()
    loads[5].wait()
    k1s[...] = jnp.zeros_like(k1s)
    for tap in range(27):
        k1s[4 * tap : 4 * tap + 4, :] = k1[tap].astype(F32)
    loads[6].wait()
    k1t = mm_nt(identity(32), k1s[...].astype(BF16)).astype(BF16)
    for phase in range(8):
        weights1[32 * phase : 32 * phase + 32, :] = mm(k1t, fold[:, 256 * phase : 256 * phase + 256]).astype(BF16)
    eye = identity(64)
    for x in range(3):
        block = w2[9 * x : 9 * x + 9].reshape(288, 64)
        forward2[64 * x : 64 * x + 64, :] = mm_nt(eye, block).astype(BF16)
        for a in (0, 2, 4, 6):
            both = jnp.concatenate([w2[9 * x + a].astype(F32), w2[9 * x + a + 1].astype(F32)], axis=1)
            backward2[32 * x : 32 * x + 32, 64 * a : 64 * a + 128] = both.astype(BF16)
        backward2[32 * x : 32 * x + 32, 512:576] = w2[9 * x + 8]
    loads[7].wait()
    for half in range(2):
        spread_i[:, 512 * half : 512 * half + 512] = mm_nt(cot[:, 128 * half : 128 * half + 128], pool[...])
    far = pl.multiple_of(g * (17 * 32), 32)
    p2[pl.ds(far, 32), :] = jnp.zeros((32, 256), BF16)
    far = pl.multiple_of(g * (17 * 64), 64)
    pg[pl.ds(far, 64), :] = jnp.zeros((64, 256), BF16)
    gshift[...] = jnp.zeros_like(gshift)
    early_edge.wait_recv()
    first_core = jnp.where(g == 0, jnp.float32(1.0), jnp.float32(0.0))
    half_row = lax.broadcasted_iota(jnp.int32, (8, 1), 0)

    def beyond(edge):
        edge = edge.astype(F32)
        edge = jnp.where(half_row < 4, edge[0:8] * first_core, edge[8:16] * (1.0 - first_core))
        return jnp.concatenate([edge, jnp.zeros_like(edge)], axis=0).astype(BF16)

    lraw[128:144, 0:512] = beyond(edge_a[...])
    for load in loads[8:]:
        load.wait()

    def early_step(step, carry):
        early[step] = mm(lraw[:, 0:512], inside[step])
        return carry

    lax.fori_loop(0, 8, early_step, 0, unroll=True)

    for copy in rim_copies:
        copy.wait_recv()
    for j in range(2):
        low = unstrip(y_recv[0, 0:64].astype(F32), 0, 64, j)
        high = unstrip(y_recv[1, 0:64].astype(F32), 64, 64, j)
        lraw[64 * j : 64 * j + 64, 768:896] = jnp.where(lane < 64, low, high).astype(BF16)
    lraw[0:128, 896:1024] = z_recv[0, 0:128]
    lraw[0:128, 1024:1152] = z_recv[1, 0:128]
    y_low, y_high = y_recv[0, 64:80].astype(F32), y_recv[1, 64:80].astype(F32)
    for j in range(8):
        at = slice(128 + 16 * (j % 2), 144 + 16 * (j % 2))
        z_low, z_high = z_recv[0, at].astype(F32), z_recv[1, at].astype(F32)
        block = jnp.where(lane < 16, unstrip(y_low, 0, 16, j), unstrip(y_high, 16, 16, j))
        block = jnp.where(lane < 32, block, unstrip(z_low, 32, 32, j // 2))
        block = jnp.where(lane < 64, block, unstrip(z_high, 64, 32, j // 2))
        lraw[16 * j : 16 * j + 16, 512:640] = block.astype(BF16)
    for j in range(4):
        block = jnp.zeros((32, 128), F32)
        for k in range(4):
            block = jnp.where(lane // 32 == k, unstrip(c_recv[k, 0:32].astype(F32), 32 * k, 32, j), block)
        lraw[32 * j : 32 * j + 32, 640:768] = block.astype(BF16)
    copy = remote(lraw.at[pl.ds(mine, 16), 512:1280], edge_b, S_CORE + 1, other)
    copy.start()
    core_copies.append(copy)
    copy.wait_recv()
    lraw[128:144, 512:1280] = beyond(edge_b[...])

    def gather_step(step, carry):
        mid = mm(lraw[:, 512:768], nearby[step]) + early[step]
        rim = mm(lraw[:, 512:1280], around[step])
        low = half_row < 4
        for shift in range(2):
            at = pl.multiple_of(step * 32 + shift * 16, 16)
            lanes = slice(128 * shift, 128 * shift + 128)
            for x in range(16):
                for got, side in ((mid[:, lanes], 0), (rim[:, lanes], 1)):
                    after = got[8 * x + 8 : 8 * x + 16]
                    before = got[8 * x - 8 : 8 * x] if x else got[128:136]
                    block = jnp.concatenate([got[8 * x : 8 * x + 8], jnp.where(low, after, before)], axis=0)
                    block = block.astype(BF16)
                    x4[x, pl.ds(at, 16), 128 * side : 128 * side + 128] = block
                    if side == 0:
                        x4i[pl.ds(at, 16), 128 * x : 128 * x + 128] = block
        return carry

    lax.fori_loop(0, 8, gather_step, 0, unroll=True)

    def flag(test):
        return jnp.where(test, jnp.float32(1.0), jnp.float32(0.0))

    outside = jnp.maximum(
        jnp.maximum(sides[0:1, :] * flag(by == 0), sides[1:2, :] * flag(by == PY - 1)),
        jnp.maximum(sides[2:3, :] * flag(bz == 0), sides[3:4, :] * flag(bz == PZ - 1)),
    )
    scale = (1.0 - outside) * 0.125

    def first_layer(x, carry):
        pre = mm(weights1[...], x4[x])
        pre1[x] = pre[:, 0:128]
        act = leaky(pre[0:32])
        for phase in range(1, 8):
            act = act + leaky(pre[32 * phase : 32 * phase + 32])
        p2[pl.ds(pl.multiple_of(32 * x + 32, 32), 32), :] = (act * scale).astype(BF16)
        return carry

    lax.fori_loop(0, 16, first_layer, 0, unroll=True)
    near_src = pl.multiple_of(jnp.where(g == 0, 16 * 32, 32), 32)
    near_dst = pl.multiple_of(jnp.where(g == 0, 0, 17 * 32), 32)
    copy = remote(p2.at[pl.ds(near_src, 32), :], p2.at[pl.ds(near_dst, 32), :], S_CORE + 2, other)
    copy.start()
    core_copies.append(copy)

    zs, ys, cs = [], [], []
    for j in range(2):
        low, high = z_recv[0, 160:192].astype(F32), z_recv[1, 160:192].astype(F32)
        zs.append(jnp.where(lane >= 64, unstrip(low, 64, 64, j), unstrip(high, 0, 64, j)))
    late = lane % 4 == 3
    for j in range(4):
        low, high = y_recv[0, 80:96].astype(F32), y_recv[1, 80:96].astype(F32)
        ys.append(jnp.where(lane >= 32, unstrip(low, 32, 32, j), unstrip(high, 0, 32, j)))
        ends = [unstrip(c_recv[k, 32:48].astype(F32), 32 if k < 2 else 0, 32, j) for k in range(4)]
        cs.append(
            jnp.where(lane >= 32, jnp.where(late, ends[0], ends[1]), jnp.where(late, ends[2], ends[3]))
        )
    zs, ys, cs = (jnp.concatenate(parts, axis=0) for parts in (zs, ys, cs))
    rim = jnp.concatenate([zs, ys, cs], axis=1).astype(BF16)
    spread_r[...] = mm(rim, cot_in[...])

    copy.wait_recv()

    def shift_step(tap, carry):
        got = mm(p2[...], second[tap])
        at = pl.multiple_of(tap * 32, 32)
        for x in range(18):
            block = got[32 * x : 32 * x + 32].astype(BF16)
            b2i[pl.ds(at, 32), 128 * x : 128 * x + 128] = block[:, 0:128]
            b2r[pl.ds(at, 32), 128 * x : 128 * x + 128] = block[:, 128:256]
        return carry

    lax.fori_loop(0, 9, shift_step, 0, unroll=True)

    def second_layer(chunk, carry):
        at = pl.ds(pl.multiple_of(chunk * 256, 256), 256)
        t2i[:, at] = mm(forward2[...], b2i[:, at])
        t2r[:, at] = mm(forward2[...], b2r[:, at])
        return carry

    lax.fori_loop(0, 9, second_layer, 0, unroll=True)

    for half in range(8):
        lifted = spread_i[:, 128 * half : 128 * half + 128] * 0.125
        lifted_rim = spread_r[:, 128 * half : 128 * half + 128] * 0.125
        pair = jnp.zeros((64, 128), F32)
        for x in (2 * half, 2 * half + 1):
            at = [slice(128 * (x + d), 128 * (x + d) + 128) for d in range(3)]
            pre = t2i[0:64, at[0]] + t2i[64:128, at[1]] + t2i[128:192, at[2]]
            pair = pair + leaky(pre)
            grad = (lifted * slope(pre)).astype(BF16)
            pg[64 * x + 64 : 64 * x + 128, 0:128] = grad
            for d in range(3):
                gshift[64 * d : 64 * d + 64, at[d]] = grad
            pre = t2r[0:64, at[0]] + t2r[64:128, at[1]] + t2r[128:192, at[2]]
            pg[64 * x + 64 : 64 * x + 128, 128:256] = (lifted_rim * slope(pre)).astype(BF16)
        high, low = split(pair)
        at = slice(128 * (half % 4), 128 * (half % 4) + 128)
        pooled[half // 4, 0:64, at] = high
        pooled[half // 4, 64:128, at] = low
    near_src = pl.multiple_of(jnp.where(g == 0, 16 * 64, 64), 64)
    near_dst = pl.multiple_of(jnp.where(g == 0, 0, 17 * 64), 64)
    copy = remote(pg.at[pl.ds(near_src, 64), :], pg.at[pl.ds(near_dst, 64), :], S_CORE + 3, other)
    copy.start()
    core_copies.append(copy)
    for half in range(2):
        sums = mm(pooled[half], pool[...])
        feat[:, 128 * half : 128 * half + 128] = ((sums[0:64] + sums[64:128]) * 0.125).astype(BF16)
    stores = [pltpu.make_async_copy(feat, feat_out, local_sem.at[15])]
    stores[0].start()

    grad2 = mm_nt(b2i[...], gshift[...])
    total[0:288, :] = grad2[:, 0:128]
    total[288:432, 0:64] = grad2[0:144, 128:192]
    total[288:432, 64:128] = grad2[144:288, 128:192]
    total[432:512, :] = jnp.zeros((80, 128), F32)
    mine = pl.multiple_of(g * 256, 256)
    theirs = pl.multiple_of((1 - g) * 256, 256)
    halves = remote(total.at[pl.ds(theirs, 256), :], core_in, S_CORE + 4, other)
    halves.start()
    core_copies.append(halves)
    copy.wait_recv()

    def back_step(step, carry):
        got = mm(pg[...], back[step])
        at = pl.multiple_of(step * 128, 128)
        for x in range(18):
            block = got[64 * x : 64 * x + 64].astype(BF16)
            bg[pl.ds(at, 64), 128 * x : 128 * x + 128] = block[:, 0:128]
            bg[pl.ds(at + 64, 64), 128 * x : 128 * x + 128] = block[:, 128:256]
        return carry

    lax.fori_loop(0, 5, back_step, 0, unroll=True)

    halves.wait_recv()
    core_in[...] = core_in[...] + total[pl.ds(mine, 256), :]
    xy_copies = []
    for i, (a, b) in enumerate(XY):
        piece = ((dp + a) % 4) * 4 + (yi + b) % 4
        source = core_in.at[pl.ds(pl.multiple_of(piece * 16, 16), 16), :]
        copy = remote(source, xy_in.at[i], S_XY + i, flat[i])
        copy.start()
        xy_copies.append(copy)

    def back_layer(chunk, carry):
        at = pl.ds(pl.multiple_of(chunk * 256, 256), 256)
        t3[:, at] = mm(backward2[...], bg[0:576, at])
        return carry

    lax.fori_loop(0, 9, back_layer, 0, unroll=True)

    for x in range(16):
        grad = (
            t3[0:32, 128 * (x + 2) : 128 * (x + 3)]
            + t3[32:64, 128 * (x + 1) : 128 * (x + 2)]
            + t3[64:96, 128 * x : 128 * (x + 1)]
        )
        grads[pl.ds(x, 32, stride=16), :] = grad
        eighth = grad * 0.125
        for phase in range(8):
            at = slice(32 * phase, 32 * phase + 32)
            g1[at, 128 * x : 128 * x + 128] = (eighth * slope(pre1[x, at, :])).astype(BF16)
    stores.append(pltpu.make_async_copy(grads, grad_out, local_sem.at[16]))
    stores[1].start()
    wide = mm_nt(g1[...], x4i[...])
    partial = jnp.zeros((64, 128), F32)
    for phase in range(8):
        high, low = split(wide[32 * phase : 32 * phase + 32])
        partial = partial + mm_nt(jnp.concatenate([high, low], axis=0), fold[:, 256 * phase : 256 * phase + 256])
    first_part[...] = partial[0:32] + partial[32:64]

    my_half = pl.multiple_of(g * 16, 16)
    their_half = pl.multiple_of((1 - g) * 16, 16)
    swap = remote(first_part.at[pl.ds(their_half, 16), :], first_in, S_CORE + 5, other)
    swap.start()
    core_copies.append(swap)
    spot = dp * 4 + yi
    place = pl.multiple_of(spot * 16, 16)
    part = core_in[pl.ds(place, 16), :]
    for i, copy in enumerate(xy_copies):
        copy.wait_recv()
        part = part + xy_in[i]
    z_in[zi] = part
    z_copies = []
    for k in range(7):
        copy = remote(z_in.at[zi], z_in.at[zi], S_Z + k, tall[k])
        copy.start()
        z_copies.append(copy)
    swap.wait_recv()
    first_xy[spot] = first_in[...] + first_part[pl.ds(my_half, 16), :]
    fxy_copies = []
    for i in range(15):
        copy = remote(first_xy.at[spot], first_xy.at[spot], S_FXY + i, flat[i])
        copy.start()
        fxy_copies.append(copy)
    for copy in z_copies:
        copy.wait_recv()
    part = z_in[0]
    for k in range(1, 8):
        part = part + z_in[k]
    rows = pl.ds(pl.multiple_of(mine + place, 16), 16)
    final[rows, :] = part
    ag_copies = []
    for i in range(15):
        copy = remote(final.at[rows, :], final.at[rows, :], S_AG + i, flat[i])
        copy.start()
        ag_copies.append(copy)
    for copy in fxy_copies:
        copy.wait_recv()
    part = first_xy[0]
    for k in range(1, 16):
        part = part + first_xy[k]
    first_z[zi] = part
    fz_copies = []
    for k in range(7):
        copy = remote(first_z.at[zi], first_z.at[zi], S_FZ + k, tall[k])
        copy.start()
        fz_copies.append(copy)
    for copy in ag_copies:
        copy.wait_recv()
    half = pl.ds(mine, 256)
    joined = remote(final.at[half, :], final.at[half, :], S_CORE + 6, other)
    joined.start()
    core_copies.append(joined)
    for copy in fz_copies:
        copy.wait_recv()
    part = first_z[0]
    for k in range(1, 8):
        part = part + first_z[k]
    half = pl.ds(my_half, 16)
    first_final[half, :] = part
    copy = remote(first_final.at[half, :], first_final.at[half, :], S_CORE + 7, other)
    copy.start()
    core_copies.append(copy)
    joined.wait_recv()
    stores.append(pltpu.make_async_copy(final.at[0:432, :], second_out, local_sem.at[17]))
    stores[2].start()
    copy.wait_recv()
    stores.append(pltpu.make_async_copy(first_final, first_out, local_sem.at[18]))
    stores[3].start()
    for store in stores:
        store.wait()

    for copy in rim_copies + core_copies + xy_copies + z_copies + ag_copies + fxy_copies + fz_copies:
        copy.wait_send()


def arrange(feat, grad, second, first, feat_out, grad_out, first_out, second_out):
    feat_out[...] = feat[...]
    grad_out[...] = grad[...]
    for a in range(9):
        at = slice(32 * a, 32 * a + 32)
        second_out[a] = second[at, 0:64]
        second_out[9 + a] = second[at, 64:128]
    for a in range(36):
        row = 288 + (8 * a) % 144
        lanes = slice(0, 64) if a < 18 else slice(64, 128)
        second_out[18 + a // 4, 8 * (a % 4) : 8 * (a % 4) + 8, :] = second[row : row + 8, lanes]
    flipped = first[...].T
    for tap in range(27):
        first_out[tap] = flipped[4 * tap : 4 * tap + 4, :]


def on_device(volumes, first_kernel, second_kernel, cotangent):
    consts = matrices()
    here = pl.BlockSpec(memory_space=pltpu.VMEM)
    there = pl.BlockSpec(memory_space=pltpu.HBM)
    vmem = pltpu.VMEM
    scratch = [
        vmem((4, 16384), BF16), vmem((27, 4, 32), BF16), vmem((27, 32, 64), BF16), vmem((64, 256), BF16), vmem((8, 256), F32),
        vmem((64, 256), BF16), vmem((512, 128), F32),
    ] + [vmem(m.shape, BF16) for m in consts[:-1]] + [
        vmem((128, 512), F32), vmem((144, KRAW), BF16),
        vmem((2, 96, 128), BF16), vmem((2, 192, 128), BF16), vmem((4, 48, 128), BF16),
        vmem((2, 96, 128), BF16), vmem((2, 192, 128), BF16), vmem((4, 48, 128), BF16),
        vmem((16, 512), BF16), vmem((16, 768), BF16), vmem((8, 144, 256), F32),
        vmem((16, 256, 256), BF16), vmem((256, 2048), BF16), vmem((16, 256, 128), F32),
        vmem((256, 256), BF16), vmem((192, 288), BF16), vmem((96, 576), BF16), vmem((128, 32), F32),
        vmem((576, 256), BF16), vmem((288, 2304), BF16), vmem((288, 2304), BF16),
        vmem((192, 2304), F32), vmem((192, 2304), F32), vmem((64, 1024), F32), vmem((64, 1024), F32),
        vmem((2, 128, 512), BF16), vmem((1152, 256), BF16), vmem((192, 2304), BF16),
        vmem((640, 2304), BF16), vmem((96, 2304), F32), vmem((256, 2048), BF16),
        vmem((512, 128), F32), vmem((256, 128), F32), vmem((15, 16, 128), F32), vmem((8, 16, 128), F32), vmem((512, 128), F32),
        vmem((32, 128), F32), vmem((16, 128), F32), vmem((16, 16, 128), F32), vmem((8, 16, 128), F32), vmem((32, 128), F32),
        pltpu.SemaphoreType.DMA((19,)), pltpu.SemaphoreType.DMA((75,)), pltpu.SemaphoreType.DMA((75,)),
    ]
    parts = pl.pallas_call(
        body,
        out_shape=(
            jax.ShapeDtypeStruct((64, 256), BF16),
            jax.ShapeDtypeStruct((512, 128), F32),
            jax.ShapeDtypeStruct((432, 128), F32),
            jax.ShapeDtypeStruct((32, 128), F32),
        ),
        in_specs=[there] * 15,
        out_specs=(there,) * 4,
        scratch_shapes=scratch,
        compiler_params=pltpu.CompilerParams(
            collective_id=0, has_side_effects=True, vmem_limit_bytes=60 * 1024 * 1024
        ),
    )(
        volumes.reshape(4, 16384),
        first_kernel.transpose(2, 3, 4, 1, 0).reshape(27, 4, 32),
        second_kernel.transpose(2, 3, 4, 1, 0).reshape(27, 32, 64),
        cotangent.reshape(64, 256),
        *(jnp.asarray(m) for m in consts),
    )
    features, act_grad, first_grad, second_grad = pl.pallas_call(
        arrange,
        out_shape=(
            jax.ShapeDtypeStruct((64, 256), BF16),
            jax.ShapeDtypeStruct((512, 128), F32),
            jax.ShapeDtypeStruct((27, 4, 32), F32),
            jax.ShapeDtypeStruct((27, 32, 64), F32),
        ),
        in_specs=[here] * 4,
        out_specs=(here,) * 4,
    )(*parts)
    return (
        features.reshape(1, 64, 1, 1, 256),
        act_grad.reshape(1, 32, 1, 1, 2048),
        first_grad.reshape(3, 3, 3, 4, 32).transpose(4, 3, 0, 1, 2),
        second_grad.reshape(3, 3, 3, 32, 64).transpose(4, 3, 0, 1, 2),
    )


def solution(mesh):
    placed = (P("dp", None, "gx", "yz", None), P(), P(), P("dp", None, "gx", "yz", None))
    return jax.shard_map(
        on_device,
        mesh=mesh,
        in_specs=placed,
        out_specs=(P("dp", None, "gx", "yz", None), P("dp", None, "gx", "yz", None), P(), P()),
        check_vma=False,
    )
```

```python
import functools

import jax
import jax.numpy as jnp
import numpy as np
from jax import lax
from jax.experimental import pallas as pl
from jax.experimental.pallas import tpu as pltpu
from jax.sharding import PartitionSpec as P

F32 = jnp.float32
BF16 = jnp.bfloat16
PY, PZ = 4, 8
NY = 4
KRAW = 1280
MESH = pl.DeviceIdType.MESH


def plane_order(rim):
    lanes = {(y, z): y * 8 + z for y in range(16) for z in range(8)}
    for y in range(-rim, 16 + rim):
        for z in range(-rim, 8 + rim):
            if (y, z) not in lanes:
                lanes[(y, z)] = len(lanes)
    return lanes


def on_edge(y, z):
    return y in (0, 31) or z in (0, 15)


EDGE = {place: i for i, place in enumerate((y, z) for y in range(32) for z in range(16) if on_edge(y, z))}


def rim_lane(y, z):
    if 0 <= y < 32 and 0 <= z < 16:
        return 640 + EDGE[(y, z)]
    if 0 <= z < 16:
        if y in (-1, 32):
            return (0 if y < 0 else 16) + z
        return 256 + ((y + 5) * 16 if y < 0 else 64 + (y - 33) * 16) + z
    if 0 <= y < 32:
        if z in (-1, 16):
            return (32 if z < 0 else 64) + y
        return 384 + ((z + 5) * 32 if z < 0 else 128 + (z - 17) * 32) + y
    row = y + 5 if y < 0 else y - 32
    col = z + 5 if z < 0 else z - 16
    return 128 + ((y >= 32) * 2 + (z >= 16)) * 32 + row * 5 + col


@functools.cache
def matrices():
    wide, ring = plane_order(2), plane_order(1)
    inside = np.zeros((8, 512, 256), np.float32)
    nearby = np.zeros((8, 256, 256), np.float32)
    around = np.zeros((8, 768, 256), np.float32)
    for dy in range(4):
        for dz in range(4):
            step, shift = divmod(dy * 4 + dz, 2)
            for (qy, qz), lane in wide.items():
                y, z = 2 * qy - 1 + dy, 2 * qz - 1 + dz
                if lane >= 128:
                    around[step, rim_lane(y, z), shift * 128 + lane - 128] = 1
                elif 0 <= y < 32 and 0 <= z < 16:
                    inside[step, y * 16 + z, shift * 128 + lane] = 1
                else:
                    nearby[step, rim_lane(y, z), shift * 128 + lane] = 1
    outgoing = np.zeros((512, 768), np.float32)
    for r in range(4):
        for z in range(16):
            outgoing[(27 + r) * 16 + z, r * 16 + z] = 1
            outgoing[(1 + r) * 16 + z, 64 + r * 16 + z] = 1
    for z in range(16):
        outgoing[31 * 16 + z, 128 + z] = 1
        outgoing[z, 144 + z] = 1
    for y in range(32):
        outgoing[y * 16 + 15, 160 + y] = 1
        outgoing[y * 16, 192 + y] = 1
        for c in range(4):
            outgoing[y * 16 + 11 + c, 256 + c * 32 + y] = 1
            outgoing[y * 16 + 1 + c, 384 + c * 32 + y] = 1
    for k in range(4):
        for r in range(5):
            for c in range(5):
                y = r if k // 2 else 27 + r
                z = c if k % 2 else 11 + c
                outgoing[y * 16 + z, 512 + k * 32 + r * 5 + c] = 1
    for (y, z), i in EDGE.items():
        outgoing[y * 16 + z, 640 + i] = 1
    second = np.zeros((9, 256, 256), np.float32)
    back = np.zeros((5, 256, 256), np.float32)
    for dy in range(3):
        for dz in range(3):
            tap = dy * 3 + dz
            for (y, z), lane in ring.items():
                second[tap, wide[(y + dy - 1, z + dz - 1)], lane] = 1
            for y in range(16):
                for z in range(8):
                    source = ring[(y - dy + 1, z - dz + 1)]
                    back[tap // 2, source, (tap % 2) * 128 + y * 8 + z] = 1
    fold = np.zeros((128, 2048), np.float32)
    for phase in range(8):
        px, py, pz = phase // 4, phase // 2 % 2, phase % 2
        for tx in range(3):
            for ty in range(3):
                for tz in range(3):
                    for channel in range(4):
                        x, y, z = tx + px, ty + py, tz + pz
                        row = (y * 4 + z) * 16 + ((x - 1) % 4) * 4 + channel
                        fold[((tx * 3 + ty) * 3 + tz) * 4 + channel, phase * 256 + row] = 1
    pool = np.zeros((512, 128), np.float32)
    for x in range(4):
        for y in range(16):
            for z in range(8):
                pool[x * 128 + y * 8 + z, x * 32 + (y // 2) * 4 + z // 2] = 1
    cot_out = np.zeros((256, 256), np.float32)
    cot_in = np.zeros((384, 1024), np.float32)
    for x in range(8):
        for y in range(8):
            cot_out[x * 32 + y * 4, x * 8 + y] = 1
            cot_out[x * 32 + y * 4 + 3, 64 + x * 8 + y] = 1
        for z in range(4):
            cot_out[x * 32 + z, 128 + x * 4 + z] = 1
            cot_out[x * 32 + 28 + z, 160 + x * 4 + z] = 1
        for (y, z), lane in ring.items():
            if lane < 128:
                continue
            if 0 <= y < 16:
                source = x * 8 + y // 2 + (64 if z < 0 else 0)
            elif 0 <= z < 8:
                source = 128 + x * 4 + z // 2 + (32 if y < 0 else 0)
            else:
                source = 256 + x * 4 + (3 if z < 0 else 0) + (32 if y < 0 else 0)
            cot_in[source, x * 128 + lane - 128] = 1
    sides = np.zeros((8, 256), np.float32)
    for (y, z), lane in wide.items():
        sides[:4, lane] = (y < 0, y >= 16, z < 0, z >= 8)
    sixteen = (inside, nearby, around, outgoing, second, back, fold, pool, cot_out, cot_in)
    return tuple(m.astype(jnp.bfloat16) for m in sixteen) + (sides,)


def mm(a, b):
    return jnp.dot(a, b, preferred_element_type=F32)


def mm_nt(a, b):
    return lax.dot_general(a, b, (((1,), (1,)), ((), ())), preferred_element_type=F32)


def identity(n):
    rows = lax.broadcasted_iota(jnp.int32, (n, n), 0)
    return jnp.where(rows == lax.broadcasted_iota(jnp.int32, (n, n), 1), 1.0, 0.0).astype(BF16)


def leaky(t):
    return jnp.where(t > 0, t, 0.3 * t)


def slope(t):
    return jnp.where(t > 0, jnp.float32(1.0), jnp.float32(0.3))


def strip(block, start, width):
    parts = 128 // width
    rows = block.shape[0] // parts
    lane = lax.broadcasted_iota(jnp.int32, (1, 128), 1)
    packed = jnp.zeros((rows, 128), F32)
    for j in range(parts):
        piece = block[rows * j : rows * j + rows]
        shift = (width * j - start) % 128
        packed = jnp.where(lane // width == j, pltpu.roll(piece, shift, 1) if shift else piece, packed)
    return packed


def unstrip(packed, start, width, j):
    shift = (start - width * j) % 128
    return pltpu.roll(packed, shift, 1) if shift else packed


def split(t):
    high = t.astype(BF16)
    return high, (t - high.astype(F32)).astype(BF16)


FACES = ((1, 0), (-1, 0), (0, 1), (0, -1))
CORNERS = ((1, 1), (1, -1), (-1, 1), (-1, -1))
DIRS = FACES + CORNERS
XY = sorted(
    ((a, b) for a in range(4) for b in range(4) if (a, b) != (0, 0)),
    key=lambda p: -min(p[0], 4 - p[0]) - min(p[1], 4 - p[1]),
)
TALL = (4, 3, 5, 2, 6, 1, 7)
S_RIM, S_CORE, S_XY, S_Z, S_AG, S_FXY, S_FZ = 0, 8, 16, 31, 38, 53, 68


def body(
    vol_h, k1_h, w2_h, cot_h, inside_h, nearby_h, around_h, outgoing_h, second_h, back_h, fold_h, pool_h, cot_out_h, cot_in_h,
    sides_h, feat_out, grad_out, second_out, first_out,
    vol, k1, w2, cot, sides, feat, grads,
    inside, nearby, around, outgoing, second, back, fold, pool, cot_out, cot_in,
    rows32, lraw, y_send, z_send, c_send, y_recv, z_recv, c_recv, edge_a, edge_b, early,
    x4, x4i, pre1, weights1, forward2, backward2, k1s,
    p2, b2i, b2r, t2i, t2r, spread_i, spread_r, pooled, pg, gshift, bg, t3, g1,
    total, core_in, xy_in, z_in, final, first_part, first_in, first_xy, first_z, first_final,
    local_sem, send_sem, recv_sem,
):
    dp, g, s = lax.axis_index("dp"), lax.axis_index("gx"), lax.axis_index("yz")
    by, bz = s // PZ, s % PZ
    yi, zi = s % NY, s // NY
    other = (dp, 1 - g, s)
    near = [(dp, g, ((by + a) % PY) * PZ + (bz + b) % PZ) for a, b in DIRS]
    flat = [((dp + a) % 4, g, zi * NY + (yi + b) % NY) for a, b in XY]
    tall = [(dp, g, ((zi + k) % 8) * NY + yi) for k in TALL]

    loads = [
        pltpu.make_async_copy(a, b, local_sem.at[i])
        for i, (a, b) in enumerate(
            (
                (vol_h, vol), (outgoing_h, outgoing), (cot_h, cot), (cot_out_h, cot_out), (k1_h, k1), (w2_h, w2),
                (fold_h, fold), (pool_h, pool), (inside_h, inside), (cot_in_h, cot_in), (nearby_h, nearby),
                (around_h, around), (second_h, second), (back_h, back), (sides_h, sides),
            )
        )
    ]
    for load in loads:
        load.start()

    barrier = pltpu.get_barrier_semaphore()
    everyone = [other] + near + flat + tall
    for device in everyone:
        pl.semaphore_signal(barrier, inc=1, device_id=device, device_id_type=MESH)

    def remote(source, target, slot, device):
        return pltpu.make_async_remote_copy(
            src_ref=source, dst_ref=target, send_sem=send_sem.at[slot], recv_sem=recv_sem.at[slot],
            device_id=device, device_id_type=MESH,
        )

    def valid(a, b):
        ok = jnp.logical_and(
            jnp.logical_and(by + a >= 0, by + a < PY), jnp.logical_and(bz + b >= 0, bz + b < PZ)
        )
        return jnp.where(ok, jnp.float32(1.0), jnp.float32(0.0))

    lane = lax.broadcasted_iota(jnp.int32, (1, 128), 1)

    loads[0].wait()
    for x in range(32):
        rows32[4 * x : 4 * x + 4, :] = vol[:, x * 512 : (x + 1) * 512].astype(F32)
    lraw[0:128, 0:512] = rows32[...].astype(BF16)
    loads[1].wait()
    out = mm(lraw[0:128, 0:512], outgoing[...])
    loads[2].wait()
    loads[3].wait()
    strips = mm(cot[...], cot_out[...])
    for i, (a, b) in enumerate(DIRS):
        ok = valid(a, b)
        if i < 2:
            y_send[i, 0:64] = (strip(out[:, 0:128], 64 * i, 64) * ok).astype(BF16)
            y_send[i, 64:80] = (strip(out[:, 128:256], 16 * i, 16) * ok).astype(BF16)
            y_send[i, 80:96] = (strip(strips[:, 128:256], 32 - 32 * i, 32) * ok).astype(BF16)
        elif i < 4:
            j = i - 2
            z_send[j, 0:128] = (out[:, 256 + 128 * j : 384 + 128 * j] * ok).astype(BF16)
            z_send[j, 128:160] = (strip(out[:, 128:256], 32 + 32 * j, 32) * ok).astype(BF16)
            z_send[j, 160:192] = (strip(strips[:, 0:128], 64 - 64 * j, 64) * ok).astype(BF16)
        else:
            j = i - 4
            c_send[j, 0:32] = (strip(out[:, 512:640], 32 * j, 32) * ok).astype(BF16)
            c_send[j, 32:48] = (strip(strips[:, 128:256], 32 if a > 0 else 0, 32) * ok).astype(BF16)

    pl.semaphore_wait(barrier, len(everyone))
    rim_copies = []
    for i in (4, 5, 6, 7, 2, 3, 0, 1):
        pair = ((y_send, y_recv), (z_send, z_recv), (c_send, c_recv), (c_send, c_recv))[i // 2]
        slot = i - 4 if i >= 4 else i % 2
        copy = remote(pair[0].at[slot], pair[1].at[slot], S_RIM + i, near[i])
        copy.start()
        rim_copies.append(copy)
    mine = pl.multiple_of(jnp.where(g == 0, 112, 0), 16)
    early_edge = remote(lraw.at[pl.ds(mine, 16), 0:512], edge_a, S_CORE, other)
    early_edge.start()
    core_copies = [early_edge]
    lraw[0:128, 1152:1280] = out[:, 640:768].astype(BF16)

    loads[4].wait()
    loads[5].wait()
    k1s[...] = jnp.zeros_like(k1s)
    for tap in range(27):
        k1s[4 * tap : 4 * tap + 4, :] = k1[tap].astype(F32)
    loads[6].wait()
    k1t = mm_nt(identity(32), k1s[...].astype(BF16)).astype(BF16)
    for phase in range(8):
        weights1[32 * phase : 32 * phase + 32, :] = mm(k1t, fold[:, 256 * phase : 256 * phase + 256]).astype(BF16)
    eye = identity(64)
    for x in range(3):
        block = w2[9 * x : 9 * x + 9].reshape(288, 64)
        forward2[64 * x : 64 * x + 64, :] = mm_nt(eye, block).astype(BF16)
        for a in (0, 2, 4, 6):
            both = jnp.concatenate([w2[9 * x + a].astype(F32), w2[9 * x + a + 1].astype(F32)], axis=1)
            backward2[32 * x : 32 * x + 32, 64 * a : 64 * a + 128] = both.astype(BF16)
        backward2[32 * x : 32 * x + 32, 512:576] = w2[9 * x + 8]
    loads[7].wait()
    for half in range(2):
        spread_i[:, 512 * half : 512 * half + 512] = mm_nt(cot[:, 128 * half : 128 * half + 128], pool[...])
    far = pl.multiple_of(g * (17 * 32), 32)
    p2[pl.ds(far, 32), :] = jnp.zeros((32, 256), BF16)
    far = pl.multiple_of(g * (17 * 64), 64)
    pg[pl.ds(far, 64), :] = jnp.zeros((64, 256), BF16)
    gshift[...] = jnp.zeros_like(gshift)
    early_edge.wait_recv()
    first_core = jnp.where(g == 0, jnp.float32(1.0), jnp.float32(0.0))
    half_row = lax.broadcasted_iota(jnp.int32, (8, 1), 0)

    def beyond(edge):
        edge = edge.astype(F32)
        edge = jnp.where(half_row < 4, edge[0:8] * first_core, edge[8:16] * (1.0 - first_core))
        return jnp.concatenate([edge, jnp.zeros_like(edge)], axis=0).astype(BF16)

    lraw[128:144, 0:512] = beyond(edge_a[...])
    for load in loads[8:]:
        load.wait()

    def early_step(step, carry):
        early[step] = mm(lraw[:, 0:512], inside[step])
        return carry

    lax.fori_loop(0, 8, early_step, 0, unroll=True)

    for copy in rim_copies:
        copy.wait_recv()
    for j in range(2):
        low = unstrip(y_recv[0, 0:64].astype(F32), 0, 64, j)
        high = unstrip(y_recv[1, 0:64].astype(F32), 64, 64, j)
        lraw[64 * j : 64 * j + 64, 768:896] = jnp.where(lane < 64, low, high).astype(BF16)
    lraw[0:128, 896:1024] = z_recv[0, 0:128]
    lraw[0:128, 1024:1152] = z_recv[1, 0:128]
    y_low, y_high = y_recv[0, 64:80].astype(F32), y_recv[1, 64:80].astype(F32)
    def fill_inner(j):
        at = slice(128 + 16 * (j % 2), 144 + 16 * (j % 2))
        z_low, z_high = z_recv[0, at].astype(F32), z_recv[1, at].astype(F32)
        block = jnp.where(lane < 16, unstrip(y_low, 0, 16, j), unstrip(y_high, 16, 16, j))
        block = jnp.where(lane < 32, block, unstrip(z_low, 32, 32, j // 2))
        block = jnp.where(lane < 64, block, unstrip(z_high, 64, 32, j // 2))
        lraw[16 * j : 16 * j + 16, 512:640] = block.astype(BF16)
    def fill_corner(j):
        block = jnp.zeros((32, 128), F32)
        for k in range(4):
            block = jnp.where(lane // 32 == k, unstrip(c_recv[k, 0:32].astype(F32), 32 * k, 32, j), block)
        lraw[32 * j : 32 * j + 32, 640:768] = block.astype(BF16)

    for j in (0, 7):
        fill_inner(j)
    for j in (0, 3):
        fill_corner(j)
    copy = remote(lraw.at[pl.ds(mine, 16), 512:1280], edge_b, S_CORE + 1, other)
    copy.start()
    core_copies.append(copy)
    for j in range(1, 7):
        fill_inner(j)
    for j in (1, 2):
        fill_corner(j)
    copy.wait_recv()
    lraw[128:144, 512:1280] = beyond(edge_b[...])

    def gather_step(step, carry):
        mid = mm(lraw[:, 512:768], nearby[step]) + early[step]
        rim = mm(lraw[:, 512:1280], around[step])
        low = half_row < 4
        for shift in range(2):
            at = pl.multiple_of(step * 32 + shift * 16, 16)
            lanes = slice(128 * shift, 128 * shift + 128)
            for x in range(16):
                for got, side in ((mid[:, lanes], 0), (rim[:, lanes], 1)):
                    after = got[8 * x + 8 : 8 * x + 16]
                    before = got[8 * x - 8 : 8 * x] if x else got[128:136]
                    block = jnp.concatenate([got[8 * x : 8 * x + 8], jnp.where(low, after, before)], axis=0)
                    block = block.astype(BF16)
                    x4[x, pl.ds(at, 16), 128 * side : 128 * side + 128] = block
                    if side == 0:
                        x4i[pl.ds(at, 16), 128 * x : 128 * x + 128] = block
        return carry

    lax.fori_loop(0, 8, gather_step, 0, unroll=True)

    def flag(test):
        return jnp.where(test, jnp.float32(1.0), jnp.float32(0.0))

    outside = jnp.maximum(
        jnp.maximum(sides[0:1, :] * flag(by == 0), sides[1:2, :] * flag(by == PY - 1)),
        jnp.maximum(sides[2:3, :] * flag(bz == 0), sides[3:4, :] * flag(bz == PZ - 1)),
    )
    scale = (1.0 - outside) * 0.125

    def first_layer(x):
        pre = mm(weights1[...], x4[x])
        pre1[x] = pre[:, 0:128]
        act = leaky(pre[0:32])
        for phase in range(1, 8):
            act = act + leaky(pre[32 * phase : 32 * phase + 32])
        p2[32 * x + 32 : 32 * x + 64, :] = (act * scale).astype(BF16)

    first_layer(0)
    first_layer(15)
    near_src = pl.multiple_of(jnp.where(g == 0, 16 * 32, 32), 32)
    near_dst = pl.multiple_of(jnp.where(g == 0, 0, 17 * 32), 32)
    copy = remote(p2.at[pl.ds(near_src, 32), :], p2.at[pl.ds(near_dst, 32), :], S_CORE + 2, other)
    copy.start()
    core_copies.append(copy)
    for x in range(1, 15):
        first_layer(x)

    zs, ys, cs = [], [], []
    for j in range(2):
        low, high = z_recv[0, 160:192].astype(F32), z_recv[1, 160:192].astype(F32)
        zs.append(jnp.where(lane >= 64, unstrip(low, 64, 64, j), unstrip(high, 0, 64, j)))
    late = lane % 4 == 3
    for j in range(4):
        low, high = y_recv[0, 80:96].astype(F32), y_recv[1, 80:96].astype(F32)
        ys.append(jnp.where(lane >= 32, unstrip(low, 32, 32, j), unstrip(high, 0, 32, j)))
        ends = [unstrip(c_recv[k, 32:48].astype(F32), 32 if k < 2 else 0, 32, j) for k in range(4)]
        cs.append(
            jnp.where(lane >= 32, jnp.where(late, ends[0], ends[1]), jnp.where(late, ends[2], ends[3]))
        )
    zs, ys, cs = (jnp.concatenate(parts, axis=0) for parts in (zs, ys, cs))
    rim = jnp.concatenate([zs, ys, cs], axis=1).astype(BF16)
    spread_r[...] = mm(rim, cot_in[...])

    copy.wait_recv()

    def shift_step(tap, carry):
        got = mm(p2[...], second[tap])
        at = pl.multiple_of(tap * 32, 32)
        for x in range(18):
            block = got[32 * x : 32 * x + 32].astype(BF16)
            b2i[pl.ds(at, 32), 128 * x : 128 * x + 128] = block[:, 0:128]
            b2r[pl.ds(at, 32), 128 * x : 128 * x + 128] = block[:, 128:256]
        return carry

    lax.fori_loop(0, 9, shift_step, 0, unroll=True)

    def second_layer(chunk, carry):
        at = pl.ds(pl.multiple_of(chunk * 256, 256), 256)
        t2i[:, at] = mm(forward2[...], b2i[:, at])
        t2r[:, at] = mm(forward2[...], b2r[:, at])
        return carry

    lax.fori_loop(0, 9, second_layer, 0, unroll=True)

    for half in (0, 7, 1, 2, 3, 4, 5, 6):
        lifted = spread_i[:, 128 * half : 128 * half + 128] * 0.125
        lifted_rim = spread_r[:, 128 * half : 128 * half + 128] * 0.125
        pair = jnp.zeros((64, 128), F32)
        for x in (2 * half, 2 * half + 1):
            at = [slice(128 * (x + d), 128 * (x + d) + 128) for d in range(3)]
            pre = t2i[0:64, at[0]] + t2i[64:128, at[1]] + t2i[128:192, at[2]]
            pair = pair + leaky(pre)
            grad = (lifted * slope(pre)).astype(BF16)
            pg[64 * x + 64 : 64 * x + 128, 0:128] = grad
            for d in range(3):
                gshift[64 * d : 64 * d + 64, at[d]] = grad
            pre = t2r[0:64, at[0]] + t2r[64:128, at[1]] + t2r[128:192, at[2]]
            pg[64 * x + 64 : 64 * x + 128, 128:256] = (lifted_rim * slope(pre)).astype(BF16)
        high, low = split(pair)
        at = slice(128 * (half % 4), 128 * (half % 4) + 128)
        pooled[half // 4, 0:64, at] = high
        pooled[half // 4, 64:128, at] = low
        if half == 7:
            near_src = pl.multiple_of(jnp.where(g == 0, 16 * 64, 64), 64)
            near_dst = pl.multiple_of(jnp.where(g == 0, 0, 17 * 64), 64)
            copy = remote(pg.at[pl.ds(near_src, 64), :], pg.at[pl.ds(near_dst, 64), :], S_CORE + 3, other)
            copy.start()
            core_copies.append(copy)
    for half in range(2):
        sums = mm(pooled[half], pool[...])
        feat[:, 128 * half : 128 * half + 128] = ((sums[0:64] + sums[64:128]) * 0.125).astype(BF16)
    stores = [pltpu.make_async_copy(feat, feat_out, local_sem.at[15])]
    stores[0].start()

    grad2 = mm_nt(b2i[...], gshift[...])
    total[0:288, :] = grad2[:, 0:128]
    total[288:432, 0:64] = grad2[0:144, 128:192]
    total[288:432, 64:128] = grad2[144:288, 128:192]
    total[432:512, :] = jnp.zeros((80, 128), F32)
    mine = pl.multiple_of(g * 256, 256)
    theirs = pl.multiple_of((1 - g) * 256, 256)
    halves = remote(total.at[pl.ds(theirs, 256), :], core_in, S_CORE + 4, other)
    halves.start()
    core_copies.append(halves)
    copy.wait_recv()
    halves.wait_recv()
    core_in[...] = core_in[...] + total[pl.ds(mine, 256), :]
    xy_copies = []
    for i, (a, b) in enumerate(XY):
        piece = ((dp + a) % 4) * 4 + (yi + b) % 4
        source = core_in.at[pl.ds(pl.multiple_of(piece * 16, 16), 16), :]
        copy = remote(source, xy_in.at[i], S_XY + i, flat[i])
        copy.start()
        xy_copies.append(copy)

    def back_step(step, carry):
        got = mm(pg[...], back[step])
        at = pl.multiple_of(step * 128, 128)
        for x in range(18):
            block = got[64 * x : 64 * x + 64].astype(BF16)
            bg[pl.ds(at, 64), 128 * x : 128 * x + 128] = block[:, 0:128]
            bg[pl.ds(at + 64, 64), 128 * x : 128 * x + 128] = block[:, 128:256]
        return carry

    lax.fori_loop(0, 5, back_step, 0, unroll=True)

    def back_layer(chunk, carry):
        at = pl.ds(pl.multiple_of(chunk * 256, 256), 256)
        t3[:, at] = mm(backward2[...], bg[0:576, at])
        return carry

    lax.fori_loop(0, 9, back_layer, 0, unroll=True)

    for x in range(16):
        grad = (
            t3[0:32, 128 * (x + 2) : 128 * (x + 3)]
            + t3[32:64, 128 * (x + 1) : 128 * (x + 2)]
            + t3[64:96, 128 * x : 128 * (x + 1)]
        )
        grads[pl.ds(x, 32, stride=16), :] = grad
        eighth = grad * 0.125
        for phase in range(8):
            at = slice(32 * phase, 32 * phase + 32)
            g1[at, 128 * x : 128 * x + 128] = (eighth * slope(pre1[x, at, :])).astype(BF16)
    stores.append(pltpu.make_async_copy(grads, grad_out, local_sem.at[16]))
    stores[1].start()
    wide = mm_nt(g1[...], x4i[...])
    partial = jnp.zeros((64, 128), F32)
    for phase in range(8):
        high, low = split(wide[32 * phase : 32 * phase + 32])
        partial = partial + mm_nt(jnp.concatenate([high, low], axis=0), fold[:, 256 * phase : 256 * phase + 256])
    first_part[...] = partial[0:32] + partial[32:64]

    my_half = pl.multiple_of(g * 16, 16)
    their_half = pl.multiple_of((1 - g) * 16, 16)
    swap = remote(first_part.at[pl.ds(their_half, 16), :], first_in, S_CORE + 5, other)
    swap.start()
    core_copies.append(swap)
    spot = dp * 4 + yi
    place = pl.multiple_of(spot * 16, 16)
    swap.wait_recv()
    first_xy[spot] = first_in[...] + first_part[pl.ds(my_half, 16), :]
    fxy_copies = []
    for i in range(15):
        copy = remote(first_xy.at[spot], first_xy.at[spot], S_FXY + i, flat[i])
        copy.start()
        fxy_copies.append(copy)
    for sent in rim_copies + core_copies[:5]:
        sent.wait_send()
    part = core_in[pl.ds(place, 16), :]
    for i, copy in enumerate(xy_copies):
        copy.wait_recv()
        part = part + xy_in[i]
    z_in[zi] = part
    z_copies = []
    for k in range(7):
        copy = remote(z_in.at[zi], z_in.at[zi], S_Z + k, tall[k])
        copy.start()
        z_copies.append(copy)
    for copy in fxy_copies:
        copy.wait_recv()
    part = first_xy[0]
    for k in range(1, 16):
        part = part + first_xy[k]
    first_z[zi] = part
    fz_copies = []
    for k in range(7):
        copy = remote(first_z.at[zi], first_z.at[zi], S_FZ + k, tall[k])
        copy.start()
        fz_copies.append(copy)
    for copy in z_copies:
        copy.wait_recv()
    part = z_in[0]
    for k in range(1, 8):
        part = part + z_in[k]
    rows = pl.ds(pl.multiple_of(mine + place, 16), 16)
    final[rows, :] = part
    ag_copies = []
    for i in range(15):
        copy = remote(final.at[rows, :], final.at[rows, :], S_AG + i, flat[i])
        copy.start()
        ag_copies.append(copy)
    for sent in xy_copies + fxy_copies:
        sent.wait_send()
    for copy in ag_copies:
        copy.wait_recv()
    half = pl.ds(mine, 256)
    joined = remote(final.at[half, :], final.at[half, :], S_CORE + 6, other)
    joined.start()
    core_copies.append(joined)
    for copy in fz_copies:
        copy.wait_recv()
    part = first_z[0]
    for k in range(1, 8):
        part = part + first_z[k]
    half = pl.ds(my_half, 16)
    first_final[half, :] = part
    copy = remote(first_final.at[half, :], first_final.at[half, :], S_CORE + 7, other)
    copy.start()
    core_copies.append(copy)
    for sent in z_copies + ag_copies + fz_copies:
        sent.wait_send()
    joined.wait_recv()
    stores.append(pltpu.make_async_copy(final.at[0:432, :], second_out, local_sem.at[17]))
    stores[2].start()
    copy.wait_recv()
    stores.append(pltpu.make_async_copy(first_final, first_out, local_sem.at[18]))
    stores[3].start()
    for store in stores:
        store.wait()

    for sent in core_copies[5:]:
        sent.wait_send()


def arrange(feat, grad, second, first, feat_out, grad_out, first_out, second_out):
    feat_out[...] = feat[...]
    grad_out[...] = grad[...]
    for a in range(9):
        at = slice(32 * a, 32 * a + 32)
        second_out[a] = second[at, 0:64]
        second_out[9 + a] = second[at, 64:128]
    for a in range(36):
        row = 288 + (8 * a) % 144
        lanes = slice(0, 64) if a < 18 else slice(64, 128)
        second_out[18 + a // 4, 8 * (a % 4) : 8 * (a % 4) + 8, :] = second[row : row + 8, lanes]
    flipped = first[...].T
    for tap in range(27):
        first_out[tap] = flipped[4 * tap : 4 * tap + 4, :]


def on_device(volumes, first_kernel, second_kernel, cotangent):
    consts = matrices()
    here = pl.BlockSpec(memory_space=pltpu.VMEM)
    there = pl.BlockSpec(memory_space=pltpu.HBM)
    vmem = pltpu.VMEM
    scratch = [
        vmem((4, 16384), BF16), vmem((27, 4, 32), BF16), vmem((27, 32, 64), BF16), vmem((64, 256), BF16), vmem((8, 256), F32),
        vmem((64, 256), BF16), vmem((512, 128), F32),
    ] + [vmem(m.shape, BF16) for m in consts[:-1]] + [
        vmem((128, 512), F32), vmem((144, KRAW), BF16),
        vmem((2, 96, 128), BF16), vmem((2, 192, 128), BF16), vmem((4, 48, 128), BF16),
        vmem((2, 96, 128), BF16), vmem((2, 192, 128), BF16), vmem((4, 48, 128), BF16),
        vmem((16, 512), BF16), vmem((16, 768), BF16), vmem((8, 144, 256), F32),
        vmem((16, 256, 256), BF16), vmem((256, 2048), BF16), vmem((16, 256, 128), F32),
        vmem((256, 256), BF16), vmem((192, 288), BF16), vmem((96, 576), BF16), vmem((128, 32), F32),
        vmem((576, 256), BF16), vmem((288, 2304), BF16), vmem((288, 2304), BF16),
        vmem((192, 2304), F32), vmem((192, 2304), F32), vmem((64, 1024), F32), vmem((64, 1024), F32),
        vmem((2, 128, 512), BF16), vmem((1152, 256), BF16), vmem((192, 2304), BF16),
        vmem((640, 2304), BF16), vmem((96, 2304), F32), vmem((256, 2048), BF16),
        vmem((512, 128), F32), vmem((256, 128), F32), vmem((15, 16, 128), F32), vmem((8, 16, 128), F32), vmem((512, 128), F32),
        vmem((32, 128), F32), vmem((16, 128), F32), vmem((16, 16, 128), F32), vmem((8, 16, 128), F32), vmem((32, 128), F32),
        pltpu.SemaphoreType.DMA((19,)), pltpu.SemaphoreType.DMA((75,)), pltpu.SemaphoreType.DMA((75,)),
    ]
    parts = pl.pallas_call(
        body,
        out_shape=(
            jax.ShapeDtypeStruct((64, 256), BF16),
            jax.ShapeDtypeStruct((512, 128), F32),
            jax.ShapeDtypeStruct((432, 128), F32),
            jax.ShapeDtypeStruct((32, 128), F32),
        ),
        in_specs=[there] * 15,
        out_specs=(there,) * 4,
        scratch_shapes=scratch,
        compiler_params=pltpu.CompilerParams(
            collective_id=0, has_side_effects=True, vmem_limit_bytes=60 * 1024 * 1024
        ),
    )(
        volumes.reshape(4, 16384),
        first_kernel.transpose(2, 3, 4, 1, 0).reshape(27, 4, 32),
        second_kernel.transpose(2, 3, 4, 1, 0).reshape(27, 32, 64),
        cotangent.reshape(64, 256),
        *(jnp.asarray(m) for m in consts),
    )
    features, act_grad, first_grad, second_grad = pl.pallas_call(
        arrange,
        out_shape=(
            jax.ShapeDtypeStruct((64, 256), BF16),
            jax.ShapeDtypeStruct((512, 128), F32),
            jax.ShapeDtypeStruct((27, 4, 32), F32),
            jax.ShapeDtypeStruct((27, 32, 64), F32),
        ),
        in_specs=[here] * 4,
        out_specs=(here,) * 4,
    )(*parts)
    return (
        features.reshape(1, 64, 1, 1, 256),
        act_grad.reshape(1, 32, 1, 1, 2048),
        first_grad.reshape(3, 3, 3, 4, 32).transpose(4, 3, 0, 1, 2),
        second_grad.reshape(3, 3, 3, 32, 64).transpose(4, 3, 0, 1, 2),
    )


def solution(mesh):
    placed = (P("dp", None, "gx", "yz", None), P(), P(), P("dp", None, "gx", "yz", None))
    return jax.shard_map(
        on_device,
        mesh=mesh,
        in_specs=placed,
        out_specs=(P("dp", None, "gx", "yz", None), P("dp", None, "gx", "yz", None), P(), P()),
        check_vma=False,
    )
```

```python
import functools

import jax
import jax.numpy as jnp
import numpy as np
from jax import lax
from jax.experimental import pallas as pl
from jax.experimental.pallas import tpu as pltpu
from jax.sharding import PartitionSpec as P

F32 = jnp.float32
BF16 = jnp.bfloat16
PY, PZ = 4, 8
NY = 4
KRAW = 1280
MESH = pl.DeviceIdType.MESH


def plane_order(rim):
    lanes = {(y, z): y * 8 + z for y in range(16) for z in range(8)}
    for y in range(-rim, 16 + rim):
        for z in range(-rim, 8 + rim):
            if (y, z) not in lanes:
                lanes[(y, z)] = len(lanes)
    return lanes


def on_edge(y, z):
    return y in (0, 31) or z in (0, 15)


EDGE = {place: i for i, place in enumerate((y, z) for y in range(32) for z in range(16) if on_edge(y, z))}


def rim_lane(y, z):
    if 0 <= y < 32 and 0 <= z < 16:
        return 640 + EDGE[(y, z)]
    if 0 <= z < 16:
        if y in (-1, 32):
            return (0 if y < 0 else 16) + z
        return 256 + ((y + 5) * 16 if y < 0 else 64 + (y - 33) * 16) + z
    if 0 <= y < 32:
        if z in (-1, 16):
            return (32 if z < 0 else 64) + y
        return 384 + ((z + 5) * 32 if z < 0 else 128 + (z - 17) * 32) + y
    row = y + 5 if y < 0 else y - 32
    col = z + 5 if z < 0 else z - 16
    return 128 + ((y >= 32) * 2 + (z >= 16)) * 32 + row * 5 + col


@functools.cache
def matrices():
    wide, ring = plane_order(2), plane_order(1)
    inside = np.zeros((8, 512, 256), np.float32)
    nearby = np.zeros((8, 256, 256), np.float32)
    around = np.zeros((8, 768, 256), np.float32)
    for dy in range(4):
        for dz in range(4):
            step, shift = divmod(dy * 4 + dz, 2)
            for (qy, qz), lane in wide.items():
                y, z = 2 * qy - 1 + dy, 2 * qz - 1 + dz
                if lane >= 128:
                    around[step, rim_lane(y, z), shift * 128 + lane - 128] = 1
                elif 0 <= y < 32 and 0 <= z < 16:
                    inside[step, y * 16 + z, shift * 128 + lane] = 1
                else:
                    nearby[step, rim_lane(y, z), shift * 128 + lane] = 1
    outgoing = np.zeros((512, 768), np.float32)
    for r in range(4):
        for z in range(16):
            outgoing[(27 + r) * 16 + z, r * 16 + z] = 1
            outgoing[(1 + r) * 16 + z, 64 + r * 16 + z] = 1
    for z in range(16):
        outgoing[31 * 16 + z, 128 + z] = 1
        outgoing[z, 144 + z] = 1
    for y in range(32):
        outgoing[y * 16 + 15, 160 + y] = 1
        outgoing[y * 16, 192 + y] = 1
        for c in range(4):
            outgoing[y * 16 + 11 + c, 256 + c * 32 + y] = 1
            outgoing[y * 16 + 1 + c, 384 + c * 32 + y] = 1
    for k in range(4):
        for r in range(5):
            for c in range(5):
                y = r if k // 2 else 27 + r
                z = c if k % 2 else 11 + c
                outgoing[y * 16 + z, 512 + k * 32 + r * 5 + c] = 1
    for (y, z), i in EDGE.items():
        outgoing[y * 16 + z, 640 + i] = 1
    second = np.zeros((9, 256, 256), np.float32)
    back = np.zeros((5, 256, 256), np.float32)
    for dy in range(3):
        for dz in range(3):
            tap = dy * 3 + dz
            for (y, z), lane in ring.items():
                second[tap, wide[(y + dy - 1, z + dz - 1)], lane] = 1
                if lane >= 128:
                    second[tap, wide[(y + dy - 1, z + dz - 1)], lane + 64] = 1
            for y in range(16):
                for z in range(8):
                    source = ring[(y - dy + 1, z - dz + 1)]
                    for place in (source,) if source < 128 else (source, source + 64):
                        back[tap // 2, place, (tap % 2) * 128 + y * 8 + z] = 1
    fold = np.zeros((128, 2048), np.float32)
    for phase in range(8):
        px, py, pz = phase // 4, phase // 2 % 2, phase % 2
        for tx in range(3):
            for ty in range(3):
                for tz in range(3):
                    for channel in range(4):
                        x, y, z = tx + px, ty + py, tz + pz
                        row = (y * 4 + z) * 16 + ((x - 1) % 4) * 4 + channel
                        fold[((tx * 3 + ty) * 3 + tz) * 4 + channel, phase * 256 + row] = 1
    pool = np.zeros((512, 128), np.float32)
    for x in range(4):
        for y in range(16):
            for z in range(8):
                pool[x * 128 + y * 8 + z, x * 32 + (y // 2) * 4 + z // 2] = 1
    cot_out = np.zeros((256, 256), np.float32)
    cot_in = np.zeros((384, 1024), np.float32)
    for x in range(8):
        for y in range(8):
            cot_out[x * 32 + y * 4, x * 8 + y] = 1
            cot_out[x * 32 + y * 4 + 3, 64 + x * 8 + y] = 1
        for z in range(4):
            cot_out[x * 32 + z, 128 + x * 4 + z] = 1
            cot_out[x * 32 + 28 + z, 160 + x * 4 + z] = 1
        for (y, z), lane in ring.items():
            if lane < 128:
                continue
            if 0 <= y < 16:
                source = x * 8 + y // 2 + (64 if z < 0 else 0)
            elif 0 <= z < 8:
                source = 128 + x * 4 + z // 2 + (32 if y < 0 else 0)
            else:
                source = 256 + x * 4 + (3 if z < 0 else 0) + (32 if y < 0 else 0)
            cot_in[source, x * 128 + lane - 128] = 1
            cot_in[source, x * 128 + lane - 64] = 1
    sides = np.zeros((8, 256), np.float32)
    for (y, z), lane in wide.items():
        sides[:4, lane] = (y < 0, y >= 16, z < 0, z >= 8)
    sixteen = (inside, nearby, around, outgoing, second, back, fold, pool, cot_out, cot_in)
    return tuple(m.astype(jnp.bfloat16) for m in sixteen) + (sides,)


def mm(a, b):
    return jnp.dot(a, b, preferred_element_type=F32)


def mm_nt(a, b):
    return lax.dot_general(a, b, (((1,), (1,)), ((), ())), preferred_element_type=F32)


def identity(n):
    rows = lax.broadcasted_iota(jnp.int32, (n, n), 0)
    return jnp.where(rows == lax.broadcasted_iota(jnp.int32, (n, n), 1), 1.0, 0.0).astype(BF16)


def leaky(t):
    return jnp.where(t > 0, t, 0.3 * t)


def slope(t):
    return jnp.where(t > 0, jnp.float32(1.0), jnp.float32(0.3))


def strip(block, start, width):
    parts = 128 // width
    rows = block.shape[0] // parts
    lane = lax.broadcasted_iota(jnp.int32, (1, 128), 1)
    packed = jnp.zeros((rows, 128), F32)
    for j in range(parts):
        piece = block[rows * j : rows * j + rows]
        shift = (width * j - start) % 128
        packed = jnp.where(lane // width == j, pltpu.roll(piece, shift, 1) if shift else piece, packed)
    return packed


def unstrip(packed, start, width, j):
    shift = (start - width * j) % 128
    return pltpu.roll(packed, shift, 1) if shift else packed


def split(t):
    high = t.astype(BF16)
    return high, (t - high.astype(F32)).astype(BF16)


FACES = ((1, 0), (-1, 0), (0, 1), (0, -1))
CORNERS = ((1, 1), (1, -1), (-1, 1), (-1, -1))
DIRS = FACES + CORNERS
XY = sorted(
    ((a, b) for a in range(4) for b in range(4) if (a, b) != (0, 0)),
    key=lambda p: -min(p[0], 4 - p[0]) - min(p[1], 4 - p[1]),
)
TALL = (4, 3, 5, 2, 6, 1, 7)
S_RIM, S_CORE, S_XY, S_Z, S_AG, S_FXY, S_FZ = 0, 8, 16, 31, 38, 53, 68


def body(
    vol_h, k1_h, w2_h, cot_h, inside_h, nearby_h, around_h, outgoing_h, second_h, back_h, fold_h, pool_h, cot_out_h, cot_in_h,
    sides_h, feat_out, grad_out, second_out, first_out,
    vol, k1, w2, cot, sides, feat, grads,
    inside, nearby, around, outgoing, second, back, fold, pool, cot_out, cot_in,
    rows32, lraw, y_send, z_send, c_send, y_recv, z_recv, c_recv, edge_a, edge_b, early,
    x4, x4i, pre1, weights1, forward2, backward2, k1s,
    p2, b2i, b2r, t2i, t2r, spread_i, spread_r, pooled, pg, gshift, bg, t3, g1,
    total, core_in, xy_out, xy_in, z_in, final, first_part, first_in, first_xy, first_z, first_final,
    local_sem, send_sem, recv_sem,
):
    dp, g, s = lax.axis_index("dp"), lax.axis_index("gx"), lax.axis_index("yz")
    by, bz = s // PZ, s % PZ
    yi, zi = s % NY, s // NY
    other = (dp, 1 - g, s)
    near = [(dp, g, ((by + a) % PY) * PZ + (bz + b) % PZ) for a, b in DIRS]
    flat = [((dp + a) % 4, g, zi * NY + (yi + b) % NY) for a, b in XY]
    tall = [(dp, g, ((zi + k) % 8) * NY + yi) for k in TALL]

    loads = [
        pltpu.make_async_copy(a, b, local_sem.at[i])
        for i, (a, b) in enumerate(
            (
                (vol_h, vol), (outgoing_h, outgoing), (cot_h, cot), (cot_out_h, cot_out), (k1_h, k1), (w2_h, w2),
                (fold_h, fold), (pool_h, pool), (inside_h, inside), (cot_in_h, cot_in), (nearby_h, nearby),
                (around_h, around), (second_h, second), (back_h, back), (sides_h, sides),
            )
        )
    ]
    for load in loads:
        load.start()

    barrier = pltpu.get_barrier_semaphore()
    everyone = [other] + near + flat + tall
    for device in everyone:
        pl.semaphore_signal(barrier, inc=1, device_id=device, device_id_type=MESH)

    def remote(source, target, slot, device):
        return pltpu.make_async_remote_copy(
            src_ref=source, dst_ref=target, send_sem=send_sem.at[slot], recv_sem=recv_sem.at[slot],
            device_id=device, device_id_type=MESH,
        )

    def valid(a, b):
        ok = jnp.logical_and(
            jnp.logical_and(by + a >= 0, by + a < PY), jnp.logical_and(bz + b >= 0, bz + b < PZ)
        )
        return jnp.where(ok, jnp.float32(1.0), jnp.float32(0.0))

    lane = lax.broadcasted_iota(jnp.int32, (1, 128), 1)

    loads[0].wait()
    for x in range(32):
        rows32[4 * x : 4 * x + 4, :] = vol[:, x * 512 : (x + 1) * 512].astype(F32)
    lraw[0:128, 0:512] = rows32[...].astype(BF16)
    loads[1].wait()
    out = mm(lraw[0:128, 0:512], outgoing[...])
    loads[2].wait()
    loads[3].wait()
    strips = mm(cot[...], cot_out[...])
    for i, (a, b) in enumerate(DIRS):
        ok = valid(a, b)
        if i < 2:
            y_send[i, 0:64] = (strip(out[:, 0:128], 64 * i, 64) * ok).astype(BF16)
            y_send[i, 64:80] = (strip(out[:, 128:256], 16 * i, 16) * ok).astype(BF16)
            y_send[i, 80:96] = (strip(strips[:, 128:256], 32 - 32 * i, 32) * ok).astype(BF16)
        elif i < 4:
            j = i - 2
            z_send[j, 0:128] = (out[:, 256 + 128 * j : 384 + 128 * j] * ok).astype(BF16)
            z_send[j, 128:160] = (strip(out[:, 128:256], 32 + 32 * j, 32) * ok).astype(BF16)
            z_send[j, 160:192] = (strip(strips[:, 0:128], 64 - 64 * j, 64) * ok).astype(BF16)
        else:
            j = i - 4
            c_send[j, 0:32] = (strip(out[:, 512:640], 32 * j, 32) * ok).astype(BF16)
            c_send[j, 32:48] = (strip(strips[:, 128:256], 32 if a > 0 else 0, 32) * ok).astype(BF16)

    pl.semaphore_wait(barrier, len(everyone))
    rim_copies = []
    for i in (4, 5, 6, 7, 2, 3, 0, 1):
        pair = ((y_send, y_recv), (z_send, z_recv), (c_send, c_recv), (c_send, c_recv))[i // 2]
        slot = i - 4 if i >= 4 else i % 2
        copy = remote(pair[0].at[slot], pair[1].at[slot], S_RIM + i, near[i])
        copy.start()
        rim_copies.append(copy)
    mine = pl.multiple_of(jnp.where(g == 0, 112, 0), 16)
    early_edge = remote(lraw.at[pl.ds(mine, 16), 0:512], edge_a, S_CORE, other)
    early_edge.start()
    core_copies = [early_edge]
    lraw[0:128, 1152:1280] = out[:, 640:768].astype(BF16)

    loads[4].wait()
    loads[5].wait()
    k1s[...] = jnp.zeros_like(k1s)
    for tap in range(27):
        k1s[4 * tap : 4 * tap + 4, :] = k1[tap].astype(F32)
    loads[6].wait()
    k1t = mm_nt(identity(32), k1s[...].astype(BF16)).astype(BF16)
    for phase in range(8):
        weights1[32 * phase : 32 * phase + 32, :] = mm(k1t, fold[:, 256 * phase : 256 * phase + 256]).astype(BF16)
    eye = identity(64)
    for x in range(3):
        block = w2[9 * x : 9 * x + 9].reshape(288, 64)
        forward2[64 * x : 64 * x + 64, :] = mm_nt(eye, block).astype(BF16)
        for a in (0, 2, 4, 6):
            both = jnp.concatenate([w2[9 * x + a].astype(F32), w2[9 * x + a + 1].astype(F32)], axis=1)
            backward2[32 * x : 32 * x + 32, 64 * a : 64 * a + 128] = both.astype(BF16)
        backward2[32 * x : 32 * x + 32, 512:576] = w2[9 * x + 8]
    loads[7].wait()
    for half in range(2):
        spread_i[:, 512 * half : 512 * half + 512] = mm_nt(cot[:, 128 * half : 128 * half + 128], pool[...])
    far = pl.multiple_of(g * (17 * 32), 32)
    p2[pl.ds(far, 32), :] = jnp.zeros((32, 256), BF16)
    far = pl.multiple_of(g * (17 * 64), 64)
    pg[pl.ds(far, 64), :] = jnp.zeros((64, 256), BF16)
    gshift[...] = jnp.zeros_like(gshift)
    total[432:512, :] = jnp.zeros((80, 128), F32)
    early_edge.wait_recv()
    first_core = jnp.where(g == 0, jnp.float32(1.0), jnp.float32(0.0))
    half_row = lax.broadcasted_iota(jnp.int32, (8, 1), 0)

    def beyond(edge):
        edge = edge.astype(F32)
        edge = jnp.where(half_row < 4, edge[0:8] * first_core, edge[8:16] * (1.0 - first_core))
        return jnp.concatenate([edge, jnp.zeros_like(edge)], axis=0).astype(BF16)

    lraw[128:144, 0:512] = beyond(edge_a[...])
    for load in loads[8:]:
        load.wait()

    def early_step(step, carry):
        early[step] = mm(lraw[:, 0:512], inside[step])
        return carry

    lax.fori_loop(0, 8, early_step, 0, unroll=True)

    for copy in rim_copies:
        copy.wait_recv()
    for j in range(2):
        low = unstrip(y_recv[0, 0:64].astype(F32), 0, 64, j)
        high = unstrip(y_recv[1, 0:64].astype(F32), 64, 64, j)
        lraw[64 * j : 64 * j + 64, 768:896] = jnp.where(lane < 64, low, high).astype(BF16)
    lraw[0:128, 896:1024] = z_recv[0, 0:128]
    lraw[0:128, 1024:1152] = z_recv[1, 0:128]
    y_low, y_high = y_recv[0, 64:80].astype(F32), y_recv[1, 64:80].astype(F32)
    def fill_inner(j):
        at = slice(128 + 16 * (j % 2), 144 + 16 * (j % 2))
        z_low, z_high = z_recv[0, at].astype(F32), z_recv[1, at].astype(F32)
        block = jnp.where(lane < 16, unstrip(y_low, 0, 16, j), unstrip(y_high, 16, 16, j))
        block = jnp.where(lane < 32, block, unstrip(z_low, 32, 32, j // 2))
        block = jnp.where(lane < 64, block, unstrip(z_high, 64, 32, j // 2))
        lraw[16 * j : 16 * j + 16, 512:640] = block.astype(BF16)
    def fill_corner(j):
        block = jnp.zeros((32, 128), F32)
        for k in range(4):
            block = jnp.where(lane // 32 == k, unstrip(c_recv[k, 0:32].astype(F32), 32 * k, 32, j), block)
        lraw[32 * j : 32 * j + 32, 640:768] = block.astype(BF16)

    for j in (0, 7):
        fill_inner(j)
    for j in (0, 3):
        fill_corner(j)
    copy = remote(lraw.at[pl.ds(mine, 16), 512:1280], edge_b, S_CORE + 1, other)
    copy.start()
    core_copies.append(copy)
    for j in range(1, 7):
        fill_inner(j)
    for j in (1, 2):
        fill_corner(j)

    zs, ys, cs = [], [], []
    for j in range(2):
        low, high = z_recv[0, 160:192].astype(F32), z_recv[1, 160:192].astype(F32)
        zs.append(jnp.where(lane >= 64, unstrip(low, 64, 64, j), unstrip(high, 0, 64, j)))
    late = lane % 4 == 3
    for j in range(4):
        low, high = y_recv[0, 80:96].astype(F32), y_recv[1, 80:96].astype(F32)
        ys.append(jnp.where(lane >= 32, unstrip(low, 32, 32, j), unstrip(high, 0, 32, j)))
        ends = [unstrip(c_recv[k, 32:48].astype(F32), 32 if k < 2 else 0, 32, j) for k in range(4)]
        cs.append(
            jnp.where(lane >= 32, jnp.where(late, ends[0], ends[1]), jnp.where(late, ends[2], ends[3]))
        )
    zs, ys, cs = (jnp.concatenate(parts, axis=0) for parts in (zs, ys, cs))
    rim = jnp.concatenate([zs, ys, cs], axis=1).astype(BF16)
    spread_r[...] = mm(rim, cot_in[...])

    copy.wait_recv()
    lraw[128:144, 512:1280] = beyond(edge_b[...])

    def gather_step(step, carry):
        mid = mm(lraw[:, 512:768], nearby[step]) + early[step]
        rim = mm(lraw[:, 512:1280], around[step])
        low = half_row < 4
        for shift in range(2):
            at = pl.multiple_of(step * 32 + shift * 16, 16)
            lanes = slice(128 * shift, 128 * shift + 128)
            for x in range(16):
                for got, side in ((mid[:, lanes], 0), (rim[:, lanes], 1)):
                    after = got[8 * x + 8 : 8 * x + 16]
                    before = got[8 * x - 8 : 8 * x] if x else got[128:136]
                    block = jnp.concatenate([got[8 * x : 8 * x + 8], jnp.where(low, after, before)], axis=0)
                    block = block.astype(BF16)
                    x4[x, pl.ds(at, 16), 128 * side : 128 * side + 128] = block
                    if side == 0:
                        x4i[pl.ds(at, 16), 128 * x : 128 * x + 128] = block
        return carry

    lax.fori_loop(0, 8, gather_step, 0, unroll=True)

    def flag(test):
        return jnp.where(test, jnp.float32(1.0), jnp.float32(0.0))

    outside = jnp.maximum(
        jnp.maximum(sides[0:1, :] * flag(by == 0), sides[1:2, :] * flag(by == PY - 1)),
        jnp.maximum(sides[2:3, :] * flag(bz == 0), sides[3:4, :] * flag(bz == PZ - 1)),
    )
    scale = (1.0 - outside) * 0.125

    def first_layer(x):
        pre = mm(weights1[...], x4[x])
        pre1[x] = pre[:, 0:128]
        act = leaky(pre[0:32])
        for phase in range(1, 8):
            act = act + leaky(pre[32 * phase : 32 * phase + 32])
        p2[32 * x + 32 : 32 * x + 64, :] = (act * scale).astype(BF16)

    first_layer(0)
    first_layer(15)
    near_src = pl.multiple_of(jnp.where(g == 0, 16 * 32, 32), 32)
    near_dst = pl.multiple_of(jnp.where(g == 0, 0, 17 * 32), 32)
    copy = remote(p2.at[pl.ds(near_src, 32), :], p2.at[pl.ds(near_dst, 32), :], S_CORE + 2, other)
    copy.start()
    core_copies.append(copy)
    for x in range(1, 15):
        first_layer(x)

    copy.wait_recv()

    def shift_step(tap, carry):
        got = mm(p2[...], second[tap])
        at = pl.multiple_of(tap * 32, 32)
        for x in range(0, 18, 2):
            one, two = got[32 * x : 32 * x + 32], got[32 * x + 32 : 32 * x + 64]
            b2i[pl.ds(at, 32), 128 * x : 128 * x + 128] = one[:, 0:128].astype(BF16)
            b2i[pl.ds(at, 32), 128 * x + 128 : 128 * x + 256] = two[:, 0:128].astype(BF16)
            both = jnp.where(lane < 64, one[:, 128:256], two[:, 128:256])
            b2r[pl.ds(at, 32), 64 * x : 64 * x + 128] = both.astype(BF16)
        return carry

    lax.fori_loop(0, 9, shift_step, 0, unroll=True)

    for chunk in range(9):
        at = slice(256 * chunk, 256 * chunk + 256)
        t2i[:, at] = mm(forward2[...], b2i[:, at])
    for half in range(8):
        lifted = spread_i[:, 128 * half : 128 * half + 128] * 0.125
        pair = jnp.zeros((64, 128), F32)
        for x in (2 * half, 2 * half + 1):
            at = [slice(128 * (x + d), 128 * (x + d) + 128) for d in range(3)]
            pre = t2i[0:64, at[0]] + t2i[64:128, at[1]] + t2i[128:192, at[2]]
            pair = pair + leaky(pre)
            grad = (lifted * slope(pre)).astype(BF16)
            pg[64 * x + 64 : 64 * x + 128, 0:128] = grad
            for d in range(3):
                gshift[64 * d : 64 * d + 64, at[d]] = grad
        high, low = split(pair)
        at = slice(128 * (half % 4), 128 * (half % 4) + 128)
        pooled[half // 4, 0:64, at] = high
        pooled[half // 4, 64:128, at] = low

    grad2 = mm_nt(b2i[...], gshift[...])
    total[0:288, :] = grad2[:, 0:128]
    total[288:432, 0:64] = grad2[0:144, 128:192]
    total[288:432, 64:128] = grad2[144:288, 128:192]
    mine = pl.multiple_of(g * 256, 256)
    theirs = pl.multiple_of((1 - g) * 256, 256)
    halves = remote(total.at[pl.ds(theirs, 256), :], core_in, S_CORE + 4, other)
    halves.start()
    core_copies.append(halves)

    for start, end in ((0, 256), (256, 512), (512, 768), (768, 1152)):
        t2r[:, start:end] = mm(forward2[...], b2r[:, start:end])
    for half in (0, 7, 1, 2, 3, 4, 5, 6):
        lifted_rim = spread_r[:, 128 * half : 128 * half + 128] * 0.125
        here = slice(128 * half, 128 * half + 128)
        after = slice(128 * half + 128, 128 * half + 256)
        middle = pltpu.roll(jnp.where(lane < 64, t2r[64:128, after], t2r[64:128, here]), 64, 1)
        rim_grad = lifted_rim * slope(t2r[0:64, here] + middle + t2r[128:192, after])
        pg[128 * half + 64 : 128 * half + 128, 128:256] = jnp.where(lane < 64, rim_grad, 0.0).astype(BF16)
        pg[128 * half + 128 : 128 * half + 192, 128:256] = jnp.where(lane < 64, 0.0, rim_grad).astype(BF16)
        if half == 7:
            near_src = pl.multiple_of(jnp.where(g == 0, 16 * 64, 64), 64)
            near_dst = pl.multiple_of(jnp.where(g == 0, 0, 17 * 64), 64)
            edges = remote(pg.at[pl.ds(near_src, 64), :], pg.at[pl.ds(near_dst, 64), :], S_CORE + 3, other)
            edges.start()
            core_copies.append(edges)
    halves.wait_recv()
    spot = dp * 4 + yi
    place = pl.multiple_of(spot * 16, 16)
    core_in[...] = core_in[...] + total[pl.ds(mine, 256), :]
    xy_out[...] = core_in[...].astype(BF16)
    xy_copies = []
    for i, (a, b) in enumerate(XY):
        piece = ((dp + a) % 4) * 4 + (yi + b) % 4
        source = xy_out.at[pl.ds(pl.multiple_of(piece * 16, 16), 16), :]
        copy = remote(source, xy_in.at[i], S_XY + i, flat[i])
        copy.start()
        xy_copies.append(copy)
    edges.wait_recv()

    for step in range(5):
        got = mm(pg[...], back[step])
        for x in range(18):
            block = got[64 * x : 64 * x + 64].astype(BF16)
            bg[128 * step : 128 * step + 64, 128 * x : 128 * x + 128] = block[:, 0:128]
            bg[128 * step + 64 : 128 * step + 128, 128 * x : 128 * x + 128] = block[:, 128:256]

    def back_layer(chunk, carry):
        at = pl.ds(pl.multiple_of(chunk * 256, 256), 256)
        t3[:, at] = mm(backward2[...], bg[0:576, at])
        return carry

    lax.fori_loop(0, 9, back_layer, 0, unroll=True)

    for x in range(16):
        grad = (
            t3[0:32, 128 * (x + 2) : 128 * (x + 3)]
            + t3[32:64, 128 * (x + 1) : 128 * (x + 2)]
            + t3[64:96, 128 * x : 128 * (x + 1)]
        )
        grads[pl.ds(x, 32, stride=16), :] = grad
        eighth = grad * 0.125
        for phase in range(8):
            at = slice(32 * phase, 32 * phase + 32)
            g1[at, 128 * x : 128 * x + 128] = (eighth * slope(pre1[x, at, :])).astype(BF16)
    stores = [pltpu.make_async_copy(grads, grad_out, local_sem.at[16])]
    stores[0].start()
    wide = mm_nt(g1[...], x4i[...])
    partial = jnp.zeros((64, 128), F32)
    for phase in range(8):
        high, low = split(wide[32 * phase : 32 * phase + 32])
        partial = partial + mm_nt(jnp.concatenate([high, low], axis=0), fold[:, 256 * phase : 256 * phase + 256])
    first_part[...] = partial[0:32] + partial[32:64]

    my_half = pl.multiple_of(g * 16, 16)
    their_half = pl.multiple_of((1 - g) * 16, 16)
    swap = remote(first_part.at[pl.ds(their_half, 16), :], first_in, S_CORE + 5, other)
    swap.start()
    core_copies.append(swap)
    swap.wait_recv()
    first_xy[spot] = (first_in[...] + first_part[pl.ds(my_half, 16), :]).astype(BF16)
    fxy_copies = []
    for i in range(15):
        copy = remote(first_xy.at[spot], first_xy.at[spot], S_FXY + i, flat[i])
        copy.start()
        fxy_copies.append(copy)
    for sent in rim_copies + core_copies[:5]:
        sent.wait_send()
    for half in range(2):
        sums = mm(pooled[half], pool[...])
        feat[:, 128 * half : 128 * half + 128] = ((sums[0:64] + sums[64:128]) * 0.125).astype(BF16)
    stores.append(pltpu.make_async_copy(feat, feat_out, local_sem.at[15]))
    stores[1].start()
    part = core_in[pl.ds(place, 16), :]
    for i, copy in enumerate(xy_copies):
        copy.wait_recv()
        part = part + xy_in[i].astype(F32)
    z_in[zi] = part.astype(BF16)
    z_copies = []
    for k in range(7):
        copy = remote(z_in.at[zi], z_in.at[zi], S_Z + k, tall[k])
        copy.start()
        z_copies.append(copy)
    for copy in fxy_copies:
        copy.wait_recv()
    part = first_xy[0].astype(F32)
    for k in range(1, 16):
        part = part + first_xy[k].astype(F32)
    first_z[zi] = part.astype(BF16)
    fz_copies = []
    for k in range(7):
        copy = remote(first_z.at[zi], first_z.at[zi], S_FZ + k, tall[k])
        copy.start()
        fz_copies.append(copy)
    for copy in z_copies:
        copy.wait_recv()
    part = z_in[0].astype(F32)
    for k in range(1, 8):
        part = part + z_in[k].astype(F32)
    rows = pl.ds(pl.multiple_of(mine + place, 16), 16)
    final[rows, :] = part.astype(BF16)
    ag_copies = []
    for i in range(15):
        copy = remote(final.at[rows, :], final.at[rows, :], S_AG + i, flat[i])
        copy.start()
        ag_copies.append(copy)
    for sent in xy_copies + fxy_copies:
        sent.wait_send()
    for copy in ag_copies:
        copy.wait_recv()
    half = pl.ds(mine, 256)
    joined = remote(final.at[half, :], final.at[half, :], S_CORE + 6, other)
    joined.start()
    core_copies.append(joined)
    for copy in fz_copies:
        copy.wait_recv()
    part = first_z[0].astype(F32)
    for k in range(1, 8):
        part = part + first_z[k].astype(F32)
    half = pl.ds(my_half, 16)
    first_final[half, :] = part
    copy = remote(first_final.at[half, :], first_final.at[half, :], S_CORE + 7, other)
    copy.start()
    core_copies.append(copy)
    for sent in z_copies + ag_copies + fz_copies:
        sent.wait_send()
    joined.wait_recv()
    stores.append(pltpu.make_async_copy(final.at[0:432, :], second_out, local_sem.at[17]))
    stores[2].start()
    copy.wait_recv()
    stores.append(pltpu.make_async_copy(first_final, first_out, local_sem.at[18]))
    stores[3].start()
    for store in stores:
        store.wait()

    for sent in core_copies[5:]:
        sent.wait_send()


def arrange(feat, grad, second, first, feat_out, grad_out, first_out, second_out):
    feat_out[...] = feat[...]
    grad_out[...] = grad[...]
    for a in range(9):
        at = slice(32 * a, 32 * a + 32)
        second_out[a] = second[at, 0:64].astype(F32)
        second_out[9 + a] = second[at, 64:128].astype(F32)
    for a in range(18):
        row = 288 + (16 * a) % 144
        lanes = slice(0, 64) if a < 9 else slice(64, 128)
        second_out[18 + a // 2, 16 * (a % 2) : 16 * (a % 2) + 16, :] = second[row : row + 16, lanes].astype(F32)
    flipped = first[...].T
    for tap in range(27):
        first_out[tap] = flipped[4 * tap : 4 * tap + 4, :]


def on_device(volumes, first_kernel, second_kernel, cotangent):
    consts = matrices()
    here = pl.BlockSpec(memory_space=pltpu.VMEM)
    there = pl.BlockSpec(memory_space=pltpu.HBM)
    vmem = pltpu.VMEM
    scratch = [
        vmem((4, 16384), BF16), vmem((27, 4, 32), BF16), vmem((27, 32, 64), BF16), vmem((64, 256), BF16), vmem((8, 256), F32),
        vmem((64, 256), BF16), vmem((512, 128), F32),
    ] + [vmem(m.shape, BF16) for m in consts[:-1]] + [
        vmem((128, 512), F32), vmem((144, KRAW), BF16),
        vmem((2, 96, 128), BF16), vmem((2, 192, 128), BF16), vmem((4, 48, 128), BF16),
        vmem((2, 96, 128), BF16), vmem((2, 192, 128), BF16), vmem((4, 48, 128), BF16),
        vmem((16, 512), BF16), vmem((16, 768), BF16), vmem((8, 144, 256), F32),
        vmem((16, 256, 256), BF16), vmem((256, 2048), BF16), vmem((16, 256, 128), F32),
        vmem((256, 256), BF16), vmem((192, 288), BF16), vmem((96, 576), BF16), vmem((128, 32), F32),
        vmem((576, 256), BF16), vmem((288, 2304), BF16), vmem((288, 1152), BF16),
        vmem((192, 2304), F32), vmem((192, 1152), F32), vmem((64, 1024), F32), vmem((64, 1024), F32),
        vmem((2, 128, 512), BF16), vmem((1152, 256), BF16), vmem((192, 2304), BF16),
        vmem((640, 2304), BF16), vmem((96, 2304), F32), vmem((256, 2048), BF16),
        vmem((512, 128), F32), vmem((256, 128), F32), vmem((256, 128), BF16), vmem((15, 16, 128), BF16), vmem((8, 16, 128), BF16), vmem((512, 128), BF16),
        vmem((32, 128), F32), vmem((16, 128), F32), vmem((16, 16, 128), BF16), vmem((8, 16, 128), BF16), vmem((32, 128), F32),
        pltpu.SemaphoreType.DMA((19,)), pltpu.SemaphoreType.DMA((75,)), pltpu.SemaphoreType.DMA((75,)),
    ]
    parts = pl.pallas_call(
        body,
        out_shape=(
            jax.ShapeDtypeStruct((64, 256), BF16),
            jax.ShapeDtypeStruct((512, 128), F32),
            jax.ShapeDtypeStruct((432, 128), BF16),
            jax.ShapeDtypeStruct((32, 128), F32),
        ),
        in_specs=[there] * 15,
        out_specs=(there,) * 4,
        scratch_shapes=scratch,
        compiler_params=pltpu.CompilerParams(
            collective_id=0, has_side_effects=True, vmem_limit_bytes=60 * 1024 * 1024
        ),
    )(
        volumes.reshape(4, 16384),
        first_kernel.transpose(2, 3, 4, 1, 0).reshape(27, 4, 32),
        second_kernel.transpose(2, 3, 4, 1, 0).reshape(27, 32, 64),
        cotangent.reshape(64, 256),
        *(jnp.asarray(m) for m in consts),
    )
    features, act_grad, first_grad, second_grad = pl.pallas_call(
        arrange,
        out_shape=(
            jax.ShapeDtypeStruct((64, 256), BF16),
            jax.ShapeDtypeStruct((512, 128), F32),
            jax.ShapeDtypeStruct((27, 4, 32), F32),
            jax.ShapeDtypeStruct((27, 32, 64), F32),
        ),
        in_specs=[here] * 4,
        out_specs=(here,) * 4,
    )(*parts)
    return (
        features.reshape(1, 64, 1, 1, 256),
        act_grad.reshape(1, 32, 1, 1, 2048),
        first_grad.reshape(3, 3, 3, 4, 32).transpose(4, 3, 0, 1, 2),
        second_grad.reshape(3, 3, 3, 32, 64).transpose(4, 3, 0, 1, 2),
    )


def solution(mesh):
    placed = (P("dp", None, "gx", "yz", None), P(), P(), P("dp", None, "gx", "yz", None))
    return jax.shard_map(
        on_device,
        mesh=mesh,
        in_specs=placed,
        out_specs=(P("dp", None, "gx", "yz", None), P("dp", None, "gx", "yz", None), P(), P()),
        check_vma=False,
    )
```

```python
import functools

import jax
import jax.numpy as jnp
import numpy as np
from jax import lax
from jax.experimental import pallas as pl
from jax.experimental.pallas import tpu as pltpu
from jax.sharding import PartitionSpec as P

F32 = jnp.float32
BF16 = jnp.bfloat16
PY, PZ = 4, 8
NY = 4
KRAW = 1280
MESH = pl.DeviceIdType.MESH


def plane_order(rim):
    lanes = {(y, z): y * 8 + z for y in range(16) for z in range(8)}
    for y in range(-rim, 16 + rim):
        for z in range(-rim, 8 + rim):
            if (y, z) not in lanes:
                lanes[(y, z)] = len(lanes)
    return lanes


def on_edge(y, z):
    return y in (0, 31) or z in (0, 15)


EDGE = {place: i for i, place in enumerate((y, z) for y in range(32) for z in range(16) if on_edge(y, z))}


def rim_lane(y, z):
    if 0 <= y < 32 and 0 <= z < 16:
        return 640 + EDGE[(y, z)]
    if 0 <= z < 16:
        if y in (-1, 32):
            return (0 if y < 0 else 16) + z
        return 256 + ((y + 5) * 16 if y < 0 else 64 + (y - 33) * 16) + z
    if 0 <= y < 32:
        if z in (-1, 16):
            return (32 if z < 0 else 64) + y
        return 384 + ((z + 5) * 32 if z < 0 else 128 + (z - 17) * 32) + y
    row = y + 5 if y < 0 else y - 32
    col = z + 5 if z < 0 else z - 16
    return 128 + ((y >= 32) * 2 + (z >= 16)) * 32 + row * 5 + col


@functools.cache
def matrices():
    wide, ring = plane_order(2), plane_order(1)
    inside = np.zeros((8, 512, 256), np.float32)
    nearby = np.zeros((8, 256, 256), np.float32)
    around = np.zeros((8, 768, 256), np.float32)
    for dy in range(4):
        for dz in range(4):
            step, shift = divmod(dy * 4 + dz, 2)
            for (qy, qz), lane in wide.items():
                y, z = 2 * qy - 1 + dy, 2 * qz - 1 + dz
                if lane >= 128:
                    around[step, rim_lane(y, z), shift * 128 + lane - 128] = 1
                elif 0 <= y < 32 and 0 <= z < 16:
                    inside[step, y * 16 + z, shift * 128 + lane] = 1
                else:
                    nearby[step, rim_lane(y, z), shift * 128 + lane] = 1
    outgoing = np.zeros((512, 768), np.float32)
    for r in range(4):
        for z in range(16):
            outgoing[(27 + r) * 16 + z, r * 16 + z] = 1
            outgoing[(1 + r) * 16 + z, 64 + r * 16 + z] = 1
    for z in range(16):
        outgoing[31 * 16 + z, 128 + z] = 1
        outgoing[z, 144 + z] = 1
    for y in range(32):
        outgoing[y * 16 + 15, 160 + y] = 1
        outgoing[y * 16, 192 + y] = 1
        for c in range(4):
            outgoing[y * 16 + 11 + c, 256 + c * 32 + y] = 1
            outgoing[y * 16 + 1 + c, 384 + c * 32 + y] = 1
    for k in range(4):
        for r in range(5):
            for c in range(5):
                y = r if k // 2 else 27 + r
                z = c if k % 2 else 11 + c
                outgoing[y * 16 + z, 512 + k * 32 + r * 5 + c] = 1
    for (y, z), i in EDGE.items():
        outgoing[y * 16 + z, 640 + i] = 1
    second = np.zeros((9, 256, 256), np.float32)
    back = np.zeros((5, 256, 256), np.float32)
    for dy in range(3):
        for dz in range(3):
            tap = dy * 3 + dz
            for (y, z), lane in ring.items():
                second[tap, wide[(y + dy - 1, z + dz - 1)], lane] = 1
                if lane >= 128:
                    second[tap, wide[(y + dy - 1, z + dz - 1)], lane + 64] = 1
            for y in range(16):
                for z in range(8):
                    source = ring[(y - dy + 1, z - dz + 1)]
                    for place in (source,) if source < 128 else (source, source + 64):
                        back[tap // 2, place, (tap % 2) * 128 + y * 8 + z] = 1
    fold = np.zeros((128, 2048), np.float32)
    for phase in range(8):
        px, py, pz = phase // 4, phase // 2 % 2, phase % 2
        for tx in range(3):
            for ty in range(3):
                for tz in range(3):
                    for channel in range(4):
                        x, y, z = tx + px, ty + py, tz + pz
                        row = (y * 4 + z) * 16 + ((x - 1) % 4) * 4 + channel
                        fold[((tx * 3 + ty) * 3 + tz) * 4 + channel, phase * 256 + row] = 1
    pool = np.zeros((512, 128), np.float32)
    for x in range(4):
        for y in range(16):
            for z in range(8):
                pool[x * 128 + y * 8 + z, x * 32 + (y // 2) * 4 + z // 2] = 1
    cot_out = np.zeros((256, 256), np.float32)
    cot_in = np.zeros((384, 1024), np.float32)
    for x in range(8):
        for y in range(8):
            cot_out[x * 32 + y * 4, x * 8 + y] = 1
            cot_out[x * 32 + y * 4 + 3, 64 + x * 8 + y] = 1
        for z in range(4):
            cot_out[x * 32 + z, 128 + x * 4 + z] = 1
            cot_out[x * 32 + 28 + z, 160 + x * 4 + z] = 1
        for (y, z), lane in ring.items():
            if lane < 128:
                continue
            if 0 <= y < 16:
                source = x * 8 + y // 2 + (64 if z < 0 else 0)
            elif 0 <= z < 8:
                source = 128 + x * 4 + z // 2 + (32 if y < 0 else 0)
            else:
                source = 256 + x * 4 + (3 if z < 0 else 0) + (32 if y < 0 else 0)
            cot_in[source, x * 128 + lane - 128] = 1
            cot_in[source, x * 128 + lane - 64] = 1
    sides = np.zeros((8, 256), np.float32)
    for (y, z), lane in wide.items():
        sides[:4, lane] = (y < 0, y >= 16, z < 0, z >= 8)
    sixteen = (inside, nearby, around, outgoing, second, back, fold, pool, cot_out, cot_in)
    return tuple(m.astype(jnp.bfloat16) for m in sixteen) + (sides,)


def mm(a, b):
    return jnp.dot(a, b, preferred_element_type=F32)


def mm_nt(a, b):
    return lax.dot_general(a, b, (((1,), (1,)), ((), ())), preferred_element_type=F32)


def identity(n):
    rows = lax.broadcasted_iota(jnp.int32, (n, n), 0)
    return jnp.where(rows == lax.broadcasted_iota(jnp.int32, (n, n), 1), 1.0, 0.0).astype(BF16)


def leaky(t):
    return jnp.where(t > 0, t, 0.3 * t)


def slope(t):
    return jnp.where(t > 0, jnp.float32(1.0), jnp.float32(0.3))


def strip(block, start, width):
    parts = 128 // width
    rows = block.shape[0] // parts
    lane = lax.broadcasted_iota(jnp.int32, (1, 128), 1)
    packed = jnp.zeros((rows, 128), F32)
    for j in range(parts):
        piece = block[rows * j : rows * j + rows]
        shift = (width * j - start) % 128
        packed = jnp.where(lane // width == j, pltpu.roll(piece, shift, 1) if shift else piece, packed)
    return packed


def unstrip(packed, start, width, j):
    shift = (start - width * j) % 128
    return pltpu.roll(packed, shift, 1) if shift else packed


def split(t):
    high = t.astype(BF16)
    return high, (t - high.astype(F32)).astype(BF16)


FACES = ((1, 0), (-1, 0), (0, 1), (0, -1))
CORNERS = ((1, 1), (1, -1), (-1, 1), (-1, -1))
DIRS = FACES + CORNERS
XY = sorted(
    ((a, b) for a in range(4) for b in range(4) if (a, b) != (0, 0)),
    key=lambda p: -min(p[0], 4 - p[0]) - min(p[1], 4 - p[1]),
)
TALL = (4, 3, 5, 2, 6, 1, 7)
S_RIM, S_CORE, S_XY, S_Z, S_AG, S_FXY, S_FZ = 0, 8, 16, 31, 38, 53, 68


def body(
    vol_h, k1_h, w2_h, cot_h, inside_h, nearby_h, around_h, outgoing_h, second_h, back_h, fold_h, pool_h, cot_out_h, cot_in_h,
    sides_h, feat_out, grad_out, second_out, first_out,
    vol, k1, w2, cot, sides, feat, grads,
    inside, nearby, around, outgoing, second, back, fold, pool, cot_out, cot_in,
    rows32, lraw, y_send, z_send, c_send, y_recv, z_recv, c_recv, edge_a, edge_b, early,
    x4, x4i, pre1, weights1, forward2, backward2, k1s,
    p2, b2i, b2r, t2i, t2r, spread_i, spread_r, pooled, pg, gshift, bg, t3, g1,
    total, core_in, xy_out, xy_in, z_in, final, first_part, first_in, first_xy, first_z, first_final,
    local_sem, send_sem, recv_sem,
):
    dp, g, s = lax.axis_index("dp"), lax.axis_index("gx"), lax.axis_index("yz")
    by, bz = s // PZ, s % PZ
    yi, zi = s % NY, s // NY
    other = (dp, 1 - g, s)
    near = [(dp, g, ((by + a) % PY) * PZ + (bz + b) % PZ) for a, b in DIRS]
    flat = [((dp + a) % 4, g, zi * NY + (yi + b) % NY) for a, b in XY]
    tall = [(dp, g, ((zi + k) % 8) * NY + yi) for k in TALL]

    loads = [
        pltpu.make_async_copy(a, b, local_sem.at[i])
        for i, (a, b) in enumerate(
            (
                (vol_h, vol), (outgoing_h, outgoing), (cot_h, cot), (cot_out_h, cot_out), (k1_h, k1), (w2_h, w2),
                (fold_h, fold), (pool_h, pool), (inside_h, inside), (cot_in_h, cot_in), (nearby_h, nearby),
                (around_h, around), (second_h, second), (back_h, back), (sides_h, sides),
            )
        )
    ]
    for load in loads:
        load.start()

    barrier = pltpu.get_barrier_semaphore()
    everyone = [other] + near + flat + tall
    for device in everyone:
        pl.semaphore_signal(barrier, inc=1, device_id=device, device_id_type=MESH)

    def remote(source, target, slot, device):
        return pltpu.make_async_remote_copy(
            src_ref=source, dst_ref=target, send_sem=send_sem.at[slot], recv_sem=recv_sem.at[slot],
            device_id=device, device_id_type=MESH,
        )

    def valid(a, b):
        ok = jnp.logical_and(
            jnp.logical_and(by + a >= 0, by + a < PY), jnp.logical_and(bz + b >= 0, bz + b < PZ)
        )
        return jnp.where(ok, jnp.float32(1.0), jnp.float32(0.0))

    lane = lax.broadcasted_iota(jnp.int32, (1, 128), 1)

    loads[0].wait()
    for x in range(32):
        rows32[4 * x : 4 * x + 4, :] = vol[:, x * 512 : (x + 1) * 512].astype(F32)
    lraw[0:128, 0:512] = rows32[...].astype(BF16)
    loads[1].wait()
    out = mm(lraw[0:128, 0:512], outgoing[...])
    loads[2].wait()
    loads[3].wait()
    strips = mm(cot[...], cot_out[...])
    for i, (a, b) in enumerate(DIRS):
        ok = valid(a, b)
        if i < 2:
            y_send[i, 0:64] = (strip(out[:, 0:128], 64 * i, 64) * ok).astype(BF16)
            y_send[i, 64:80] = (strip(out[:, 128:256], 16 * i, 16) * ok).astype(BF16)
            y_send[i, 80:96] = (strip(strips[:, 128:256], 32 - 32 * i, 32) * ok).astype(BF16)
        elif i < 4:
            j = i - 2
            z_send[j, 0:128] = (out[:, 256 + 128 * j : 384 + 128 * j] * ok).astype(BF16)
            z_send[j, 128:160] = (strip(out[:, 128:256], 32 + 32 * j, 32) * ok).astype(BF16)
            z_send[j, 160:192] = (strip(strips[:, 0:128], 64 - 64 * j, 64) * ok).astype(BF16)
        else:
            j = i - 4
            c_send[j, 0:32] = (strip(out[:, 512:640], 32 * j, 32) * ok).astype(BF16)
            c_send[j, 32:48] = (strip(strips[:, 128:256], 32 if a > 0 else 0, 32) * ok).astype(BF16)

    pl.semaphore_wait(barrier, len(everyone))
    rim_copies = []
    for i in (4, 5, 6, 7, 2, 3, 0, 1):
        pair = ((y_send, y_recv), (z_send, z_recv), (c_send, c_recv), (c_send, c_recv))[i // 2]
        slot = i - 4 if i >= 4 else i % 2
        copy = remote(pair[0].at[slot], pair[1].at[slot], S_RIM + i, near[i])
        copy.start()
        rim_copies.append(copy)
    mine = pl.multiple_of(jnp.where(g == 0, 112, 0), 16)
    early_edge = remote(lraw.at[pl.ds(mine, 16), 0:512], edge_a, S_CORE, other)
    early_edge.start()
    core_copies = [early_edge]
    lraw[0:128, 1152:1280] = out[:, 640:768].astype(BF16)

    loads[4].wait()
    loads[5].wait()
    k1s[...] = jnp.zeros_like(k1s)
    for tap in range(27):
        k1s[4 * tap : 4 * tap + 4, :] = k1[tap].astype(F32)
    loads[6].wait()
    k1t = mm_nt(identity(32), k1s[...].astype(BF16)).astype(BF16)
    for phase in range(8):
        weights1[32 * phase : 32 * phase + 32, :] = mm(k1t, fold[:, 256 * phase : 256 * phase + 256]).astype(BF16)
    eye = identity(64)
    for x in range(3):
        block = w2[9 * x : 9 * x + 9].reshape(288, 64)
        forward2[64 * x : 64 * x + 64, :] = mm_nt(eye, block).astype(BF16)
        for a in (0, 2, 4, 6):
            both = jnp.concatenate([w2[9 * x + a].astype(F32), w2[9 * x + a + 1].astype(F32)], axis=1)
            backward2[32 * x : 32 * x + 32, 64 * a : 64 * a + 128] = both.astype(BF16)
        backward2[32 * x : 32 * x + 32, 512:576] = w2[9 * x + 8]
    loads[7].wait()
    for half in range(2):
        spread_i[:, 512 * half : 512 * half + 512] = mm_nt(cot[:, 128 * half : 128 * half + 128], pool[...])
    far = pl.multiple_of(g * (17 * 32), 32)
    p2[pl.ds(far, 32), :] = jnp.zeros((32, 256), BF16)
    far = pl.multiple_of(g * (17 * 64), 64)
    pg[pl.ds(far, 64), :] = jnp.zeros((64, 256), BF16)
    gshift[...] = jnp.zeros_like(gshift)
    total[432:512, :] = jnp.zeros((80, 128), F32)
    early_edge.wait_recv()
    first_core = jnp.where(g == 0, jnp.float32(1.0), jnp.float32(0.0))
    half_row = lax.broadcasted_iota(jnp.int32, (8, 1), 0)

    def beyond(edge):
        edge = edge.astype(F32)
        edge = jnp.where(half_row < 4, edge[0:8] * first_core, edge[8:16] * (1.0 - first_core))
        return jnp.concatenate([edge, jnp.zeros_like(edge)], axis=0).astype(BF16)

    lraw[128:144, 0:512] = beyond(edge_a[...])
    for load in loads[8:]:
        load.wait()

    def early_step(step, carry):
        early[step] = mm(lraw[:, 0:512], inside[step])
        return carry

    lax.fori_loop(0, 8, early_step, 0, unroll=True)

    for copy in rim_copies:
        copy.wait_recv()
    for j in range(2):
        low = unstrip(y_recv[0, 0:64].astype(F32), 0, 64, j)
        high = unstrip(y_recv[1, 0:64].astype(F32), 64, 64, j)
        lraw[64 * j : 64 * j + 64, 768:896] = jnp.where(lane < 64, low, high).astype(BF16)
    lraw[0:128, 896:1024] = z_recv[0, 0:128]
    lraw[0:128, 1024:1152] = z_recv[1, 0:128]
    y_low, y_high = y_recv[0, 64:80].astype(F32), y_recv[1, 64:80].astype(F32)
    def fill_inner(j):
        at = slice(128 + 16 * (j % 2), 144 + 16 * (j % 2))
        z_low, z_high = z_recv[0, at].astype(F32), z_recv[1, at].astype(F32)
        block = jnp.where(lane < 16, unstrip(y_low, 0, 16, j), unstrip(y_high, 16, 16, j))
        block = jnp.where(lane < 32, block, unstrip(z_low, 32, 32, j // 2))
        block = jnp.where(lane < 64, block, unstrip(z_high, 64, 32, j // 2))
        lraw[16 * j : 16 * j + 16, 512:640] = block.astype(BF16)
    def fill_corner(j):
        block = jnp.zeros((32, 128), F32)
        for k in range(4):
            block = jnp.where(lane // 32 == k, unstrip(c_recv[k, 0:32].astype(F32), 32 * k, 32, j), block)
        lraw[32 * j : 32 * j + 32, 640:768] = block.astype(BF16)

    for j in (0, 7):
        fill_inner(j)
    for j in (0, 3):
        fill_corner(j)
    copy = remote(lraw.at[pl.ds(mine, 16), 512:1280], edge_b, S_CORE + 1, other)
    copy.start()
    core_copies.append(copy)
    for j in range(1, 7):
        fill_inner(j)
    for j in (1, 2):
        fill_corner(j)

    zs, ys, cs = [], [], []
    for j in range(2):
        low, high = z_recv[0, 160:192].astype(F32), z_recv[1, 160:192].astype(F32)
        zs.append(jnp.where(lane >= 64, unstrip(low, 64, 64, j), unstrip(high, 0, 64, j)))
    late = lane % 4 == 3
    for j in range(4):
        low, high = y_recv[0, 80:96].astype(F32), y_recv[1, 80:96].astype(F32)
        ys.append(jnp.where(lane >= 32, unstrip(low, 32, 32, j), unstrip(high, 0, 32, j)))
        ends = [unstrip(c_recv[k, 32:48].astype(F32), 32 if k < 2 else 0, 32, j) for k in range(4)]
        cs.append(
            jnp.where(lane >= 32, jnp.where(late, ends[0], ends[1]), jnp.where(late, ends[2], ends[3]))
        )
    zs, ys, cs = (jnp.concatenate(parts, axis=0) for parts in (zs, ys, cs))
    rim = jnp.concatenate([zs, ys, cs], axis=1).astype(BF16)
    spread_r[...] = mm(rim, cot_in[...])

    copy.wait_recv()
    lraw[128:144, 512:1280] = beyond(edge_b[...])

    def gather_step(step, carry):
        mid = mm(lraw[:, 512:768], nearby[step]) + early[step]
        rim = mm(lraw[:, 512:1280], around[step])
        low = half_row < 4
        for shift in range(2):
            at = pl.multiple_of(step * 32 + shift * 16, 16)
            lanes = slice(128 * shift, 128 * shift + 128)
            for x in range(16):
                for got, side in ((mid[:, lanes], 0), (rim[:, lanes], 1)):
                    after = got[8 * x + 8 : 8 * x + 16]
                    before = got[8 * x - 8 : 8 * x] if x else got[128:136]
                    block = jnp.concatenate([got[8 * x : 8 * x + 8], jnp.where(low, after, before)], axis=0)
                    block = block.astype(BF16)
                    x4[x, pl.ds(at, 16), 128 * side : 128 * side + 128] = block
                    if side == 0:
                        x4i[pl.ds(at, 16), 128 * x : 128 * x + 128] = block
        return carry

    lax.fori_loop(0, 8, gather_step, 0, unroll=True)

    def flag(test):
        return jnp.where(test, jnp.float32(1.0), jnp.float32(0.0))

    outside = jnp.maximum(
        jnp.maximum(sides[0:1, :] * flag(by == 0), sides[1:2, :] * flag(by == PY - 1)),
        jnp.maximum(sides[2:3, :] * flag(bz == 0), sides[3:4, :] * flag(bz == PZ - 1)),
    )
    scale = (1.0 - outside) * 0.125

    def first_layer(x):
        pre = mm(weights1[...], x4[x])
        pre1[x] = pre[:, 0:128]
        act = leaky(pre[0:32])
        for phase in range(1, 8):
            act = act + leaky(pre[32 * phase : 32 * phase + 32])
        p2[32 * x + 32 : 32 * x + 64, :] = (act * scale).astype(BF16)

    first_layer(0)
    first_layer(15)
    near_src = pl.multiple_of(jnp.where(g == 0, 16 * 32, 32), 32)
    near_dst = pl.multiple_of(jnp.where(g == 0, 0, 17 * 32), 32)
    copy = remote(p2.at[pl.ds(near_src, 32), :], p2.at[pl.ds(near_dst, 32), :], S_CORE + 2, other)
    copy.start()
    core_copies.append(copy)
    for x in range(1, 15):
        first_layer(x)

    copy.wait_recv()

    def shift_step(tap, carry):
        got = mm(p2[...], second[tap])
        at = pl.multiple_of(tap * 32, 32)
        for x in range(0, 18, 2):
            one, two = got[32 * x : 32 * x + 32], got[32 * x + 32 : 32 * x + 64]
            b2i[pl.ds(at, 32), 128 * x : 128 * x + 128] = one[:, 0:128].astype(BF16)
            b2i[pl.ds(at, 32), 128 * x + 128 : 128 * x + 256] = two[:, 0:128].astype(BF16)
            both = jnp.where(lane < 64, one[:, 128:256], two[:, 128:256])
            b2r[pl.ds(at, 32), 64 * x : 64 * x + 128] = both.astype(BF16)
        return carry

    lax.fori_loop(0, 9, shift_step, 0, unroll=True)

    for chunk in range(9):
        at = slice(256 * chunk, 256 * chunk + 256)
        t2i[:, at] = mm(forward2[...], b2i[:, at])
    for half in range(8):
        lifted = spread_i[:, 128 * half : 128 * half + 128] * 0.125
        pair = jnp.zeros((64, 128), F32)
        for x in (2 * half, 2 * half + 1):
            at = [slice(128 * (x + d), 128 * (x + d) + 128) for d in range(3)]
            pre = t2i[0:64, at[0]] + t2i[64:128, at[1]] + t2i[128:192, at[2]]
            pair = pair + leaky(pre)
            grad = (lifted * slope(pre)).astype(BF16)
            pg[64 * x + 64 : 64 * x + 128, 0:128] = grad
            for d in range(3):
                gshift[64 * d : 64 * d + 64, at[d]] = grad
        high, low = split(pair)
        at = slice(128 * (half % 4), 128 * (half % 4) + 128)
        pooled[half // 4, 0:64, at] = high
        pooled[half // 4, 64:128, at] = low

    grad2 = mm_nt(b2i[...], gshift[...])
    total[0:288, :] = grad2[:, 0:128]
    total[288:432, 0:64] = grad2[0:144, 128:192]
    total[288:432, 64:128] = grad2[144:288, 128:192]
    mine = pl.multiple_of(g * 256, 256)
    theirs = pl.multiple_of((1 - g) * 256, 256)
    halves = remote(total.at[pl.ds(theirs, 256), :], core_in, S_CORE + 4, other)
    halves.start()
    core_copies.append(halves)

    for start, end in ((0, 256), (256, 512), (512, 768), (768, 1152)):
        t2r[:, start:end] = mm(forward2[...], b2r[:, start:end])
    for half in (0, 7, 1, 2, 3, 4, 5, 6):
        lifted_rim = spread_r[:, 128 * half : 128 * half + 128] * 0.125
        here = slice(128 * half, 128 * half + 128)
        after = slice(128 * half + 128, 128 * half + 256)
        middle = pltpu.roll(jnp.where(lane < 64, t2r[64:128, after], t2r[64:128, here]), 64, 1)
        rim_grad = lifted_rim * slope(t2r[0:64, here] + middle + t2r[128:192, after])
        pg[128 * half + 64 : 128 * half + 128, 128:256] = jnp.where(lane < 64, rim_grad, 0.0).astype(BF16)
        pg[128 * half + 128 : 128 * half + 192, 128:256] = jnp.where(lane < 64, 0.0, rim_grad).astype(BF16)
        if half == 7:
            near_src = pl.multiple_of(jnp.where(g == 0, 16 * 64, 64), 64)
            near_dst = pl.multiple_of(jnp.where(g == 0, 0, 17 * 64), 64)
            edges = remote(pg.at[pl.ds(near_src, 64), :], pg.at[pl.ds(near_dst, 64), :], S_CORE + 3, other)
            edges.start()
            core_copies.append(edges)
    halves.wait_recv()
    spot = dp * 4 + yi
    place = pl.multiple_of(spot * 16, 16)
    core_in[...] = core_in[...] + total[pl.ds(mine, 256), :]
    xy_out[...] = core_in[...].astype(BF16)
    xy_copies = []
    for i, (a, b) in enumerate(XY):
        piece = ((dp + a) % 4) * 4 + (yi + b) % 4
        source = xy_out.at[pl.ds(pl.multiple_of(piece * 16, 16), 16), :]
        copy = remote(source, xy_in.at[i], S_XY + i, flat[i])
        copy.start()
        xy_copies.append(copy)
    edges.wait_recv()

    for step in range(5):
        got = mm(pg[...], back[step])
        for x in range(18):
            block = got[64 * x : 64 * x + 64].astype(BF16)
            bg[128 * step : 128 * step + 64, 128 * x : 128 * x + 128] = block[:, 0:128]
            bg[128 * step + 64 : 128 * step + 128, 128 * x : 128 * x + 128] = block[:, 128:256]

    def back_layer(chunk, carry):
        at = pl.ds(pl.multiple_of(chunk * 256, 256), 256)
        t3[:, at] = mm(backward2[...], bg[0:576, at])
        return carry

    lax.fori_loop(0, 9, back_layer, 0, unroll=True)

    for x in range(16):
        grad = (
            t3[0:32, 128 * (x + 2) : 128 * (x + 3)]
            + t3[32:64, 128 * (x + 1) : 128 * (x + 2)]
            + t3[64:96, 128 * x : 128 * (x + 1)]
        )
        grads[pl.ds(x, 32, stride=16), :] = grad
        eighth = grad * 0.125
        for phase in range(8):
            at = slice(32 * phase, 32 * phase + 32)
            g1[at, 128 * x : 128 * x + 128] = (eighth * slope(pre1[x, at, :])).astype(BF16)
    stores = [pltpu.make_async_copy(grads, grad_out, local_sem.at[16])]
    stores[0].start()
    wide = mm_nt(g1[...], x4i[...])
    partial = jnp.zeros((64, 128), F32)
    for phase in range(8):
        high, low = split(wide[32 * phase : 32 * phase + 32])
        partial = partial + mm_nt(jnp.concatenate([high, low], axis=0), fold[:, 256 * phase : 256 * phase + 256])
    first_part[...] = partial[0:32] + partial[32:64]

    my_half = pl.multiple_of(g * 16, 16)
    their_half = pl.multiple_of((1 - g) * 16, 16)
    swap = remote(first_part.at[pl.ds(their_half, 16), :], first_in, S_CORE + 5, other)
    swap.start()
    core_copies.append(swap)
    swap.wait_recv()
    first_xy[spot] = (first_in[...] + first_part[pl.ds(my_half, 16), :]).astype(BF16)
    fxy_copies = []
    for i in range(15):
        copy = remote(first_xy.at[spot], first_xy.at[spot], S_FXY + i, flat[i])
        copy.start()
        fxy_copies.append(copy)
    part = core_in[pl.ds(place, 16), :]
    for i, copy in enumerate(xy_copies):
        copy.wait_recv()
        part = part + xy_in[i].astype(F32)
    z_in[zi] = part.astype(BF16)
    z_copies = []
    for k in range(7):
        copy = remote(z_in.at[zi], z_in.at[zi], S_Z + k, tall[k])
        copy.start()
        z_copies.append(copy)
    for sent in rim_copies + core_copies[:5]:
        sent.wait_send()
    for half in range(2):
        sums = mm(pooled[half], pool[...])
        feat[:, 128 * half : 128 * half + 128] = ((sums[0:64] + sums[64:128]) * 0.125).astype(BF16)
    stores.append(pltpu.make_async_copy(feat, feat_out, local_sem.at[15]))
    stores[1].start()
    for copy in fxy_copies:
        copy.wait_recv()
    part = first_xy[0].astype(F32)
    for k in range(1, 16):
        part = part + first_xy[k].astype(F32)
    first_z[zi] = part.astype(BF16)
    fz_copies = []
    for k in range(7):
        copy = remote(first_z.at[zi], first_z.at[zi], S_FZ + k, tall[k])
        copy.start()
        fz_copies.append(copy)
    for copy in z_copies:
        copy.wait_recv()
    part = z_in[0].astype(F32)
    for k in range(1, 8):
        part = part + z_in[k].astype(F32)
    rows = pl.ds(pl.multiple_of(mine + place, 16), 16)
    final[rows, :] = part.astype(BF16)
    ag_copies = []
    for i in range(15):
        copy = remote(final.at[rows, :], final.at[rows, :], S_AG + i, flat[i])
        copy.start()
        ag_copies.append(copy)
    for sent in xy_copies + fxy_copies:
        sent.wait_send()
    for copy in ag_copies:
        copy.wait_recv()
    half = pl.ds(mine, 256)
    joined = remote(final.at[half, :], final.at[half, :], S_CORE + 6, other)
    joined.start()
    core_copies.append(joined)
    for copy in fz_copies:
        copy.wait_recv()
    part = first_z[0].astype(F32)
    for k in range(1, 8):
        part = part + first_z[k].astype(F32)
    half = pl.ds(my_half, 16)
    first_final[half, :] = part
    copy = remote(first_final.at[half, :], first_final.at[half, :], S_CORE + 7, other)
    copy.start()
    core_copies.append(copy)
    for sent in z_copies + ag_copies + fz_copies:
        sent.wait_send()
    joined.wait_recv()
    stores.append(pltpu.make_async_copy(final.at[0:432, :], second_out, local_sem.at[17]))
    stores[2].start()
    copy.wait_recv()
    stores.append(pltpu.make_async_copy(first_final, first_out, local_sem.at[18]))
    stores[3].start()
    for store in stores:
        store.wait()

    for sent in core_copies[5:]:
        sent.wait_send()


def arrange(feat, grad, second, first, feat_out, grad_out, first_out, second_out):
    feat_out[...] = feat[...]
    grad_out[...] = grad[...]
    for a in range(9):
        at = slice(32 * a, 32 * a + 32)
        second_out[a] = second[at, 0:64].astype(F32)
        second_out[9 + a] = second[at, 64:128].astype(F32)
    for a in range(18):
        row = 288 + (16 * a) % 144
        lanes = slice(0, 64) if a < 9 else slice(64, 128)
        second_out[18 + a // 2, 16 * (a % 2) : 16 * (a % 2) + 16, :] = second[row : row + 16, lanes].astype(F32)
    flipped = first[...].T
    for tap in range(27):
        first_out[tap] = flipped[4 * tap : 4 * tap + 4, :]


def on_device(volumes, first_kernel, second_kernel, cotangent):
    consts = matrices()
    here = pl.BlockSpec(memory_space=pltpu.VMEM)
    there = pl.BlockSpec(memory_space=pltpu.HBM)
    vmem = pltpu.VMEM
    scratch = [
        vmem((4, 16384), BF16), vmem((27, 4, 32), BF16), vmem((27, 32, 64), BF16), vmem((64, 256), BF16), vmem((8, 256), F32),
        vmem((64, 256), BF16), vmem((512, 128), F32),
    ] + [vmem(m.shape, BF16) for m in consts[:-1]] + [
        vmem((128, 512), F32), vmem((144, KRAW), BF16),
        vmem((2, 96, 128), BF16), vmem((2, 192, 128), BF16), vmem((4, 48, 128), BF16),
        vmem((2, 96, 128), BF16), vmem((2, 192, 128), BF16), vmem((4, 48, 128), BF16),
        vmem((16, 512), BF16), vmem((16, 768), BF16), vmem((8, 144, 256), F32),
        vmem((16, 256, 256), BF16), vmem((256, 2048), BF16), vmem((16, 256, 128), F32),
        vmem((256, 256), BF16), vmem((192, 288), BF16), vmem((96, 576), BF16), vmem((128, 32), F32),
        vmem((576, 256), BF16), vmem((288, 2304), BF16), vmem((288, 1152), BF16),
        vmem((192, 2304), F32), vmem((192, 1152), F32), vmem((64, 1024), F32), vmem((64, 1024), F32),
        vmem((2, 128, 512), BF16), vmem((1152, 256), BF16), vmem((192, 2304), BF16),
        vmem((640, 2304), BF16), vmem((96, 2304), F32), vmem((256, 2048), BF16),
        vmem((512, 128), F32), vmem((256, 128), F32), vmem((256, 128), BF16), vmem((15, 16, 128), BF16), vmem((8, 16, 128), BF16), vmem((512, 128), BF16),
        vmem((32, 128), F32), vmem((16, 128), F32), vmem((16, 16, 128), BF16), vmem((8, 16, 128), BF16), vmem((32, 128), F32),
        pltpu.SemaphoreType.DMA((19,)), pltpu.SemaphoreType.DMA((75,)), pltpu.SemaphoreType.DMA((75,)),
    ]
    parts = pl.pallas_call(
        body,
        out_shape=(
            jax.ShapeDtypeStruct((64, 256), BF16),
            jax.ShapeDtypeStruct((512, 128), F32),
            jax.ShapeDtypeStruct((432, 128), BF16),
            jax.ShapeDtypeStruct((32, 128), F32),
        ),
        in_specs=[there] * 15,
        out_specs=(there,) * 4,
        scratch_shapes=scratch,
        compiler_params=pltpu.CompilerParams(
            collective_id=0, has_side_effects=True, vmem_limit_bytes=60 * 1024 * 1024
        ),
    )(
        volumes.reshape(4, 16384),
        first_kernel.transpose(2, 3, 4, 1, 0).reshape(27, 4, 32),
        second_kernel.transpose(2, 3, 4, 1, 0).reshape(27, 32, 64),
        cotangent.reshape(64, 256),
        *(jnp.asarray(m) for m in consts),
    )
    features, act_grad, first_grad, second_grad = pl.pallas_call(
        arrange,
        out_shape=(
            jax.ShapeDtypeStruct((64, 256), BF16),
            jax.ShapeDtypeStruct((512, 128), F32),
            jax.ShapeDtypeStruct((27, 4, 32), F32),
            jax.ShapeDtypeStruct((27, 32, 64), F32),
        ),
        in_specs=[here] * 4,
        out_specs=(here,) * 4,
    )(*parts)
    return (
        features.reshape(1, 64, 1, 1, 256),
        act_grad.reshape(1, 32, 1, 1, 2048),
        first_grad.reshape(3, 3, 3, 4, 32).transpose(4, 3, 0, 1, 2),
        second_grad.reshape(3, 3, 3, 32, 64).transpose(4, 3, 0, 1, 2),
    )


def solution(mesh):
    placed = (P("dp", None, "gx", "yz", None), P(), P(), P("dp", None, "gx", "yz", None))
    return jax.shard_map(
        on_device,
        mesh=mesh,
        in_specs=placed,
        out_specs=(P("dp", None, "gx", "yz", None), P("dp", None, "gx", "yz", None), P(), P()),
        check_vma=False,
    )
```
